128 devices in a mesh: row: 8 (over y, x_hi), col: 16 (over x_lo, z, core).
Axes of the slice: x: 4 (x_hi: 2, x_lo: 2; x = x_hi * 2 + x_lo), y: 4, z: 4, core: 2. Of those that a mesh axis runs over, the one named last changes fastest.
Arguments:
- a_blocks: float32 [8, 16, 4, 128, 128], P('row', 'col'), may hold values from -1.2 to 1.2
- a_index: int32 [8, 16, 4], P('row', 'col'), may hold values from -1 to 63, as said below
- b_blocks: float32 [8, 16, 2, 8, 128, 128], P('row', 'col'), may hold values from -1.2 to 1.2
- b_index: int32 [8, 16, 2, 8], P('row', 'col'), may hold values from -1 to 63, as said below
- c_index: int32 [8, 16, 16], P('row', 'col'), may hold values from -1 to 63, as said below
Outputs:
- c_blocks: float32 [8, 16, 16, 128, 128], P('row', 'col')
The draws below stay inside these ranges and needn't reach their ends.
Inputs may be any that keep to these rules, and one draw needn't show every extreme that they name: `a_index`: within each tile the non-negative entries are distinct and come before the entries -1, which mark empty slots; every tile has at least one block and some tile has all 4 slots filled. `b_index`: within each panel of a device the non-negative entries are distinct and come before the entries -1, which mark empty slots; every panel has at least one block and some panel has all 8 slots filled. `c_index`: within each tile the non-negative entries are distinct and come before the entries -1, which mark empty slots; every tile keeps at least one block and some tile has all 16 slots filled.
All inputs are finite; a program needn't handle non-finite values.
Results may differ from the reference program's by a relative error of at most 0.0003.
Values sent between devices are 32-bit elements; how exact they have to be, the bound alone decides.
No kernel may reach another device: no remote copies, remote signals or barrier semaphores. Data moves between devices by JAX's collectives and lax.ppermute only.
A program may use at most 192 MiB of HBM per device.

```python
import jax
import jax.numpy as jnp
from jax import lax

BS = 128
MBD = 8
PK = 8
NBD = 8
H = 2
SA = 4
SB = 8
SC = 16
N_ROW = 8
N_COL = 16


def band_level(row_place, col_place, period):
    gap = jnp.abs(row_place - col_place) % period
    gap = jnp.minimum(gap, period - gap)
    return gap * 4 // (period // 2 + 1)


def draw_pattern(key, nearness, positions, slots):
    tiles = nearness.shape[0]
    key_perm, key_count, key_full, key_sparse = jax.random.split(key, 4)
    keys = jax.random.split(key_perm, tiles)
    orders = jax.vmap(lambda one: jax.random.permutation(one, positions))(keys)[:, :slots]
    least = max(1, slots // 4)
    upper = slots - nearness * (slots - least) // 4
    counts = jax.random.randint(key_count, (tiles,), least, upper + 1)
    full_tile = jax.random.randint(key_full, (), 0, tiles)
    sparse_tile = (full_tile + 1 + jax.random.randint(key_sparse, (), 0, tiles - 1)) % tiles
    tile_ids = jnp.arange(tiles)
    counts = jnp.where(tile_ids == full_tile, slots, counts)
    counts = jnp.where(tile_ids == sparse_tile, least, counts)
    live = jnp.arange(slots)[None, :] < counts[:, None]
    return jnp.where(live, orders, -1).astype(jnp.int32)


def tile_levels():
    rows = jnp.arange(N_ROW, dtype=jnp.int32)[:, None]
    cols = jnp.arange(N_COL, dtype=jnp.int32)[None, :]
    return band_level((2 * rows + 1) * N_COL, (2 * cols + 1) * N_ROW, 2 * N_ROW * N_COL).reshape(-1)


def draw_a_index(key, part):
    key = jax.random.fold_in(key, 11)
    return draw_pattern(key, tile_levels(), MBD * PK, SA).reshape(N_ROW, N_COL, SA)


def draw_b_index(key, part):
    key = jax.random.fold_in(key, 23)
    rows = jnp.arange(N_ROW, dtype=jnp.int32)[:, None, None]
    cols = jnp.arange(N_COL, dtype=jnp.int32)[None, :, None]
    inner = jnp.arange(N_COL // N_ROW, dtype=jnp.int32)[None, None, :]
    panel = rows * (N_COL // N_ROW) + inner
    levels = band_level(2 * panel + 1 + 0 * cols, 2 * cols + 1 + 0 * panel, 2 * N_COL).reshape(-1)
    return draw_pattern(key, levels, PK * NBD, SB).reshape(N_ROW, N_COL, N_COL // N_ROW, SB)


def draw_c_index(key, part):
    key = jax.random.fold_in(key, 37)
    return draw_pattern(key, tile_levels(), MBD * NBD, SC).reshape(N_ROW, N_COL, SC)


def steps_of(stream_key, extent, pieces, smallest, largest):
    gain, own = 1.0, jax.random.fold_in(stream_key, 6)
    for dim, shards_of in pieces:
        steps = jnp.exp(jax.random.uniform(jax.random.fold_in(own, dim), (shards_of,), jnp.float32, smallest / len(pieces), largest / len(pieces)))
        gain = gain * jnp.repeat(steps, extent[dim] // shards_of).reshape([-1 if axis == dim else 1 for axis in range(len(extent))])
    return gain


def bell_draw(key, dims, spread, limit, cuts=(), kind=jnp.bfloat16):
    values = spread * jax.random.normal(key, dims, jnp.float32)
    if cuts:
        values = values * steps_of(key, dims, cuts, -0.22, 0.18)
    return jnp.clip(values, -limit, limit).astype(kind)


def setup_inputs(seed: int = 0) -> dict:
    streams_of = jax.random.split(jax.random.key(seed), 6)
    a_blocks = bell_draw(streams_of[0], (N_ROW, N_COL, SA, BS, BS), 0.2, 1.2, ((0, 8), (1, 16)), jnp.float32)
    a_index = draw_a_index(jax.random.fold_in(streams_of[5], 71), 0)
    b_blocks = bell_draw(streams_of[2], (N_ROW, N_COL, H, SB, BS, BS), 0.2, 1.2, ((0, 8), (1, 16)), jnp.float32)
    b_index = draw_b_index(jax.random.fold_in(streams_of[5], 71), 0)
    c_index = draw_c_index(jax.random.fold_in(streams_of[5], 71), 0)
    return {"a_blocks": a_blocks, "a_index": a_index, "b_blocks": b_blocks, "b_index": b_index, "c_index": c_index}


def panel_product(a_tile, a_where, b_tile, b_where, height, depth, width):
    size = a_tile.shape[-1]
    a_live = a_where >= 0
    a_rows = jnp.where(a_live, a_where // depth, -1)
    a_inner = jnp.where(a_live, a_where % depth, -1)
    b_live = b_where >= 0
    b_inner = jnp.where(b_live, b_where // width, -2)
    b_cols = jnp.where(b_live, b_where % width, -1)
    spots = jnp.arange(width, dtype=jnp.int32)
    match = (a_inner[:, None, None] == b_inner[None, :, None]) & (b_cols[None, :, None] == spots[None, None, :])
    picker = match.astype(jnp.float32)
    chosen = jnp.einsum('stj,txy->sxjy', picker, b_tile, precision=lax.Precision.HIGHEST)
    chosen = chosen.reshape(a_tile.shape[0], size, width * size)
    product = jnp.einsum('sab,sbc->sac', a_tile, chosen, precision=lax.Precision.HIGHEST)
    levels = jnp.arange(height, dtype=jnp.int32)
    placer = (a_rows[None, :] == levels[:, None]).astype(jnp.float32)
    return jnp.einsum('is,sac->iac', placer, product, precision=lax.Precision.HIGHEST)


def extract(total, index, height, width):
    size = total.shape[1]
    blocks = total.reshape(height, size, width, size)
    places = jnp.arange(height * width, dtype=jnp.int32).reshape(height, width)
    picker = (index[:, None, None] == places[None, :, :]).astype(jnp.float32)
    return jnp.einsum('sij,iajb->sab', picker, blocks, precision=lax.Precision.HIGHEST)


def reference(a_blocks, a_index, b_blocks, b_index, c_index):
    hold = N_COL // N_ROW

    def one_row(row_args):
        a_row, a_where, c_where = row_args

        def add_panel(total, panel):
            a_tile = a_row[panel]
            a_spots = a_where[panel]
            owner = panel // hold
            inner = panel % hold
            b_part = b_blocks[owner, :, inner]
            b_spots = b_index[owner, :, inner]
            terms = jax.vmap(lambda blk, idx: panel_product(a_tile, a_spots, blk, idx, MBD, PK, NBD))(b_part, b_spots)
            return total + terms, None

        start = jnp.zeros((N_COL, MBD, BS, NBD * BS), jnp.float32)
        total, _ = lax.scan(add_panel, start, jnp.arange(N_COL, dtype=jnp.int32))
        return jax.vmap(lambda dense, idx: extract(dense, idx, MBD, NBD))(total, c_where)

    return lax.map(one_row, (a_blocks, a_index, c_index))
```

```python
import functools

import jax
import jax.numpy as jnp
from jax import lax
from jax.experimental import pallas as pl
from jax.experimental.pallas import tpu as pltpu
from jax.sharding import PartitionSpec as P

PK = 8
NBD = 8
CAP = 6
AHEAD = 4


def targets(a_where, b_where):
    meet = (a_where >= 0) & (b_where >= 0) & (a_where % PK == b_where // NBD)
    return jnp.where(meet, (a_where // PK) * NBD + b_where % NBD, -2)


def pack_kernel(order_ref, count_ref, blocks_ref, *rest):
    outs, sems = rest[:2], rest[2]

    def each(act):
        for half in range(2):
            for e in range(CAP):

                @pl.when(e < count_ref[half])
                def _():
                    act(
                        pltpu.make_async_copy(
                            blocks_ref.at[order_ref[half, e]],
                            outs[half].at[e],
                            sems.at[half, e],
                        )
                    )

    each(lambda copy: copy.start())
    each(lambda copy: copy.wait())


def pack(order, count, blocks):
    whole = pl.BlockSpec((CAP,) + blocks.shape[1:], lambda i, *_: (0, 0, 0))
    return pl.pallas_call(
        pack_kernel,
        grid_spec=pltpu.PrefetchScalarGridSpec(
            num_scalar_prefetch=2,
            grid=(1,),
            in_specs=[pl.BlockSpec(memory_space=pl.ANY)],
            out_specs=[whole] * 2,
            scratch_shapes=[pltpu.SemaphoreType.DMA((2, CAP))],
        ),
        out_shape=[jax.ShapeDtypeStruct((CAP,) + blocks.shape[1:], blocks.dtype)] * 2,
        compiler_params=pltpu.CompilerParams(vmem_limit_bytes=48 << 20),
        name="pack",
    )(order, count, blocks)


def product_kernel(first, parts, a_at, b_part, b_at, c_at, count_ref, a_ref, *rest):
    b_refs, rest = rest[:parts], rest[parts:]
    if first:
        out_ref, a_buf, b_buf, a_sem, b_sem = rest
    else:
        sum_ref, out_ref, a_buf, b_buf, a_sem, b_sem = rest

    def a_copy(n):
        slot = n % AHEAD
        return pltpu.make_async_copy(a_ref.at[a_at[n]], a_buf.at[slot], a_sem.at[slot])

    def b_copy(n, part):
        slot = n % AHEAD
        return pltpu.make_async_copy(b_refs[part].at[b_at[n]], b_buf.at[slot], b_sem.at[slot])

    def fetch(n):
        a_copy(n).start()
        for part in range(parts):

            @pl.when(b_part[n] == part)
            def _():
                b_copy(n, part).start()

    count = count_ref[0]
    for n in range(AHEAD):

        @pl.when(n < count)
        def _():
            fetch(n)

    if first:
        out_ref[...] = jnp.zeros_like(out_ref)
    else:
        out_ref[...] = sum_ref[...]

    def step(n, carry):
        a_copy(n).wait()
        b_copy(n, 0).wait()
        slot = n % AHEAD
        out_ref[c_at[n]] += jnp.dot(
            a_buf[slot],
            b_buf[slot],
            precision=lax.Precision.HIGHEST,
            preferred_element_type=jnp.float32,
        )

        @pl.when(n + AHEAD < count)
        def _():
            fetch(n + AHEAD)

        return carry

    lax.fori_loop(0, count, step, 0)


def products(lists, count, a_all, b_parts, total, slots):
    first = total is None
    size = a_all.shape[-1]
    whole = pl.BlockSpec((slots, size, size), lambda i, *_: (0, 0, 0))
    anywhere = pl.BlockSpec(memory_space=pl.ANY)
    return pl.pallas_call(
        functools.partial(product_kernel, first, len(b_parts)),
        grid_spec=pltpu.PrefetchScalarGridSpec(
            num_scalar_prefetch=5,
            grid=(1,),
            in_specs=[anywhere] * (1 + len(b_parts)) + ([] if first else [whole]),
            out_specs=whole,
            scratch_shapes=[
                pltpu.VMEM((AHEAD, size, size), jnp.float32),
                pltpu.VMEM((AHEAD, size, size), jnp.float32),
                pltpu.SemaphoreType.DMA((AHEAD,)),
                pltpu.SemaphoreType.DMA((AHEAD,)),
            ],
        ),
        out_shape=jax.ShapeDtypeStruct((slots, size, size), jnp.float32),
        compiler_params=pltpu.CompilerParams(vmem_limit_bytes=48 << 20),
        name="products",
    )(*lists, count, a_all, *b_parts, *([] if first else [total]))


def before(flags):
    n = flags.shape[0]
    earlier = jnp.arange(n)[None, :] < jnp.arange(n)[:, None]
    return jnp.sum(jnp.where(earlier & flags[None, :], 1, 0), axis=1, dtype=jnp.int32)


def listed(flags, place, values, length):
    hit = flags[None, :] & (place[None, :] == jnp.arange(length)[:, None])
    return [jnp.sum(jnp.where(hit, v[None, :], 0), axis=1, dtype=jnp.int32) for v in values]


def ring(block, rows, step):
    return lax.ppermute(block, "row", [((i + 2 * step) % rows, i) for i in range(rows)])


def around(block, rows):
    behind, ahead = ring(block, rows, -1), ring(block, rows, 1)
    far = (ring(behind[: CAP // 2], rows, -1), ring(ahead[CAP // 2 :], rows, 1))
    return [block, behind, ahead, *far]


def per_device(a_blocks, a_index, b_blocks, b_index, c_index):
    rows = lax.axis_size("row")
    columns = lax.axis_size("col")
    row = lax.axis_index("row")
    column = lax.axis_index("col")
    hold = columns // rows
    sa, sb, sc = a_blocks.shape[2], b_blocks.shape[3], c_index.shape[2]
    held = hold * sb
    size = a_blocks.shape[-1]
    half = row % 2

    mine = jnp.concatenate([a_index[0, 0], b_index[0, 0].reshape(-1), c_index[0, 0]])
    mine = jnp.pad(mine, (0, 128 - mine.shape[0]))[None]
    spots = lax.all_gather(mine, ("row", "col"), tiled=True).reshape(rows, columns, -1)
    a_all = lax.all_gather(a_blocks[0, 0], "col").reshape(columns * sa, size, size)
    a_where = spots[:, :, :sa]
    b_where = spots[:, :, sa : sa + held]
    c_where = spots[:, :, sa + held : sa + held + sc]

    a_wide = jnp.repeat(a_where.transpose(0, 2, 1), sb, axis=2)
    b_wide = b_where.transpose(1, 0, 2).reshape(columns, rows * held)

    def needed(b_line, c_column):
        lands = targets(a_wide, b_line[None, None, :])
        kept = lands[:, :, None, :] == c_column[:, None, :, None]
        kept = kept.reshape(rows // 2, 2, sa, sc, rows * held)
        return jnp.any(kept, axis=(0, 2, 3)).reshape(2, rows, held)

    b_mine = lax.dynamic_index_in_dim(b_wide, column, 0, keepdims=False)
    c_mine = lax.dynamic_index_in_dim(c_where, column, 1, keepdims=False)
    need = needed(b_mine, c_mine)
    earlier = jnp.arange(held)[None, :] < jnp.arange(held)[:, None]
    place = jnp.sum(
        jnp.where(earlier & need[:, :, None, :], 1, 0), axis=3, dtype=jnp.int32
    )

    own_need = lax.dynamic_index_in_dim(need, row, 1, keepdims=False)
    own_place = lax.dynamic_index_in_dim(place, row, 1, keepdims=False)
    own_count = jnp.sum(own_need, axis=1, dtype=jnp.int32)

    a_row = lax.dynamic_index_in_dim(a_wide, row, 0, keepdims=False)
    lands = targets(a_row, b_mine[None, :])
    hits = lands[:, None, :] == c_index[0, 0][None, :, None]
    live = jnp.any(hits, axis=1).reshape(-1)
    c_slot = jnp.sum(
        jnp.where(hits, jnp.arange(sc)[None, :, None], 0), axis=1, dtype=jnp.int32
    ).reshape(-1)
    line = jnp.arange(columns * sb)
    a_slot = ((line // sb)[None, :] * sa + jnp.arange(sa)[:, None]).reshape(-1)
    owner = line // held
    across = owner % 2 != half
    steps = (owner // 2 - row // 2) % (rows // 2)
    b_ring = jnp.select([steps == 0, steps == 3, steps == 1], [0, 1, 2], 3)
    b_place = lax.dynamic_index_in_dim(place, half, 0, keepdims=False).reshape(-1)

    def for_all(values):
        return jnp.broadcast_to(values[None, :], (sa, columns * sb)).reshape(-1)

    counts = jnp.sum(jax.vmap(needed, in_axes=(0, 1))(b_wide, c_where), axis=3, dtype=jnp.int32)
    most = jnp.max(counts)

    b_held = b_blocks[0, 0].reshape(held, size, size)

    def one_round(turn, total):
        base = turn * CAP
        orders = [
            listed(own_need[h], own_place[h] - base, [jnp.arange(held)], CAP)[0]
            for h in range(2)
        ]
        orders = jnp.stack(orders)
        amounts = jnp.clip(own_count - base, 0, CAP)
        keep = lax.dynamic_index_in_dim(orders, half, 0)
        give = lax.dynamic_index_in_dim(orders, 1 - half, 0)
        amounts = jnp.stack([amounts[half], amounts[1 - half]])
        here, there = pack(jnp.concatenate([keep, give]), amounts, b_held)
        crossed = lax.ppermute(there, "row", [(i ^ 1, i) for i in range(rows)])
        parts = around(here, rows) + around(crossed, rows)

        spot = b_place - base
        late = (b_ring == 3) & (spot >= CAP // 2)
        part = b_ring + jnp.where(late, 1, 0) + jnp.where(across, 5, 0)
        spot_in = spot - jnp.where(late, CAP // 2, 0)
        now = live & for_all((spot >= 0) & (spot < CAP))
        lists = listed(
            now,
            before(now),
            [a_slot, for_all(part), for_all(spot_in), c_slot],
            now.shape[0],
        )
        return products(lists, jnp.sum(now, dtype=jnp.int32)[None], a_all, parts, total, sc)

    total = one_round(0, None)
    rounds = (most + CAP - 1) // CAP
    _, total = lax.while_loop(
        lambda state: state[0] < rounds,
        lambda state: (state[0] + 1, one_round(state[0], state[1])),
        (jnp.int32(1), total),
    )
    return total[None, None]


def solution(mesh):
    in_specs = (
        P("row", "col", None, None, None),
        P("row", "col", None),
        P("row", "col", None, None, None, None),
        P("row", "col", None, None),
        P("row", "col", None),
    )
    out_specs = P("row", "col", None, None, None)
    return jax.shard_map(
        per_device, mesh=mesh, in_specs=in_specs, out_specs=out_specs, check_vma=False
    )
```

```python
import functools

import jax
import jax.numpy as jnp
from jax import lax
from jax.experimental import pallas as pl
from jax.experimental.pallas import tpu as pltpu
from jax.sharding import PartitionSpec as P

PK = 8
NBD = 8
CAP = 6
AHEAD = 4


def targets(a_where, b_where):
    meet = (a_where >= 0) & (b_where >= 0) & (a_where % PK == b_where // NBD)
    return jnp.where(meet, (a_where // PK) * NBD + b_where % NBD, -2)


def pack_kernel(order_ref, count_ref, blocks_ref, *rest):
    outs, sems = rest[:2], rest[2]

    def each(act):
        for half in range(2):
            for e in range(CAP):

                @pl.when(e < count_ref[half])
                def _():
                    act(
                        pltpu.make_async_copy(
                            blocks_ref.at[order_ref[half, e]],
                            outs[half].at[e],
                            sems.at[half, e],
                        )
                    )

    each(lambda copy: copy.start())
    each(lambda copy: copy.wait())


def pack(order, count, blocks):
    whole = pl.BlockSpec((CAP,) + blocks.shape[1:], lambda i, *_: (0, 0, 0))
    return pl.pallas_call(
        pack_kernel,
        grid_spec=pltpu.PrefetchScalarGridSpec(
            num_scalar_prefetch=2,
            grid=(1,),
            in_specs=[pl.BlockSpec(memory_space=pl.ANY)],
            out_specs=[whole] * 2,
            scratch_shapes=[pltpu.SemaphoreType.DMA((2, CAP))],
        ),
        out_shape=[jax.ShapeDtypeStruct((CAP,) + blocks.shape[1:], blocks.dtype)] * 2,
        compiler_params=pltpu.CompilerParams(vmem_limit_bytes=48 << 20),
        name="pack",
    )(order, count, blocks)


def product_kernel(first, parts, a_at, b_part, b_at, c_at, count_ref, a_ref, *rest):
    b_refs, rest = rest[:parts], rest[parts:]
    if first:
        out_ref, a_buf, b_buf, a_sem, b_sem = rest
    else:
        sum_ref, out_ref, a_buf, b_buf, a_sem, b_sem = rest

    def a_copy(n):
        slot = n % AHEAD
        return pltpu.make_async_copy(a_ref.at[a_at[n]], a_buf.at[slot], a_sem.at[slot])

    def b_copy(n, part):
        slot = n % AHEAD
        return pltpu.make_async_copy(b_refs[part].at[b_at[n]], b_buf.at[slot], b_sem.at[slot])

    def fetch(n):
        a_copy(n).start()
        for part in range(parts):

            @pl.when(b_part[n] == part)
            def _():
                b_copy(n, part).start()

    count = count_ref[0]
    for n in range(AHEAD):

        @pl.when(n < count)
        def _():
            fetch(n)

    if first:
        out_ref[...] = jnp.zeros_like(out_ref)
    else:
        out_ref[...] = sum_ref[...]

    def step(n, carry):
        a_copy(n).wait()
        b_copy(n, 0).wait()
        slot = n % AHEAD
        out_ref[c_at[n]] += jnp.dot(
            a_buf[slot],
            b_buf[slot],
            precision=lax.Precision.HIGHEST,
            preferred_element_type=jnp.float32,
        )

        @pl.when(n + AHEAD < count)
        def _():
            fetch(n + AHEAD)

        return carry

    lax.fori_loop(0, count, step, 0)


def products(lists, count, a_all, b_parts, total, slots):
    first = total is None
    size = a_all.shape[-1]
    whole = pl.BlockSpec((slots, size, size), lambda i, *_: (0, 0, 0))
    anywhere = pl.BlockSpec(memory_space=pl.ANY)
    return pl.pallas_call(
        functools.partial(product_kernel, first, len(b_parts)),
        grid_spec=pltpu.PrefetchScalarGridSpec(
            num_scalar_prefetch=5,
            grid=(1,),
            in_specs=[anywhere] * (1 + len(b_parts)) + ([] if first else [whole]),
            out_specs=whole,
            scratch_shapes=[
                pltpu.VMEM((AHEAD, size, size), jnp.float32),
                pltpu.VMEM((AHEAD, size, size), jnp.float32),
                pltpu.SemaphoreType.DMA((AHEAD,)),
                pltpu.SemaphoreType.DMA((AHEAD,)),
            ],
        ),
        out_shape=jax.ShapeDtypeStruct((slots, size, size), jnp.float32),
        compiler_params=pltpu.CompilerParams(vmem_limit_bytes=48 << 20),
        name="products",
    )(*lists, count, a_all, *b_parts, *([] if first else [total]))


def before(flags):
    n = flags.shape[0]
    earlier = jnp.arange(n)[None, :] < jnp.arange(n)[:, None]
    return jnp.sum(jnp.where(earlier & flags[None, :], 1, 0), axis=1, dtype=jnp.int32)


def listed(flags, place, values, length):
    hit = flags[None, :] & (place[None, :] == jnp.arange(length)[:, None])
    return [jnp.sum(jnp.where(hit, v[None, :], 0), axis=1, dtype=jnp.int32) for v in values]


def ring(block, rows, step):
    return lax.ppermute(block, "row", [((i + 2 * step) % rows, i) for i in range(rows)])


def around(block, rows):
    behind, ahead = ring(block, rows, -1), ring(block, rows, 1)
    far = (ring(behind[: CAP // 2], rows, -1), ring(ahead[CAP // 2 :], rows, 1))
    return [block, behind, ahead, *far]


def everywhere(mine, rows, columns):
    me = lax.axis_index("row") * columns + lax.axis_index("col")
    held = mine
    for bits in ((5, 6), (3, 4), (1, 2), (0,)):
        group = jnp.zeros((2 ** len(bits),) + held.shape, held.dtype)
        for move in range(2 ** len(bits)):
            flip = sum(((move >> n) & 1) << bit for n, bit in enumerate(bits))
            got = held
            if move:
                got = lax.ppermute(
                    held, ("row", "col"), [(i ^ flip, i) for i in range(rows * columns)]
                )
            spot = sum((((me ^ flip) >> bit) & 1) << n for n, bit in enumerate(bits))
            group = lax.dynamic_update_index_in_dim(group, got, spot, 0)
        held = group
    length = mine.shape[0]
    held = held.reshape(2, 4, 2, 2, 4, length).transpose(4, 2, 3, 1, 0, 5)
    return held.reshape(rows, columns, length)


def per_device(a_blocks, a_index, b_blocks, b_index, c_index):
    rows = lax.axis_size("row")
    columns = lax.axis_size("col")
    row = lax.axis_index("row")
    column = lax.axis_index("col")
    hold = columns // rows
    sa, sb, sc = a_blocks.shape[2], b_blocks.shape[3], c_index.shape[2]
    held = hold * sb
    size = a_blocks.shape[-1]
    half = row % 2

    mine = jnp.concatenate([a_index[0, 0], b_index[0, 0].reshape(-1), c_index[0, 0]])
    mine = jnp.pad(mine, (0, 128 - mine.shape[0]))
    spots = everywhere(mine, rows, columns)
    a_all = lax.all_gather(a_blocks[0, 0], "col").reshape(columns * sa, size, size)
    a_where = spots[:, :, :sa]
    b_where = spots[:, :, sa : sa + held]
    c_where = spots[:, :, sa + held : sa + held + sc]

    a_wide = jnp.repeat(a_where.transpose(0, 2, 1), sb, axis=2)
    b_wide = b_where.transpose(1, 0, 2).reshape(columns, rows * held)

    def needed(b_line, c_column):
        lands = targets(a_wide, b_line[None, None, :])
        kept = lands[:, :, None, :] == c_column[:, None, :, None]
        kept = kept.reshape(rows // 2, 2, sa, sc, rows * held)
        return jnp.any(kept, axis=(0, 2, 3)).reshape(2, rows, held)

    b_mine = lax.dynamic_index_in_dim(b_wide, column, 0, keepdims=False)
    c_mine = lax.dynamic_index_in_dim(c_where, column, 1, keepdims=False)
    need = needed(b_mine, c_mine)
    earlier = jnp.arange(held)[None, :] < jnp.arange(held)[:, None]
    place = jnp.sum(
        jnp.where(earlier & need[:, :, None, :], 1, 0), axis=3, dtype=jnp.int32
    )

    own_need = lax.dynamic_index_in_dim(need, row, 1, keepdims=False)
    own_place = lax.dynamic_index_in_dim(place, row, 1, keepdims=False)
    own_count = jnp.sum(own_need, axis=1, dtype=jnp.int32)

    a_row = lax.dynamic_index_in_dim(a_wide, row, 0, keepdims=False)
    lands = targets(a_row, b_mine[None, :])
    hits = lands[:, None, :] == c_index[0, 0][None, :, None]
    live = jnp.any(hits, axis=1).reshape(-1)
    c_slot = jnp.sum(
        jnp.where(hits, jnp.arange(sc)[None, :, None], 0), axis=1, dtype=jnp.int32
    ).reshape(-1)
    line = jnp.arange(columns * sb)
    a_slot = ((line // sb)[None, :] * sa + jnp.arange(sa)[:, None]).reshape(-1)
    owner = line // held
    across = owner % 2 != half
    steps = (owner // 2 - row // 2) % (rows // 2)
    b_ring = jnp.select([steps == 0, steps == 3, steps == 1], [0, 1, 2], 3)
    b_place = lax.dynamic_index_in_dim(place, half, 0, keepdims=False).reshape(-1)

    def for_all(values):
        return jnp.broadcast_to(values[None, :], (sa, columns * sb)).reshape(-1)

    counts = jnp.sum(jax.vmap(needed, in_axes=(0, 1))(b_wide, c_where), axis=3, dtype=jnp.int32)
    most = jnp.max(counts)

    b_held = b_blocks[0, 0].reshape(held, size, size)

    def one_round(turn, total):
        base = turn * CAP
        orders = [
            listed(own_need[h], own_place[h] - base, [jnp.arange(held)], CAP)[0]
            for h in range(2)
        ]
        orders = jnp.stack(orders)
        amounts = jnp.clip(own_count - base, 0, CAP)
        keep = lax.dynamic_index_in_dim(orders, half, 0)
        give = lax.dynamic_index_in_dim(orders, 1 - half, 0)
        amounts = jnp.stack([amounts[half], amounts[1 - half]])
        here, there = pack(jnp.concatenate([keep, give]), amounts, b_held)
        crossed = lax.ppermute(there, "row", [(i ^ 1, i) for i in range(rows)])
        parts = around(here, rows) + around(crossed, rows)

        spot = b_place - base
        late = (b_ring == 3) & (spot >= CAP // 2)
        part = b_ring + jnp.where(late, 1, 0) + jnp.where(across, 5, 0)
        spot_in = spot - jnp.where(late, CAP // 2, 0)
        now = live & for_all((spot >= 0) & (spot < CAP))
        lists = listed(
            now,
            before(now),
            [a_slot, for_all(part), for_all(spot_in), c_slot],
            now.shape[0],
        )
        return products(lists, jnp.sum(now, dtype=jnp.int32)[None], a_all, parts, total, sc)

    total = one_round(0, None)
    rounds = (most + CAP - 1) // CAP
    _, total = lax.while_loop(
        lambda state: state[0] < rounds,
        lambda state: (state[0] + 1, one_round(state[0], state[1])),
        (jnp.int32(1), total),
    )
    return total[None, None]


def solution(mesh):
    in_specs = (
        P("row", "col", None, None, None),
        P("row", "col", None),
        P("row", "col", None, None, None, None),
        P("row", "col", None, None),
        P("row", "col", None),
    )
    out_specs = P("row", "col", None, None, None)
    return jax.shard_map(
        per_device, mesh=mesh, in_specs=in_specs, out_specs=out_specs, check_vma=False
    )
```

```python
import functools

import jax
import jax.numpy as jnp
from jax import lax
from jax.experimental import pallas as pl
from jax.experimental.pallas import tpu as pltpu
from jax.sharding import PartitionSpec as P

PK = 8
NBD = 8
CROSS = 6
FAR = 2
AHEAD = 8


def targets(a_where, b_where):
    meet = (a_where >= 0) & (b_where >= 0) & (a_where % PK == b_where // NBD)
    return jnp.where(meet, (a_where // PK) * NBD + b_where % NBD, -2)


def code(a_slot, part, at, c_slot):
    return ((a_slot * 16 + part) * 128 + at) * 16 + c_slot


def a_of(word):
    return word >> 15


def part_of(word):
    return (word >> 11) & 15


def at_of(word):
    return (word >> 4) & 127


def c_of(word):
    return word & 15


def fetch_block(word, refs, dst, sem):
    for part, ref in enumerate(refs):

        def start(ref=ref):
            pltpu.make_async_copy(ref.at[at_of(word)], dst, sem).start()

        if len(refs) == 1:
            start()
        else:
            pl.when(part_of(word) == part)(start)


def pack_kernel(parts, slots, list_ref, count_ref, *rest):
    refs, (out_ref, sems) = rest[:parts], rest[parts:]
    for e in range(slots):

        @pl.when(e < count_ref[0])
        def _():
            fetch_block(list_ref[e], refs, out_ref.at[e], sems.at[e])

    for e in range(slots):

        @pl.when(e < count_ref[0])
        def _():
            pltpu.make_async_copy(refs[0].at[0], out_ref.at[e], sems.at[e]).wait()


def pack(listing, count, blocks, slots):
    size = blocks[0].shape[-1]
    return pl.pallas_call(
        functools.partial(pack_kernel, len(blocks), slots),
        in_specs=[pl.BlockSpec(memory_space=pltpu.SMEM)] * 2
        + [pl.BlockSpec(memory_space=pl.ANY)] * len(blocks),
        out_specs=pl.BlockSpec(memory_space=pltpu.VMEM),
        scratch_shapes=[pltpu.SemaphoreType.DMA((slots,))],
        out_shape=jax.ShapeDtypeStruct((slots, size, size), jnp.float32),
        compiler_params=pltpu.CompilerParams(vmem_limit_bytes=16 << 20),
        name="pack",
    )(listing, count, *blocks)


def halves(x):
    high = x.astype(jnp.bfloat16)
    return high, (x - high.astype(jnp.float32)).astype(jnp.bfloat16)


def block_product(a, b):
    a_high, a_low = halves(a)
    b_high, b_low = halves(b)
    dot = functools.partial(jnp.dot, preferred_element_type=jnp.float32)
    return dot(a_high, b_high) + (dot(a_high, b_low) + dot(a_low, b_high))


def product_kernel(first, parts, list_ref, count_ref, a_ref, *rest):
    b_refs, rest = rest[:parts], rest[parts:]
    out_ref, a_buf, b_buf, a_sem, b_sem = rest if first else rest[1:]
    count = count_ref[0]

    def fetch(n):
        slot = n % AHEAD
        word = list_ref[n]
        pltpu.make_async_copy(a_ref.at[a_of(word)], a_buf.at[slot], a_sem.at[slot]).start()
        fetch_block(word, b_refs, b_buf.at[slot], b_sem.at[slot])

    for n in range(AHEAD):

        @pl.when(n < count)
        def _():
            fetch(n)

    if first:
        out_ref[...] = jnp.zeros_like(out_ref)

    def step(n, carry):
        slot = n % AHEAD
        pltpu.make_async_copy(a_ref.at[0], a_buf.at[slot], a_sem.at[slot]).wait()
        pltpu.make_async_copy(b_refs[0].at[0], b_buf.at[slot], b_sem.at[slot]).wait()
        out_ref[c_of(list_ref[n])] += block_product(a_buf[slot], b_buf[slot])

        @pl.when(n + AHEAD < count)
        def _():
            fetch(n + AHEAD)

        return carry

    lax.fori_loop(0, count, step, 0)


def products(listing, count, a_all, b_parts, total, slots):
    first = total is None
    size = a_all.shape[-1]
    smem = pl.BlockSpec(memory_space=pltpu.SMEM)
    vmem = pl.BlockSpec(memory_space=pltpu.VMEM)
    anywhere = pl.BlockSpec(memory_space=pl.ANY)
    operands = [listing, count, a_all, *b_parts] + ([] if first else [total])
    return pl.pallas_call(
        functools.partial(product_kernel, first, len(b_parts)),
        in_specs=[smem, smem, anywhere] + [anywhere] * len(b_parts) + ([] if first else [vmem]),
        out_specs=vmem,
        scratch_shapes=[
            pltpu.VMEM((AHEAD, size, size), jnp.float32),
            pltpu.VMEM((AHEAD, size, size), jnp.float32),
            pltpu.SemaphoreType.DMA((AHEAD,)),
            pltpu.SemaphoreType.DMA((AHEAD,)),
        ],
        out_shape=jax.ShapeDtypeStruct((slots, size, size), jnp.float32),
        input_output_aliases={} if first else {len(operands) - 1: 0},
        compiler_params=pltpu.CompilerParams(vmem_limit_bytes=16 << 20),
        cost_estimate=pl.CostEstimate(
            flops=8 * 3 * 2 * size**3, bytes_accessed=24 * size * size * 4, transcendentals=0
        ),
        name="products",
    )(*operands)


def before(flags):
    n = flags.shape[0]
    earlier = jnp.arange(n)[None, :] < jnp.arange(n)[:, None]
    return jnp.sum(jnp.where(earlier & flags[None, :], 1, 0), axis=1, dtype=jnp.int32)


def listed(flags, place, values, length):
    hit = flags[None, :] & (place[None, :] == jnp.arange(length)[:, None])
    count = jnp.sum(flags, dtype=jnp.int32)
    return jnp.sum(jnp.where(hit, values[None, :], 0), axis=1, dtype=jnp.int32), count[None]


def ring(block, rows, step):
    return lax.ppermute(block, "row", [((i + 2 * step) % rows, i) for i in range(rows)])


def everywhere(mine, rows, columns):
    me = lax.axis_index("row") * columns + lax.axis_index("col")
    held = mine
    for bits in ((5, 6), (3, 4), (1, 2), (0,)):
        group = jnp.zeros((2 ** len(bits),) + held.shape, held.dtype)
        for move in range(2 ** len(bits)):
            flip = sum(((move >> n) & 1) << bit for n, bit in enumerate(bits))
            got = held
            if move:
                got = lax.ppermute(
                    held, ("row", "col"), [(i ^ flip, i) for i in range(rows * columns)]
                )
            spot = sum((((me ^ flip) >> bit) & 1) << n for n, bit in enumerate(bits))
            group = lax.dynamic_update_index_in_dim(group, got, spot, 0)
        held = group
    length = mine.shape[0]
    held = held.reshape(2, 4, 2, 2, 4, length).transpose(4, 2, 3, 1, 0, 5)
    return held.reshape(rows, columns, length)


def per_device(a_blocks, a_index, b_blocks, b_index, c_index):
    rows = lax.axis_size("row")
    columns = lax.axis_size("col")
    row = lax.axis_index("row")
    column = lax.axis_index("col")
    hold = columns // rows
    sa, sb, sc = a_blocks.shape[2], b_blocks.shape[3], c_index.shape[2]
    held = hold * sb
    lines = columns * sb
    size = a_blocks.shape[-1]
    ys = rows // 2

    def pick(array, i, axis=0):
        return lax.dynamic_index_in_dim(array, i, axis, keepdims=False)

    own = b_blocks[0, 0].reshape(held, size, size)
    behind, ahead = ring(own, rows, -1), ring(own, rows, 1)
    a_all = lax.all_gather(a_blocks[0, 0], "col").reshape(columns * sa, size, size)

    mine = jnp.concatenate([a_index[0, 0], b_index[0, 0].reshape(-1), c_index[0, 0]])
    mine = jnp.pad(mine, (0, 128 - mine.shape[0]))
    spots = everywhere(mine, rows, columns)
    a_where = spots[:, :, :sa]
    b_where = spots[:, :, sa : sa + held]
    c_where = spots[:, :, sa + held : sa + held + sc]

    a_wide = jnp.repeat(a_where.transpose(0, 2, 1), sb, axis=2)
    b_wide = b_where.transpose(1, 0, 2).reshape(columns, lines)
    b_mine = pick(b_wide, column)

    line = jnp.arange(lines)
    owner = line // held
    slot = line % held
    row_ids = jnp.arange(rows)
    across = owner[None, :] % 2 != row_ids[:, None] % 2
    far = (owner[None, :] // 2 - row_ids[:, None] // 2) % ys == 2

    def needs(b_line, c_column):
        lands = targets(a_wide, b_line[None, None, :])
        kept = lands[:, :, None, :] == c_column[:, None, :, None]
        need = jnp.any(kept, axis=(1, 2))
        return need, jnp.any(need & far, axis=0)

    earlier = line[None, :] < line[:, None]
    same = owner[None, :] == owner[:, None]

    need, forward = needs(b_mine, pick(c_where, column, 1))
    far_place = jnp.sum(
        jnp.where(earlier & same & forward[None, :], 1, 0), axis=1, dtype=jnp.int32
    )
    reached = ~far | (far_place < 2 * FAR)[None, :]
    crossing = need & across & reached
    cross_place = jnp.sum(
        jnp.where(earlier[None] & crossing[:, None, :], 1, 0), axis=2, dtype=jnp.int32
    )

    def forwarded(block, holder, odd, step):
        mine_to_send = (
            forward & (owner == holder) & (far_place % 2 == odd) & (far_place < 2 * FAR)
        )
        listing = listed(mine_to_send, far_place // 2, code(0, 0, slot, 0), FAR)
        return ring(pack(*listing, [block], FAR), rows, step)

    far_even = forwarded(behind, (row - 2) % rows, 0, -1)
    far_odd = forwarded(ahead, (row + 2) % rows, 1, 1)
    near = [own, behind, ahead, far_even, far_odd]

    steps = (owner // 2 - row // 2) % ys
    part = jnp.select([steps == 0, steps == 3, steps == 1], [0, 1, 2], 3 + far_place % 2)
    at = jnp.where(steps == 2, far_place // 2, slot)

    give, give_place = pick(crossing, row ^ 1), pick(cross_place, row ^ 1)
    packed = pack(
        *listed(give & (give_place < CROSS), give_place, code(0, part, at, 0), CROSS), near, CROSS
    )
    crossed = lax.ppermute(packed, "row", [(i ^ 1, i) for i in range(rows)])

    hits = targets(pick(a_wide, row), b_mine[None, :])[:, None, :] == c_index[0, 0][None, :, None]
    live = jnp.any(hits, axis=1).reshape(-1)
    c_slot = jnp.sum(
        jnp.where(hits, jnp.arange(sc)[None, :, None], 0), axis=1, dtype=jnp.int32
    ).reshape(-1)
    a_slot = ((line // sb)[None, :] * sa + jnp.arange(sa)[:, None]).reshape(-1)

    def for_all(values):
        return jnp.broadcast_to(values[None, :], (sa, lines)).reshape(-1)

    my_across, my_reached, my_place = pick(across, row), pick(reached, row), pick(cross_place, row)
    by_ring = ~my_across & my_reached
    by_cross = my_across & my_reached & (my_place < CROSS)

    def add(total, chosen, blocks, part, at):
        now = live & for_all(chosen)
        words = code(a_slot, for_all(part), for_all(at), c_slot)
        listing = listed(now, before(now), words, now.shape[0])
        return products(*listing, a_all, blocks, total, sc)

    total = add(None, by_ring, near, part, at)
    total = add(total, by_cross, [crossed], 0 * line, my_place)

    def overflow(b_line, c_column):
        need, forward = needs(b_line, c_column)
        across_count = jnp.sum(need & across, axis=1, dtype=jnp.int32)
        far_count = jnp.sum(forward.reshape(rows, held), axis=1, dtype=jnp.int32)
        return (across_count > CROSS) | (far_count > 2 * FAR)

    trips = jnp.any(jax.vmap(overflow, in_axes=(0, 1))(b_wide, c_where)).astype(jnp.int32)

    def trip(state):
        done, total = state
        whole = lax.all_gather(own, "row").reshape(rows * held, size, size)
        return done + 1, add(total, ~by_ring & ~by_cross, [whole], 0 * line, line)

    _, total = lax.while_loop(lambda state: state[0] < trips, trip, (jnp.int32(0), total))
    return total[None, None]


def solution(mesh):
    in_specs = (
        P("row", "col", None, None, None),
        P("row", "col", None),
        P("row", "col", None, None, None, None),
        P("row", "col", None, None),
        P("row", "col", None),
    )
    out_specs = P("row", "col", None, None, None)
    return jax.shard_map(
        per_device, mesh=mesh, in_specs=in_specs, out_specs=out_specs, check_vma=False
    )
```

```python
import functools

import jax
import jax.numpy as jnp
from jax import lax
from jax.experimental import pallas as pl
from jax.experimental.pallas import tpu as pltpu
from jax.sharding import Mesh
from jax.sharding import PartitionSpec as P

PK = 8
NBD = 8
NEAR = 6
AHEAD_FAR, BEHIND_FAR = 2, 1
COL = ("x_lo", "z", "core")
AHEAD = 8


def targets(a_where, b_where):
    meet = (a_where >= 0) & (b_where >= 0) & (a_where % PK == b_where // NBD)
    return jnp.where(meet, (a_where // PK) * NBD + b_where % NBD, -2)


def code(a_slot, part, at, c_slot):
    return ((a_slot * 16 + part) * 128 + at) * 16 + c_slot


def a_of(word):
    return word >> 15


def part_of(word):
    return (word >> 11) & 15


def at_of(word):
    return (word >> 4) & 127


def c_of(word):
    return word & 15


def fetch_block(part, at, refs, dst, sem):
    for i, ref in enumerate(refs):

        def start(ref=ref):
            pltpu.make_async_copy(ref.at[at], dst, sem).start()

        if len(refs) == 1:
            start()
        else:
            pl.when(part == i)(start)


def pack_kernel(parts, sizes, list_ref, *rest):
    refs, outs, sems = rest[:parts], rest[parts + 1 : parts + 1 + len(sizes)], rest[-1]
    places = [(i, e) for i, size in enumerate(sizes) for e in range(size)]
    for n, (i, e) in enumerate(places):

        @pl.when(list_ref[n] >= 0)
        def _():
            word = list_ref[n]
            fetch_block(part_of(word), at_of(word), refs, outs[i].at[e], sems.at[n])

    for n, (i, e) in enumerate(places):

        @pl.when(list_ref[n] >= 0)
        def _():
            pltpu.make_async_copy(refs[0].at[0], outs[i].at[e], sems.at[n]).wait()


def pack(listing, blocks, sizes, later):
    size = blocks[0].shape[-1]
    anywhere = pl.BlockSpec(memory_space=pl.ANY)
    return pl.pallas_call(
        functools.partial(pack_kernel, len(blocks), sizes),
        in_specs=[pl.BlockSpec(memory_space=pltpu.SMEM)] + [anywhere] * (len(blocks) + 1),
        out_specs=[pl.BlockSpec(memory_space=pltpu.VMEM)] * len(sizes) + [anywhere],
        scratch_shapes=[pltpu.SemaphoreType.DMA((sum(sizes),))],
        out_shape=[jax.ShapeDtypeStruct((n, size, size), jnp.float32) for n in sizes]
        + [jax.ShapeDtypeStruct(later.shape, later.dtype)],
        input_output_aliases={1 + len(blocks): len(sizes)},
        compiler_params=pltpu.CompilerParams(vmem_limit_bytes=16 << 20),
        name="pack",
    )(listing, *blocks, later)


def halves(x):
    high = x.astype(jnp.bfloat16)
    return high, (x - high.astype(jnp.float32)).astype(jnp.bfloat16)


def block_product(a, b):
    a_high, a_low = halves(a)
    b_high, b_low = halves(b)
    dot = functools.partial(jnp.dot, preferred_element_type=jnp.float32)
    return dot(a_high, b_high) + (dot(a_high, b_low) + dot(a_low, b_high))


def product_kernel(first, a_parts, parts, list_ref, count_ref, *rest):
    a_refs, b_refs, rest = rest[:a_parts], rest[a_parts : a_parts + parts], rest[a_parts + parts :]
    out_ref, a_buf, b_buf, a_sem, b_sem = rest if first else rest[1:]
    count = count_ref[0]

    def fetch(n):
        slot = n % AHEAD
        word = list_ref[n]
        fetch_block(0, a_of(word), a_refs, a_buf.at[slot], a_sem.at[slot])
        fetch_block(part_of(word), at_of(word), b_refs, b_buf.at[slot], b_sem.at[slot])

    for n in range(AHEAD):

        @pl.when(n < count)
        def _():
            fetch(n)

    if first:
        out_ref[...] = jnp.zeros_like(out_ref)

    def step(n, carry):
        slot = n % AHEAD
        pltpu.make_async_copy(a_refs[0].at[0], a_buf.at[slot], a_sem.at[slot]).wait()
        pltpu.make_async_copy(b_refs[0].at[0], b_buf.at[slot], b_sem.at[slot]).wait()
        out_ref[c_of(list_ref[n])] += block_product(a_buf[slot], b_buf[slot])

        @pl.when(n + AHEAD < count)
        def _():
            fetch(n + AHEAD)

        return carry

    lax.fori_loop(0, count, step, 0)


def products(listing, count, a_parts, b_parts, total, slots):
    first = total is None
    size = a_parts[0].shape[-1]
    smem = pl.BlockSpec(memory_space=pltpu.SMEM)
    vmem = pl.BlockSpec(memory_space=pltpu.VMEM)
    operands = [listing, count, *a_parts, *b_parts] + ([] if first else [total])
    parts = len(a_parts) + len(b_parts)
    return pl.pallas_call(
        functools.partial(product_kernel, first, len(a_parts), len(b_parts)),
        in_specs=[smem, smem]
        + [pl.BlockSpec(memory_space=pl.ANY)] * parts
        + ([] if first else [vmem]),
        out_specs=vmem,
        scratch_shapes=[
            pltpu.VMEM((AHEAD, size, size), jnp.float32),
            pltpu.VMEM((AHEAD, size, size), jnp.float32),
            pltpu.SemaphoreType.DMA((AHEAD,)),
            pltpu.SemaphoreType.DMA((AHEAD,)),
        ],
        out_shape=jax.ShapeDtypeStruct((slots, size, size), jnp.float32),
        input_output_aliases={} if first else {len(operands) - 1: 0},
        compiler_params=pltpu.CompilerParams(vmem_limit_bytes=16 << 20),
        cost_estimate=pl.CostEstimate(
            flops=8 * 3 * 2 * size**3, bytes_accessed=24 * size * size * 4, transcendentals=0
        ),
        name="products",
    )(*operands)


def before(flags):
    n = flags.shape[0]
    earlier = jnp.arange(n)[None, :] < jnp.arange(n)[:, None]
    return jnp.sum(jnp.where(earlier & flags[None, :], 1, 0), axis=1, dtype=jnp.int32)


def listed(flags, place, values, length):
    hit = flags[None, :] & (place[None, :] == jnp.arange(length)[:, None])
    count = jnp.sum(flags, dtype=jnp.int32)
    return jnp.sum(jnp.where(hit, values[None, :], 0), axis=1, dtype=jnp.int32), count[None]


def to_row(block, rows, there):
    return lax.ppermute(block, "row", [(i, there(i)) for i in range(rows)])


def everywhere(mine, rows, columns):
    axes = ("row", *COL)
    me = lax.axis_index("row") * columns + lax.axis_index(COL)
    held = mine
    for bits in ((5, 6), (3, 4), (1, 2), (0,)):
        group = jnp.zeros((2 ** len(bits),) + held.shape, held.dtype)
        for move in range(2 ** len(bits)):
            flip = sum(((move >> n) & 1) << bit for n, bit in enumerate(bits))
            got = held
            if move:
                got = lax.ppermute(held, axes, [(i ^ flip, i) for i in range(rows * columns)])
            spot = sum((((me ^ flip) >> bit) & 1) << n for n, bit in enumerate(bits))
            group = lax.dynamic_update_index_in_dim(group, got, spot, 0)
        held = group
    length = mine.shape[0]
    held = held.reshape(2, 4, 2, 2, 4, length).transpose(4, 2, 3, 1, 0, 5)
    return held.reshape(rows, columns, length)


def per_device(a_blocks, a_index, b_blocks, b_index, c_index):
    rows = lax.axis_size("row")
    columns = lax.axis_size(COL)
    row = lax.axis_index("row")
    column = lax.axis_index(COL)
    hold = columns // rows
    sa, sb, sc = a_blocks.shape[2], b_blocks.shape[3], c_index.shape[2]
    held = hold * sb
    lines = columns * sb
    size = a_blocks.shape[-1]
    ys = rows // 2

    def pick(array, i, axis=0):
        return lax.dynamic_index_in_dim(array, i, axis, keepdims=False)

    a_parts = [lax.all_gather(a_blocks[0, 0], COL).reshape(columns * sa, size, size)]

    own = b_blocks[0, 0].reshape(held, size, size)
    behind = to_row(own, rows, lambda i: (i + 2) % rows)
    ahead = to_row(own, rows, lambda i: (i - 2) % rows)
    near = [own, behind, ahead]

    mine = jnp.concatenate([a_index[0, 0], b_index[0, 0].reshape(-1), c_index[0, 0]])
    mine = jnp.pad(mine, (0, 128 - mine.shape[0]))
    spots = everywhere(mine, rows, columns)

    def split(spots):
        a_where = spots[:, :, :sa]
        b_where = spots[:, :, sa : sa + held]
        c_where = spots[:, :, sa + held : sa + held + sc]
        a_wide = jnp.repeat(a_where.transpose(0, 2, 1), sb, axis=2)
        b_wide = b_where.transpose(1, 0, 2).reshape(columns, lines)
        return a_wide, b_wide, c_where

    line = jnp.arange(lines)
    owner = line // held
    slot = line % held
    row_ids = jnp.arange(rows)
    across = owner[None, :] % 2 != row_ids[:, None] % 2
    far = (owner[None, :] // 2 - row_ids[:, None] // 2) % ys == 2
    way = jnp.where(across, 1, 0) + jnp.where(far, 2, 0)
    far_slots = AHEAD_FAR + BEHIND_FAR

    def needs(a_wide, b_line, c_column):
        lands = targets(a_wide, b_line[None, None, :])
        return jnp.any(lands[:, :, None, :] == c_column[:, None, :, None], axis=(1, 2))

    a_wide, b_wide, c_where = split(spots)
    need = needs(a_wide, pick(b_wide, column), pick(c_where, column, 1))
    earlier = line[None, :] < line[:, None]
    rank = jnp.sum(
        jnp.where(earlier[None] & need[:, None, :] & (way[:, None, :] == way[:, :, None]), 1, 0),
        axis=2,
        dtype=jnp.int32,
    )
    order = jnp.where(need, way * 128 + rank, -1)

    sends = [
        (NEAR, 1, 0, lambda i: i ^ 1),
        (AHEAD_FAR, 2, 0, lambda i: (i + 2) % rows),
        (BEHIND_FAR, 2, AHEAD_FAR, lambda i: (i - 2) % rows),
        (AHEAD_FAR, 3, 0, lambda i: ((i + 2) % rows) ^ 1),
        (BEHIND_FAR, 3, AHEAD_FAR, lambda i: ((i - 2) % rows) ^ 1),
    ]
    wanted = jnp.array([w * 128 + first + e for n, w, first, _ in sends for e in range(n)])
    goes_to = jnp.concatenate([jnp.full((n,), there(row)) for n, _, _, there in sends])
    steps = (owner // 2 - row // 2) % ys
    near_part = jnp.select([steps == 0, steps == 3], [0, 1], 2)
    hit = (order[None] == wanted[:, None, None]) & (row_ids[None, :, None] == goes_to[:, None, None])
    word = code(0, near_part, slot, 0)
    listing = jnp.sum(jnp.where(hit, word[None, None, :] + 1, 0), axis=(1, 2), dtype=jnp.int32) - 1
    *packed, spots = pack(listing, near, [n for n, *_ in sends], spots)
    arrived = [to_row(block, rows, there) for block, (*_, there) in zip(packed, sends)]

    a_wide, b_wide, c_where = split(spots)
    lands = targets(pick(a_wide, row), pick(b_wide, column)[None, :])
    hits = lands[:, None, :] == pick(pick(c_where, row), column)[None, :, None]
    live = jnp.any(hits, axis=1).reshape(-1)
    c_slot = jnp.sum(
        jnp.where(hits, jnp.arange(sc)[None, :, None], 0), axis=1, dtype=jnp.int32
    ).reshape(-1)
    a_slot = ((line // sb)[None, :] * sa + jnp.arange(sa)[:, None]).reshape(-1)

    def for_all(values):
        return jnp.broadcast_to(values[None, :], (sa, lines)).reshape(-1)

    def add(total, chosen, blocks, part, at):
        now = live & for_all(chosen)
        words = code(a_slot, for_all(part), for_all(at), c_slot)
        listing = listed(now, before(now), words, now.shape[0])
        return products(*listing, a_parts, blocks, total, sc)

    my_way, my_rank = pick(way, row), pick(rank, row)
    by_ring = my_way == 0
    back = (my_way >= 2) & (my_rank >= AHEAD_FAR)
    sent_part = jnp.where(my_way >= 2, my_way * 2 - 3, 0) + jnp.where(back, 1, 0)
    sent_at = my_rank - jnp.where(back, AHEAD_FAR, 0)
    by_send = ~by_ring & (my_rank < jnp.where(my_way == 1, NEAR, far_slots))

    total = add(None, by_ring, near, near_part, slot)
    total = add(total, by_send, arrived, sent_part, sent_at)

    def overflow(b_line, c_column):
        need = needs(a_wide, b_line, c_column)

        def most(which):
            return jnp.max(jnp.sum(need & (way == which), axis=1, dtype=jnp.int32))

        return (most(1) > NEAR) | (most(2) > far_slots) | (most(3) > far_slots)

    trips = jnp.any(jax.vmap(overflow, in_axes=(0, 1))(b_wide, c_where)).astype(jnp.int32)

    def trip(state):
        done, total = state
        whole = lax.all_gather(own, "row").reshape(rows * held, size, size)
        return done + 1, add(total, ~by_ring & ~by_send, [whole], 0 * line, line)

    _, total = lax.while_loop(lambda state: state[0] < trips, trip, (jnp.int32(0), total))
    return total[None, None]


def solution(mesh):
    rows, columns = mesh.devices.shape
    mesh = Mesh(mesh.devices.reshape(rows, 2, columns // 4, 2), ("row", *COL))
    in_specs = (
        P("row", COL, None, None, None),
        P("row", COL, None),
        P("row", COL, None, None, None, None),
        P("row", COL, None, None),
        P("row", COL, None),
    )
    out_specs = P("row", COL, None, None, None)
    return jax.shard_map(
        per_device, mesh=mesh, in_specs=in_specs, out_specs=out_specs, check_vma=False
    )
```

```python
import functools

import jax
import jax.numpy as jnp
import numpy as np
from jax import lax
from jax.experimental import pallas as pl
from jax.experimental.pallas import tpu as pltpu
from jax.sharding import Mesh
from jax.sharding import PartitionSpec as P

SA = 4
PK = 8
NBD = 8
NEAR = 6
AHEAD_FAR, BEHIND_FAR = 2, 1
COL = ("x_lo", "z", "core")
LIST = 512
AHEAD = 8


def lane_maps(columns, lines_per, rows):
    lane = np.arange(rows * columns)
    r, p = lane // columns, lane % columns
    owner = p // lines_per
    across = owner % 2 != r % 2
    far = (owner // 2 - r // 2) % (rows // 2) == 2
    way = across * 1 + far * 2
    first = (lane % columns == 0)[:, None]
    holder = [
        first & (r[:, None] == owner[None, :]) & (p[None, :] % lines_per == h)
        for h in range(lines_per)
    ]
    consumer = first & (r[:, None] == r[None, :])
    alike = (r[:, None] == r[None, :]) & (way[:, None] == way[None, :])
    earlier = alike & (lane[:, None] < lane[None, :])
    return np.stack([*holder, consumer, alike, earlier]).astype(jnp.bfloat16)


def lane_order(rows, columns):
    lane = np.arange(rows * columns)
    y, xh, xl, z, core = lane >> 5, (lane >> 4) & 1, (lane >> 3) & 1, (lane >> 1) & 3, lane & 1
    place = (((core * 4 + z) * 2 + xh) * 2 + xl) * 4 + y
    return (lane[:, None] == place[None, :]).astype(jnp.bfloat16)


def matmul(a, b):
    return jnp.dot(a.astype(jnp.bfloat16), b, preferred_element_type=jnp.float32)


def lands_at(a_line, b):
    meet = (a_line >= 0) & (b >= 0) & ((a_line & (PK - 1)) == (b >> 3))
    return jnp.where(meet, (a_line >> 3) * NBD + (b & (NBD - 1)), -2)


def needed(a, b, c):
    need = jnp.zeros(b.shape, jnp.bool_)
    for s in range(SA):
        lands = lands_at(a[s : s + 1], b)
        for n in range(c.shape[0]):
            need = need | (lands == c[n : n + 1])
    return need


def lane_facts(shape):
    lane = lax.broadcasted_iota(jnp.int32, shape, 1)
    r, p = lane >> 4, lane & 15
    owner = p >> 1
    far = (((owner >> 1) - (r >> 1)) & 3) == 2
    way = ((owner ^ r) & 1) + jnp.where(far, 2, 0)
    return r, p, owner, way


def code(a_slot, part, at, c_slot):
    return ((a_slot * 16 + part) * 128 + at) * 16 + c_slot


def a_of(word):
    return word >> 15


def part_of(word):
    return (word >> 11) & 15


def at_of(word):
    return (word >> 4) & 127


def c_of(word):
    return word & 15


def fetch_block(part, at, refs, dst, sem):
    for i, ref in enumerate(refs):

        def start(ref=ref):
            pltpu.make_async_copy(ref.at[at], dst, sem).start()

        if len(refs) == 1:
            start()
        else:
            pl.when(part == i)(start)


def positions(spots_ref, order_ref):
    spots = spots_ref[...].astype(jnp.float32).astype(jnp.bfloat16)
    return lax.dot_general(
        spots, order_ref[...], (((0,), (0,)), ((), ())), preferred_element_type=jnp.float32
    )


def pack_kernel(sends, me_ref, spots_ref, order_ref, maps_ref, *rest):
    near, packed, info_ref, sems = rest[:3], rest[3 : 3 + len(sends)], rest[-2], rest[-1]
    row, column = me_ref[0], me_ref[1]
    held = positions(spots_ref, order_ref)
    a = held[:8].astype(jnp.int32)
    turned = pltpu.roll(held[8:40], (128 - column) & 127, 1)
    b = matmul(turned[:8], maps_ref[0]) + matmul(turned[8:16], maps_ref[1])
    b = b.astype(jnp.int32)
    c = matmul(turned[16:32], maps_ref[2]).astype(jnp.int32)
    need = needed(a, b, c)

    r, p, owner, way = lane_facts(b.shape)
    t = lax.broadcasted_iota(jnp.int32, b.shape, 0)
    flags = jnp.where(need, 1.0, 0.0)
    alike = matmul(flags, maps_ref[3])
    upto = alike
    for step in (1, 2, 4):
        upto = upto + jnp.where(t >= step, pltpu.roll(upto, step, 0), 0.0)
    rank = (upto - alike + matmul(flags, maps_ref[4])).astype(jnp.int32)
    order = jnp.where(need, way * 128 + rank, -1)

    steps = ((owner >> 1) - (row >> 1)) & 3
    part = jnp.where(steps == 0, 0, jnp.where(steps == 3, 1, 2))
    word = (part * 16 + (p & 1) * 8 + t).astype(jnp.float32)
    words = []
    for slots, which, first, there in sends:
        for e in range(slots):
            hit = (order == which * 128 + first + e) & (r == there(row))
            words.append(jnp.max(jnp.where(hit, word, -1.0)).astype(jnp.int32))
    places = [(i, e) for i, send in enumerate(sends) for e in range(send[0])]
    for n, (i, e) in enumerate(places):

        @pl.when(words[n] >= 0)
        def _():
            fetch_block(words[n] >> 4, words[n] & 15, near, packed[i].at[e], sems.at[n])

    info_ref[0:8] = a
    info_ref[8:16] = b
    info_ref[16:32] = c
    info_ref[32:40] = order
    for n, (i, e) in enumerate(places):

        @pl.when(words[n] >= 0)
        def _():
            pltpu.make_async_copy(near[0].at[0], packed[i].at[e], sems.at[n]).wait()


def pack(me, spots, order, maps, near, sends):
    size = near[0].shape[-1]
    vmem = pl.BlockSpec(memory_space=pltpu.VMEM)
    return pl.pallas_call(
        functools.partial(pack_kernel, sends),
        in_specs=[pl.BlockSpec(memory_space=pltpu.SMEM), vmem, vmem, vmem]
        + [pl.BlockSpec(memory_space=pl.ANY)] * 3,
        out_specs=[vmem] * (len(sends) + 1),
        scratch_shapes=[pltpu.SemaphoreType.DMA((sum(n for n, *_ in sends),))],
        out_shape=[jax.ShapeDtypeStruct((n, size, size), jnp.float32) for n, *_ in sends]
        + [jax.ShapeDtypeStruct((40, 128), jnp.int32)],
        compiler_params=pltpu.CompilerParams(vmem_limit_bytes=16 << 20),
        name="pack",
    )(me, spots, order, maps, *near)


def overflow_kernel(spots_ref, order_ref, maps_ref, over_ref):
    held = positions(spots_ref, order_ref)
    a = held[:8].astype(jnp.int32)
    turned = [held[8:40]] + [pltpu.roll(held[8:40], 128 - q, 1) for q in range(1, 16)]
    b = matmul(jnp.concatenate([x[:8] for x in turned]), maps_ref[0])
    b = b + matmul(jnp.concatenate([x[8:16] for x in turned]), maps_ref[1])
    b = b.astype(jnp.int32)
    c = matmul(jnp.concatenate([x[16:32] for x in turned]), maps_ref[2]).astype(jnp.int32)
    flags = [
        jnp.where(needed(a, b[q * 8 : q * 8 + 8], c[q * 16 : q * 16 + 16]), 1.0, 0.0)
        for q in range(16)
    ]
    alike = matmul(jnp.concatenate(flags), maps_ref[3])
    most = jnp.sum(alike[:8], axis=0, keepdims=True)
    for q in range(1, 16):
        most = jnp.maximum(most, jnp.sum(alike[q * 8 : q * 8 + 8], axis=0, keepdims=True))
    *_, way = lane_facts(most.shape)
    slots = jnp.where(way == 0, 128, jnp.where(way == 1, NEAR, AHEAD_FAR + BEHIND_FAR))
    over_ref[0] = jnp.max(jnp.where(most > slots.astype(jnp.float32), 1.0, 0.0)).astype(jnp.int32)


def overflow(spots, order, maps):
    vmem = pl.BlockSpec(memory_space=pltpu.VMEM)
    return pl.pallas_call(
        overflow_kernel,
        in_specs=[vmem] * 3,
        out_specs=pl.BlockSpec(memory_space=pltpu.SMEM),
        out_shape=jax.ShapeDtypeStruct((1,), jnp.int32),
        compiler_params=pltpu.CompilerParams(vmem_limit_bytes=16 << 20),
        cost_estimate=pl.CostEstimate(flops=10**9, bytes_accessed=10**5, transcendentals=0),
        name="overflow",
    )(spots, order, maps)


def halves(x):
    high = x.astype(jnp.bfloat16)
    return high, (x - high.astype(jnp.float32)).astype(jnp.bfloat16)


def block_product(a, b):
    a_high, a_low = halves(a)
    b_high, b_low = halves(b)
    dot = functools.partial(jnp.dot, preferred_element_type=jnp.float32)
    return dot(a_high, b_high) + (dot(a_high, b_low) + dot(a_low, b_high))


def extract(entries, list_ref):
    def more(state):
        n, word, left = state
        list_ref[n] = word.astype(jnp.int32)
        left = jnp.where(left == word, -1.0, left)
        return n + 1, jnp.max(left), left

    n, *_ = lax.while_loop(
        lambda state: state[1] >= 0, more, (jnp.int32(0), jnp.max(entries), entries)
    )
    list_ref[LIST] = n


def entries_of(info_ref, row):
    b, c, order = info_ref[8:16], info_ref[16:32], info_ref[32:40]
    r, p, owner, way = lane_facts(b.shape)
    t = lax.broadcasted_iota(jnp.int32, b.shape, 0)
    rank = order & 127
    steps = ((owner >> 1) - (row >> 1)) & 3
    part = jnp.where(steps == 0, 0, jnp.where(steps == 3, 1, 2))
    back = (way >= 2) & (rank >= AHEAD_FAR)
    sent_part = jnp.where(way >= 2, way * 2 - 3, 0) + jnp.where(back, 1, 0)
    sent_at = rank - jnp.where(back, AHEAD_FAR, 0)
    sent = (way > 0) & (rank < jnp.where(way == 1, NEAR, AHEAD_FAR + BEHIND_FAR))
    found = [[], [], []]
    for s in range(SA):
        lands = lands_at(info_ref[s : s + 1], b)
        c_slot = jnp.full(b.shape, -1, jnp.int32)
        for n in range(c.shape[0]):
            c_slot = jnp.where(lands == c[n : n + 1], n, c_slot)
        live = (c_slot >= 0) & (r == row)
        a_slot = p * SA + s
        for found_in, mine, code_of in (
            (found[0], way == 0, code(a_slot, part, (p & 1) * 8 + t, c_slot)),
            (found[1], sent, code(a_slot, sent_part, sent_at, c_slot)),
            (found[2], (way > 0) & ~sent, code(a_slot, 0, p * 8 + t, c_slot)),
        ):
            found_in.append(jnp.where(live & mine, code_of, -1).astype(jnp.float32))
    return [jnp.concatenate(x) for x in found]


def multiply_listed(list_ref, a_ref, b_refs, out_ref, a_buf, b_buf, a_sem, b_sem, meanwhile):
    count = list_ref[LIST]

    def fetch(n):
        slot = n % AHEAD
        word = list_ref[n]
        pltpu.make_async_copy(a_ref.at[a_of(word)], a_buf.at[slot], a_sem.at[slot]).start()
        fetch_block(part_of(word), at_of(word), b_refs, b_buf.at[slot], b_sem.at[slot])

    for n in range(AHEAD):

        @pl.when(n < count)
        def _():
            fetch(n)

    meanwhile()

    def step(n, carry):
        slot = n % AHEAD
        pltpu.make_async_copy(a_ref.at[0], a_buf.at[slot], a_sem.at[slot]).wait()
        pltpu.make_async_copy(b_refs[0].at[0], b_buf.at[slot], b_sem.at[slot]).wait()
        out_ref[c_of(list_ref[n])] += block_product(a_buf[slot], b_buf[slot])

        @pl.when(n + AHEAD < count)
        def _():
            fetch(n + AHEAD)

        return carry

    lax.fori_loop(0, count, step, 0)


def own_kernel(me_ref, info_ref, a_ref, *rest):
    b_refs, (out_ref, sent_list, own_list, *buffers) = rest[:3], rest[3:]
    here, sent, _ = entries_of(info_ref, me_ref[0])
    extract(here, own_list)

    def meanwhile():
        extract(sent, sent_list)
        out_ref[...] = jnp.zeros_like(out_ref)

    multiply_listed(own_list, a_ref, b_refs, out_ref, *buffers, meanwhile)


def sent_kernel(list_ref, a_ref, *rest):
    b_refs, (total_ref, out_ref, *buffers) = rest[:-6], rest[-6:]

    def meanwhile():
        out_ref[...] = total_ref[...]

    multiply_listed(list_ref, a_ref, b_refs, out_ref, *buffers, meanwhile)


def rest_kernel(me_ref, info_ref, a_ref, b_ref, total_ref, out_ref, rest_list, *buffers):
    extract(entries_of(info_ref, me_ref[0])[2], rest_list)

    def meanwhile():
        out_ref[...] = total_ref[...]

    multiply_listed(rest_list, a_ref, [b_ref], out_ref, *buffers, meanwhile)


def products(kernel, leading, a_all, b_parts, total, slots, lists_out=False, lists=True):
    size = a_all.shape[-1]
    smem = pl.BlockSpec(memory_space=pltpu.SMEM)
    vmem = pl.BlockSpec(memory_space=pltpu.VMEM)
    operands = [*leading, a_all, *b_parts] + ([] if total is None else [total])
    out = jax.ShapeDtypeStruct((slots, size, size), jnp.float32)
    listing = (LIST + 1,)
    return pl.pallas_call(
        kernel,
        in_specs=[smem if x.ndim == 1 else vmem for x in leading]
        + [pl.BlockSpec(memory_space=pl.ANY)] * (1 + len(b_parts))
        + ([] if total is None else [vmem]),
        out_specs=[vmem, smem] if lists_out else vmem,
        out_shape=[out, jax.ShapeDtypeStruct(listing, jnp.int32)] if lists_out else out,
        scratch_shapes=([pltpu.SMEM(listing, jnp.int32)] if lists else [])
        + [
            pltpu.VMEM((AHEAD, size, size), jnp.float32),
            pltpu.VMEM((AHEAD, size, size), jnp.float32),
            pltpu.SemaphoreType.DMA((AHEAD,)),
            pltpu.SemaphoreType.DMA((AHEAD,)),
        ],
        input_output_aliases={} if total is None else {len(operands) - 1: 0},
        compiler_params=pltpu.CompilerParams(vmem_limit_bytes=16 << 20),
        cost_estimate=pl.CostEstimate(
            flops=8 * 3 * 2 * size**3, bytes_accessed=24 * size * size * 4, transcendentals=0
        ),
        name="products",
    )(*operands)


def to_row(block, rows, there):
    return lax.ppermute(block, "row", [(i, there(i)) for i in range(rows)])


def everywhere(mine, rows, columns):
    axes = ("row", *COL)
    me = lax.axis_index("row") * columns + lax.axis_index(COL)
    held = mine
    for bits in ((5, 6), (3, 4), (1, 2), (0,)):
        group = jnp.zeros((2 ** len(bits),) + held.shape, held.dtype)
        for move in range(2 ** len(bits)):
            flip = sum(((move >> n) & 1) << bit for n, bit in enumerate(bits))
            got = held
            if move:
                got = lax.ppermute(held, axes, [(i ^ flip, i) for i in range(rows * columns)])
            spot = sum((((me ^ flip) >> bit) & 1) << n for n, bit in enumerate(bits))
            group = lax.dynamic_update_index_in_dim(group, got, spot, 0)
        held = group
    return held.reshape(rows * columns, mine.shape[0])


def per_device(a_blocks, a_index, b_blocks, b_index, c_index):
    rows = lax.axis_size("row")
    columns = lax.axis_size(COL)
    row = lax.axis_index("row")
    me = jnp.stack([row, lax.axis_index(COL)])
    hold = columns // rows
    sa, sb, sc = a_blocks.shape[2], b_blocks.shape[3], c_index.shape[2]
    held = hold * sb
    size = a_blocks.shape[-1]

    a_all = lax.all_gather(a_blocks[0, 0], COL).reshape(columns * sa, size, size)

    own = b_blocks[0, 0].reshape(held, size, size)
    behind = to_row(own, rows, lambda i: (i + 2) % rows)
    ahead = to_row(own, rows, lambda i: (i - 2) % rows)
    near = [own, behind, ahead]

    blank = jnp.full((8 - sa,), -1, jnp.int32)
    mine = jnp.concatenate([a_index[0, 0], blank, b_index[0, 0].reshape(-1), c_index[0, 0]])
    spots = everywhere(jnp.pad(mine, (0, 128 - mine.shape[0])), rows, columns)

    order = jnp.asarray(lane_order(rows, columns))
    maps = jnp.asarray(lane_maps(columns, hold, rows))

    sends = [
        (NEAR, 1, 0, lambda i: i ^ 1),
        (AHEAD_FAR, 2, 0, lambda i: (i + 2) & 7),
        (BEHIND_FAR, 2, AHEAD_FAR, lambda i: (i - 2) & 7),
        (AHEAD_FAR, 3, 0, lambda i: ((i + 2) & 7) ^ 1),
        (BEHIND_FAR, 3, AHEAD_FAR, lambda i: ((i - 2) & 7) ^ 1),
    ]
    *packed, info = pack(me, spots, order, maps, near, sends)
    arrived = [to_row(block, rows, there) for block, (*_, there) in zip(packed, sends)]

    total, sent_list = products(own_kernel, [me, info], a_all, near, None, sc, lists_out=True)
    total = products(sent_kernel, [sent_list], a_all, arrived, total, sc, lists=False)

    trips = overflow(spots, order, maps)[0]

    def trip(state):
        done, total = state
        whole = lax.all_gather(own, "row").reshape(rows * held, size, size)
        return done + 1, products(rest_kernel, [me, info], a_all, [whole], total, sc)

    _, total = lax.while_loop(lambda state: state[0] < trips, trip, (jnp.int32(0), total))
    return total[None, None]


def solution(mesh):
    rows, columns = mesh.devices.shape
    mesh = Mesh(mesh.devices.reshape(rows, 2, columns // 4, 2), ("row", *COL))
    in_specs = (
        P("row", COL, None, None, None),
        P("row", COL, None),
        P("row", COL, None, None, None, None),
        P("row", COL, None, None),
        P("row", COL, None),
    )
    out_specs = P("row", COL, None, None, None)
    return jax.shard_map(
        per_device, mesh=mesh, in_specs=in_specs, out_specs=out_specs, check_vma=False
    )
```

```python
import functools

import jax
import jax.numpy as jnp
from jax import lax
from jax.experimental import pallas as pl
from jax.experimental.pallas import tpu as pltpu
from jax.sharding import Mesh
from jax.sharding import PartitionSpec as P

SA = 4
PK = 8
NBD = 8
NEAR = 6
FAR = 3
COL = ("x_lo", "z", "core")
LIST = 512
AHEAD = 8


def matmul(a, b):
    return jnp.dot(a.astype(jnp.bfloat16), b, preferred_element_type=jnp.float32)


def lands_at(a_line, b):
    meet = (a_line >= 0) & (b >= 0) & ((a_line & (PK - 1)) == (b >> 3))
    return jnp.where(meet, (a_line >> 3) * NBD + (b & (NBD - 1)), -2)


def needed(a, b, c):
    need = jnp.zeros(b.shape, jnp.bool_)
    for s in range(SA):
        lands = lands_at(a[s : s + 1], b)
        for n in range(c.shape[0]):
            need = need | (lands == c[n : n + 1])
    return need


def lane_facts(shape, axis=1):
    lane = lax.broadcasted_iota(jnp.int32, shape, axis)
    r, p = lane >> 4, lane & 15
    owner = p >> 1
    far = (((owner >> 1) - (r >> 1)) & 3) == 2
    way = ((owner ^ r) & 1) + jnp.where(far, 2, 0)
    return r, p, owner, way


def code(a_slot, part, at, c_slot):
    return ((a_slot * 16 + part) * 128 + at) * 16 + c_slot


def a_of(word):
    return word >> 15


def part_of(word):
    return (word >> 11) & 15


def at_of(word):
    return (word >> 4) & 127


def c_of(word):
    return word & 15


def fetch_block(part, at, refs, dst, sem):
    for i, ref in enumerate(refs):

        def start(ref=ref):
            pltpu.make_async_copy(ref.at[at], dst, sem).start()

        if len(refs) == 1:
            start()
        else:
            pl.when(part == i)(start)


def make_maps(maps_ref):
    shape = maps_ref.shape[1:]
    lane = lax.broadcasted_iota(jnp.int32, shape, 1)
    down = lax.broadcasted_iota(jnp.int32, shape, 0)
    r, p, owner, way = lane_facts(shape)
    r_down, p_down, _, way_down = lane_facts(shape, 0)
    holder = (p_down == 0) & (r_down == owner)
    alike = (r == r_down) & (way == way_down)
    y, xh, xl, z, core = lane >> 5, (lane >> 4) & 1, (lane >> 3) & 1, (lane >> 1) & 3, lane & 1
    listed_at = (((core * 4 + z) * 2 + xh) * 2 + xl) * 4 + y
    for n, flags in enumerate(
        [
            holder & ((p & 1) == 0),
            holder & ((p & 1) == 1),
            (p_down == 0) & (r == r_down),
            alike,
            alike & (down < lane),
            down == listed_at,
        ]
    ):
        maps_ref[n] = jnp.where(flags, 1.0, 0.0).astype(jnp.bfloat16)


def positions(spots_ref, maps_ref):
    spots = spots_ref[...].astype(jnp.float32).astype(jnp.bfloat16)
    return lax.dot_general(
        spots, maps_ref[5], (((0,), (0,)), ((), ())), preferred_element_type=jnp.float32
    )


def plan_kernel(sends, me_ref, spots_ref, pack_list, own_list, sent_list, info_ref, maps_ref):
    row, column = me_ref[0], me_ref[1]
    make_maps(maps_ref)
    held = positions(spots_ref, maps_ref)
    a = held[:8].astype(jnp.int32)
    turned = pltpu.roll(held[8:40], (128 - column) & 127, 1)
    b = matmul(turned[:8], maps_ref[0]) + matmul(turned[8:16], maps_ref[1])
    b = b.astype(jnp.int32)
    c = matmul(turned[16:32], maps_ref[2]).astype(jnp.int32)
    need = needed(a, b, c)

    r, p, owner, way = lane_facts(b.shape)
    t = lax.broadcasted_iota(jnp.int32, b.shape, 0)
    flags = jnp.where(need, 1.0, 0.0)
    alike = matmul(flags, maps_ref[3])
    upto = alike
    for step in (1, 2, 4):
        upto = upto + jnp.where(t >= step, pltpu.roll(upto, step, 0), 0.0)
    rank = (upto - alike + matmul(flags, maps_ref[4])).astype(jnp.int32)
    order = jnp.where(need, way * 128 + rank, -1)

    steps = ((owner >> 1) - (row >> 1)) & 3
    part = jnp.where(steps == 0, 0, jnp.where(steps == 3, 1, 2))
    word = (part * 16 + (p & 1) * 8 + t).astype(jnp.float32)
    n = 0
    for slots, which, there in sends:
        for e in range(slots):
            hit = (order == which * 128 + e) & (r == there(row))
            pack_list[n] = jnp.max(jnp.where(hit, word, -1.0)).astype(jnp.int32)
            n += 1

    info_ref[0:8] = a
    info_ref[8:16] = b
    info_ref[16:32] = c
    info_ref[32:40] = order
    here, sent, _ = entries_of(info_ref, row)
    extract(here, own_list)
    extract(sent, sent_list)


def plan(me, spots, sends):
    smem = pl.BlockSpec(memory_space=pltpu.SMEM)
    vmem = pl.BlockSpec(memory_space=pltpu.VMEM)
    return pl.pallas_call(
        functools.partial(plan_kernel, sends),
        in_specs=[smem, vmem],
        out_specs=[smem, smem, smem, vmem, vmem],
        out_shape=[
            jax.ShapeDtypeStruct((sum(n for n, *_ in sends),), jnp.int32),
            jax.ShapeDtypeStruct((LIST + 1,), jnp.int32),
            jax.ShapeDtypeStruct((LIST + 1,), jnp.int32),
            jax.ShapeDtypeStruct((40, 128), jnp.int32),
            jax.ShapeDtypeStruct((6, 128, 128), jnp.bfloat16),
        ],
        compiler_params=pltpu.CompilerParams(vmem_limit_bytes=16 << 20),
        name="plan",
    )(me, spots)


def pack_kernel(sizes, list_ref, *rest):
    near, packed, sems = rest[:3], rest[3:-1], rest[-1]
    places = [(i, e) for i, size in enumerate(sizes) for e in range(size)]
    for n, (i, e) in enumerate(places):
        word = list_ref[n]

        @pl.when(word >= 0)
        def _():
            fetch_block(word >> 4, word & 15, near, packed[i].at[e], sems.at[n])

    for n, (i, e) in enumerate(places):

        @pl.when(list_ref[n] >= 0)
        def _():
            pltpu.make_async_copy(near[0].at[0], packed[i].at[e], sems.at[n]).wait()


def pack(listing, near, sizes):
    size = near[0].shape[-1]
    return pl.pallas_call(
        functools.partial(pack_kernel, sizes),
        in_specs=[pl.BlockSpec(memory_space=pltpu.SMEM)]
        + [pl.BlockSpec(memory_space=pl.ANY)] * 3,
        out_specs=[pl.BlockSpec(memory_space=pltpu.VMEM)] * len(sizes),
        scratch_shapes=[pltpu.SemaphoreType.DMA((sum(sizes),))],
        out_shape=[jax.ShapeDtypeStruct((n, size, size), jnp.float32) for n in sizes],
        compiler_params=pltpu.CompilerParams(vmem_limit_bytes=16 << 20),
        name="pack",
    )(listing, *near)


def overflow_kernel(spots_ref, maps_ref, over_ref):
    held = positions(spots_ref, maps_ref)
    a = held[:8].astype(jnp.int32)
    turned = [held[8:40]] + [pltpu.roll(held[8:40], 128 - q, 1) for q in range(1, 16)]
    b = matmul(jnp.concatenate([x[:8] for x in turned]), maps_ref[0])
    b = b + matmul(jnp.concatenate([x[8:16] for x in turned]), maps_ref[1])
    b = b.astype(jnp.int32)
    c = matmul(jnp.concatenate([x[16:32] for x in turned]), maps_ref[2]).astype(jnp.int32)
    flags = [
        jnp.where(needed(a, b[q * 8 : q * 8 + 8], c[q * 16 : q * 16 + 16]), 1.0, 0.0)
        for q in range(16)
    ]
    alike = matmul(jnp.concatenate(flags), maps_ref[3])
    most = jnp.sum(alike[:8], axis=0, keepdims=True)
    for q in range(1, 16):
        most = jnp.maximum(most, jnp.sum(alike[q * 8 : q * 8 + 8], axis=0, keepdims=True))
    *_, way = lane_facts(most.shape)
    slots = jnp.where(way == 0, 128, jnp.where(way == 1, NEAR, FAR))
    over_ref[0] = jnp.max(jnp.where(most > slots.astype(jnp.float32), 1.0, 0.0)).astype(jnp.int32)


def overflow(spots, maps):
    vmem = pl.BlockSpec(memory_space=pltpu.VMEM)
    return pl.pallas_call(
        overflow_kernel,
        in_specs=[vmem] * 2,
        out_specs=pl.BlockSpec(memory_space=pltpu.SMEM),
        out_shape=jax.ShapeDtypeStruct((1,), jnp.int32),
        compiler_params=pltpu.CompilerParams(vmem_limit_bytes=16 << 20),
        cost_estimate=pl.CostEstimate(flops=10**9, bytes_accessed=10**5, transcendentals=0),
        name="overflow",
    )(spots, maps)


def halves(x):
    high = x.astype(jnp.bfloat16)
    return high, (x - high.astype(jnp.float32)).astype(jnp.bfloat16)


def block_product(a, b):
    a_high, a_low = halves(a)
    b_high, b_low = halves(b)
    dot = functools.partial(jnp.dot, preferred_element_type=jnp.float32)
    return dot(a_high, b_high) + (dot(a_high, b_low) + dot(a_low, b_high))


def extract(entries, list_ref):
    def more(state):
        n, word, left = state
        list_ref[n] = word.astype(jnp.int32)
        left = jnp.where(left == word, -1.0, left)
        return n + 1, jnp.max(left), left

    n, *_ = lax.while_loop(
        lambda state: state[1] >= 0, more, (jnp.int32(0), jnp.max(entries), entries)
    )
    list_ref[LIST] = n


def entries_of(info_ref, row):
    b, c, order = info_ref[8:16], info_ref[16:32], info_ref[32:40]
    r, p, owner, way = lane_facts(b.shape)
    t = lax.broadcasted_iota(jnp.int32, b.shape, 0)
    rank = order & 127
    steps = ((owner >> 1) - (row >> 1)) & 3
    part = jnp.where(steps == 0, 0, jnp.where(steps == 3, 1, 2))
    sent = (way > 0) & (rank < jnp.where(way == 1, NEAR, FAR))
    found = [[], [], []]
    for s in range(SA):
        lands = lands_at(info_ref[s : s + 1], b)
        c_slot = jnp.full(b.shape, -1, jnp.int32)
        for n in range(c.shape[0]):
            c_slot = jnp.where(lands == c[n : n + 1], n, c_slot)
        live = (c_slot >= 0) & (r == row)
        a_slot = p * SA + s
        for found_in, mine, code_of in (
            (found[0], way == 0, code(a_slot, part, (p & 1) * 8 + t, c_slot)),
            (found[1], sent, code(a_slot, (way - 1) & 3, rank, c_slot)),
            (found[2], (way > 0) & ~sent, code(a_slot, 0, p * 8 + t, c_slot)),
        ):
            found_in.append(jnp.where(live & mine, code_of, -1).astype(jnp.float32))
    return [jnp.concatenate(x) for x in found]


def multiply_listed(list_ref, a_ref, b_refs, out_ref, a_buf, b_buf, a_sem, b_sem, meanwhile):
    count = list_ref[LIST]

    def fetch(n):
        slot = n % AHEAD
        word = list_ref[n]
        pltpu.make_async_copy(a_ref.at[a_of(word)], a_buf.at[slot], a_sem.at[slot]).start()
        fetch_block(part_of(word), at_of(word), b_refs, b_buf.at[slot], b_sem.at[slot])

    for n in range(AHEAD):

        @pl.when(n < count)
        def _():
            fetch(n)

    meanwhile()

    def step(n, carry):
        slot = n % AHEAD
        pltpu.make_async_copy(a_ref.at[0], a_buf.at[slot], a_sem.at[slot]).wait()
        pltpu.make_async_copy(b_refs[0].at[0], b_buf.at[slot], b_sem.at[slot]).wait()
        out_ref[c_of(list_ref[n])] += block_product(a_buf[slot], b_buf[slot])

        @pl.when(n + AHEAD < count)
        def _():
            fetch(n + AHEAD)

        return carry

    lax.fori_loop(0, count, step, 0)


def own_kernel(list_ref, a_ref, *rest):
    b_refs, (out_ref, *buffers) = rest[:3], rest[3:]

    def meanwhile():
        out_ref[...] = jnp.zeros_like(out_ref)

    multiply_listed(list_ref, a_ref, b_refs, out_ref, *buffers, meanwhile)


def sent_kernel(list_ref, a_ref, *rest):
    b_refs, (total_ref, out_ref, *buffers) = rest[:-6], rest[-6:]

    def meanwhile():
        out_ref[...] = total_ref[...]

    multiply_listed(list_ref, a_ref, b_refs, out_ref, *buffers, meanwhile)


def rest_kernel(me_ref, info_ref, a_ref, b_ref, total_ref, out_ref, rest_list, *buffers):
    extract(entries_of(info_ref, me_ref[0])[2], rest_list)

    def meanwhile():
        out_ref[...] = total_ref[...]

    multiply_listed(rest_list, a_ref, [b_ref], out_ref, *buffers, meanwhile)


def products(kernel, leading, a_all, b_parts, total, slots, own_list=False):
    size = a_all.shape[-1]
    smem = pl.BlockSpec(memory_space=pltpu.SMEM)
    vmem = pl.BlockSpec(memory_space=pltpu.VMEM)
    operands = [*leading, a_all, *b_parts] + ([] if total is None else [total])
    return pl.pallas_call(
        kernel,
        in_specs=[smem if x.ndim == 1 else vmem for x in leading]
        + [pl.BlockSpec(memory_space=pl.ANY)] * (1 + len(b_parts))
        + ([] if total is None else [vmem]),
        out_specs=vmem,
        out_shape=jax.ShapeDtypeStruct((slots, size, size), jnp.float32),
        scratch_shapes=([pltpu.SMEM((LIST + 1,), jnp.int32)] if own_list else [])
        + [
            pltpu.VMEM((AHEAD, size, size), jnp.float32),
            pltpu.VMEM((AHEAD, size, size), jnp.float32),
            pltpu.SemaphoreType.DMA((AHEAD,)),
            pltpu.SemaphoreType.DMA((AHEAD,)),
        ],
        input_output_aliases={} if total is None else {len(operands) - 1: 0},
        compiler_params=pltpu.CompilerParams(vmem_limit_bytes=16 << 20),
        cost_estimate=pl.CostEstimate(
            flops=8 * 3 * 2 * size**3, bytes_accessed=24 * size * size * 4, transcendentals=0
        ),
        name="products",
    )(*operands)


def to_row(block, rows, there):
    return lax.ppermute(block, "row", [(i, there(i)) for i in range(rows)])


def everywhere(mine, rows, columns):
    axes = ("row", *COL)
    me = lax.axis_index("row") * columns + lax.axis_index(COL)
    held = mine
    for bits in ((5, 6), (3, 4), (1, 2), (0,)):
        group = jnp.zeros((2 ** len(bits),) + held.shape, held.dtype)
        for move in range(2 ** len(bits)):
            flip = sum(((move >> n) & 1) << bit for n, bit in enumerate(bits))
            got = held
            if move:
                got = lax.ppermute(held, axes, [(i ^ flip, i) for i in range(rows * columns)])
            spot = sum((((me ^ flip) >> bit) & 1) << n for n, bit in enumerate(bits))
            group = lax.dynamic_update_index_in_dim(group, got, spot, 0)
        held = group
    return held.reshape(rows * columns, mine.shape[0])


def per_device(a_blocks, a_index, b_blocks, b_index, c_index):
    rows = lax.axis_size("row")
    columns = lax.axis_size(COL)
    row = lax.axis_index("row")
    me = jnp.stack([row, lax.axis_index(COL)])
    hold = columns // rows
    sa, sb, sc = a_blocks.shape[2], b_blocks.shape[3], c_index.shape[2]
    held = hold * sb
    size = a_blocks.shape[-1]

    a_all = lax.all_gather(a_blocks[0, 0], COL).reshape(columns * sa, size, size)

    own = b_blocks[0, 0].reshape(held, size, size)
    behind = to_row(own, rows, lambda i: (i + 2) % rows)
    ahead = to_row(own, rows, lambda i: (i - 2) % rows)
    near = [own, behind, ahead]

    blank = jnp.full((8 - sa,), -1, jnp.int32)
    mine = jnp.concatenate([a_index[0, 0], blank, b_index[0, 0].reshape(-1), c_index[0, 0]])
    spots = everywhere(jnp.pad(mine, (0, 128 - mine.shape[0])), rows, columns)

    sends = [
        (FAR, 2, lambda i: (i + 2) & 7),
        (FAR, 3, lambda i: ((i + 2) & 7) ^ 1),
        (NEAR, 1, lambda i: i ^ 1),
    ]
    pack_list, own_list, sent_list, info, maps = plan(me, spots, sends)
    packed = pack(pack_list, near, [n for n, *_ in sends])
    far_own, far_other, cross = [
        to_row(block, rows, there) for block, (*_, there) in zip(packed, sends)
    ]

    total = products(own_kernel, [own_list], a_all, near, None, sc)
    total = products(sent_kernel, [sent_list], a_all, [cross, far_own, far_other], total, sc)

    trips = overflow(spots, maps)[0]

    def trip(state):
        done, total = state
        whole = lax.all_gather(own, "row").reshape(rows * held, size, size)
        rest = products(rest_kernel, [me, info], a_all, [whole], total, sc, own_list=True)
        return done + 1, rest

    _, total = lax.while_loop(lambda state: state[0] < trips, trip, (jnp.int32(0), total))
    return total[None, None]


def solution(mesh):
    rows, columns = mesh.devices.shape
    mesh = Mesh(mesh.devices.reshape(rows, 2, columns // 4, 2), ("row", *COL))
    in_specs = (
        P("row", COL, None, None, None),
        P("row", COL, None),
        P("row", COL, None, None, None, None),
        P("row", COL, None, None),
        P("row", COL, None),
    )
    out_specs = P("row", COL, None, None, None)
    return jax.shard_map(
        per_device, mesh=mesh, in_specs=in_specs, out_specs=out_specs, check_vma=False
    )
```

```python
import functools

import jax
import jax.numpy as jnp
from jax import lax
from jax.experimental import pallas as pl
from jax.experimental.pallas import tpu as pltpu
from jax.sharding import Mesh
from jax.sharding import PartitionSpec as P

SA = 4
PK = 8
NBD = 8
SLOTS = 5
COL = ("x_lo", "z", "core")
LIST = 512
AHEAD = 8


def matmul(a, b):
    return jnp.dot(a.astype(jnp.bfloat16), b, preferred_element_type=jnp.float32)


def lands_at(a_line, b):
    meet = (a_line >= 0) & (b >= 0) & ((a_line & (PK - 1)) == (b >> 3))
    return jnp.where(meet, (a_line >> 3) * NBD + (b & (NBD - 1)), -2)


def needed(a, b, c):
    need = jnp.zeros(b.shape, jnp.bool_)
    for s in range(SA):
        lands = lands_at(a[s : s + 1], b)
        for n in range(c.shape[0]):
            need = need | (lands == c[n : n + 1])
    return need


def lane_facts(shape, axis=1):
    lane = lax.broadcasted_iota(jnp.int32, shape, axis)
    r, p = lane >> 4, lane & 15
    owner = p >> 1
    way = ((owner >> 1) - (r >> 1)) & 3
    return r, p, owner, way


def code(a_slot, part, at, c_slot):
    return ((a_slot * 16 + part) * 128 + at) * 16 + c_slot


def a_of(word):
    return word >> 15


def part_of(word):
    return (word >> 11) & 15


def at_of(word):
    return (word >> 4) & 127


def c_of(word):
    return word & 15


def fetch_block(part, at, refs, dst, sem):
    for i, ref in enumerate(refs):

        def start(ref=ref):
            pltpu.make_async_copy(ref.at[at], dst, sem).start()

        if len(refs) == 1:
            start()
        else:
            pl.when(part == i)(start)


def make_maps(maps_ref):
    shape = maps_ref.shape[1:]
    lane = lax.broadcasted_iota(jnp.int32, shape, 1)
    down = lax.broadcasted_iota(jnp.int32, shape, 0)
    r, p, owner, way = lane_facts(shape)
    r_down, p_down, _, way_down = lane_facts(shape, 0)
    holder = (p_down == 0) & (r_down == owner)
    alike = (r == r_down) & (way == way_down)
    y, xh, xl, z, core = lane >> 5, (lane >> 4) & 1, (lane >> 3) & 1, (lane >> 1) & 3, lane & 1
    listed_at = (((core * 4 + z) * 4 + y) * 2 + xh) * 2 + xl
    for n, flags in enumerate(
        [
            holder & ((p & 1) == 0),
            holder & ((p & 1) == 1),
            (p_down == 0) & (r == r_down),
            alike,
            alike & (down < lane),
            down == listed_at,
        ]
    ):
        maps_ref[n] = jnp.where(flags, 1.0, 0.0).astype(jnp.bfloat16)


def positions(spots_ref, maps_ref):
    spots = spots_ref[...].astype(jnp.float32).astype(jnp.bfloat16)
    return lax.dot_general(
        spots, maps_ref[5], (((0,), (0,)), ((), ())), preferred_element_type=jnp.float32
    )


def plan_kernel(sends, me_ref, spots_ref, pack_list, own_list, sent_list, info_ref, maps_ref):
    row, column = me_ref[0], me_ref[1]
    make_maps(maps_ref)
    held = positions(spots_ref, maps_ref)
    a = held[:8].astype(jnp.int32)
    turned = pltpu.roll(held[8:40], (128 - column) & 127, 1)
    b = matmul(turned[:8], maps_ref[0]) + matmul(turned[8:16], maps_ref[1])
    b = b.astype(jnp.int32)
    c = matmul(turned[16:32], maps_ref[2]).astype(jnp.int32)
    need = needed(a, b, c)

    r, p, owner, way = lane_facts(b.shape)
    t = lax.broadcasted_iota(jnp.int32, b.shape, 0)
    flags = jnp.where(need, 1.0, 0.0)
    alike = matmul(flags, maps_ref[3])
    upto = alike
    for step in (1, 2, 4):
        upto = upto + jnp.where(t >= step, pltpu.roll(upto, step, 0), 0.0)
    rank = (upto - alike + matmul(flags, maps_ref[4])).astype(jnp.int32)
    order = jnp.where(need, way * 128 + rank, -1)

    word = (((owner ^ row) & 1) * 16 + (p & 1) * 8 + t).astype(jnp.float32)
    n = 0
    for which, there in sends:
        for e in range(SLOTS):
            hit = (order == which * 128 + e) & (r == there(row))
            pack_list[n] = jnp.max(jnp.where(hit, word, -1.0)).astype(jnp.int32)
            n += 1

    info_ref[0:8] = a
    info_ref[8:16] = b
    info_ref[16:32] = c
    info_ref[32:40] = order
    here, sent, _ = entries_of(info_ref, row)
    extract(here, own_list)
    extract(sent, sent_list)


def plan(me, spots, sends):
    smem = pl.BlockSpec(memory_space=pltpu.SMEM)
    vmem = pl.BlockSpec(memory_space=pltpu.VMEM)
    return pl.pallas_call(
        functools.partial(plan_kernel, sends),
        in_specs=[smem, vmem],
        out_specs=[smem, smem, smem, vmem, vmem],
        out_shape=[
            jax.ShapeDtypeStruct((len(sends) * SLOTS,), jnp.int32),
            jax.ShapeDtypeStruct((LIST + 1,), jnp.int32),
            jax.ShapeDtypeStruct((LIST + 1,), jnp.int32),
            jax.ShapeDtypeStruct((40, 128), jnp.int32),
            jax.ShapeDtypeStruct((6, 128, 128), jnp.bfloat16),
        ],
        compiler_params=pltpu.CompilerParams(vmem_limit_bytes=16 << 20),
        name="plan",
    )(me, spots)


def pack_kernel(parts, list_ref, *rest):
    near, packed, sems = rest[:parts], rest[parts:-1], rest[-1]
    places = [(i, e) for i in range(len(packed)) for e in range(SLOTS)]
    for n, (i, e) in enumerate(places):
        word = list_ref[n]

        @pl.when(word >= 0)
        def _():
            fetch_block(word >> 4, word & 15, near, packed[i].at[e], sems.at[n])

    for n, (i, e) in enumerate(places):

        @pl.when(list_ref[n] >= 0)
        def _():
            pltpu.make_async_copy(near[0].at[0], packed[i].at[e], sems.at[n]).wait()


def pack(listing, near, sends):
    size = near[0].shape[-1]
    return pl.pallas_call(
        functools.partial(pack_kernel, len(near)),
        in_specs=[pl.BlockSpec(memory_space=pltpu.SMEM)]
        + [pl.BlockSpec(memory_space=pl.ANY)] * len(near),
        out_specs=[pl.BlockSpec(memory_space=pltpu.VMEM)] * len(sends),
        scratch_shapes=[pltpu.SemaphoreType.DMA((len(sends) * SLOTS,))],
        out_shape=[jax.ShapeDtypeStruct((SLOTS, size, size), jnp.float32)] * len(sends),
        compiler_params=pltpu.CompilerParams(vmem_limit_bytes=16 << 20),
        name="pack",
    )(listing, *near)


def overflow_kernel(spots_ref, maps_ref, over_ref):
    held = positions(spots_ref, maps_ref)
    a = held[:8].astype(jnp.int32)
    turned = [held[8:40]] + [pltpu.roll(held[8:40], 128 - q, 1) for q in range(1, 16)]
    b = matmul(jnp.concatenate([x[:8] for x in turned]), maps_ref[0])
    b = b + matmul(jnp.concatenate([x[8:16] for x in turned]), maps_ref[1])
    b = b.astype(jnp.int32)
    c = matmul(jnp.concatenate([x[16:32] for x in turned]), maps_ref[2]).astype(jnp.int32)
    flags = [
        jnp.where(needed(a, b[q * 8 : q * 8 + 8], c[q * 16 : q * 16 + 16]), 1.0, 0.0)
        for q in range(16)
    ]
    alike = matmul(jnp.concatenate(flags), maps_ref[3])
    most = jnp.sum(alike[:8], axis=0, keepdims=True)
    for q in range(1, 16):
        most = jnp.maximum(most, jnp.sum(alike[q * 8 : q * 8 + 8], axis=0, keepdims=True))
    *_, way = lane_facts(most.shape)
    slots = jnp.where(way == 0, 128, SLOTS)
    over_ref[0] = jnp.max(jnp.where(most > slots.astype(jnp.float32), 1.0, 0.0)).astype(jnp.int32)


def overflow(spots, maps):
    vmem = pl.BlockSpec(memory_space=pltpu.VMEM)
    return pl.pallas_call(
        overflow_kernel,
        in_specs=[vmem] * 2,
        out_specs=pl.BlockSpec(memory_space=pltpu.SMEM),
        out_shape=jax.ShapeDtypeStruct((1,), jnp.int32),
        compiler_params=pltpu.CompilerParams(vmem_limit_bytes=16 << 20),
        cost_estimate=pl.CostEstimate(flops=10**9, bytes_accessed=10**5, transcendentals=0),
        name="overflow",
    )(spots, maps)


def halves(x):
    high = x.astype(jnp.bfloat16)
    return high, (x - high.astype(jnp.float32)).astype(jnp.bfloat16)


def block_product(a, b):
    a_high, a_low = halves(a)
    b_high, b_low = halves(b)
    dot = functools.partial(jnp.dot, preferred_element_type=jnp.float32)
    return dot(a_high, b_high) + (dot(a_high, b_low) + dot(a_low, b_high))


def extract(entries, list_ref):
    def more(state):
        n, word, left = state
        list_ref[n] = word.astype(jnp.int32)
        left = jnp.where(left == word, -1.0, left)
        return n + 1, jnp.max(left), left

    n, *_ = lax.while_loop(
        lambda state: state[1] >= 0, more, (jnp.int32(0), jnp.max(entries), entries)
    )
    list_ref[LIST] = n


def entries_of(info_ref, row):
    b, c, order = info_ref[8:16], info_ref[16:32], info_ref[32:40]
    r, p, owner, way = lane_facts(b.shape)
    t = lax.broadcasted_iota(jnp.int32, b.shape, 0)
    rank = order & 127
    part = (owner ^ row) & 1
    sent = (way > 0) & (rank < SLOTS)
    found = [[], [], []]
    for s in range(SA):
        lands = lands_at(info_ref[s : s + 1], b)
        c_slot = jnp.full(b.shape, -1, jnp.int32)
        for n in range(c.shape[0]):
            c_slot = jnp.where(lands == c[n : n + 1], n, c_slot)
        live = (c_slot >= 0) & (r == row)
        a_slot = p * SA + s
        for found_in, mine, code_of in (
            (found[0], way == 0, code(a_slot, part, (p & 1) * 8 + t, c_slot)),
            (found[1], sent, code(a_slot, (way - 1) & 3, rank, c_slot)),
            (found[2], (way > 0) & ~sent, code(a_slot, 0, p * 8 + t, c_slot)),
        ):
            found_in.append(jnp.where(live & mine, code_of, -1).astype(jnp.float32))
    return [jnp.concatenate(x) for x in found]


def multiply_listed(list_ref, a_ref, b_refs, acc, a_buf, b_buf, a_sem, b_sem, meanwhile):
    count = list_ref[LIST]

    def fetch(n):
        slot = n % AHEAD
        word = list_ref[n]
        pltpu.make_async_copy(a_ref.at[a_of(word)], a_buf.at[slot], a_sem.at[slot]).start()
        fetch_block(part_of(word), at_of(word), b_refs, b_buf.at[slot], b_sem.at[slot])

    for n in range(AHEAD):

        @pl.when(n < count)
        def _():
            fetch(n)

    meanwhile()

    def step(n, carry):
        slot = n % AHEAD
        pltpu.make_async_copy(a_ref.at[0], a_buf.at[slot], a_sem.at[slot]).wait()
        pltpu.make_async_copy(b_refs[0].at[0], b_buf.at[slot], b_sem.at[slot]).wait()
        acc[c_of(list_ref[n])] += block_product(a_buf[slot], b_buf[slot])

        @pl.when(n + AHEAD < count)
        def _():
            fetch(n + AHEAD)

        return carry

    lax.fori_loop(0, count, step, 0)


def own_kernel(parts, list_ref, a_ref, *rest):
    b_refs, (out_ref, acc, c_sem, _, *buffers) = rest[:parts], rest[parts:]

    def meanwhile():
        acc[...] = jnp.zeros_like(acc)

    multiply_listed(list_ref, a_ref, b_refs, acc, *buffers, meanwhile)
    copy = pltpu.make_async_copy(acc, out_ref, c_sem.at[0])
    copy.start()
    copy.wait()


def add_listed(list_ref, a_ref, b_refs, total_ref, out_ref, acc, c_sem, stage, *buffers):
    count = list_ref[LIST]

    def touched(was, act):
        def step(n, carry):
            c = c_of(list_ref[n])

            @pl.when(stage[c] == was)
            def _():
                stage[c] = was + 1
                act(c)

            return carry

        lax.fori_loop(0, count, step, 0)

    def fetched(c):
        return pltpu.make_async_copy(total_ref.at[c], acc.at[c], c_sem.at[c])

    def stored(c):
        return pltpu.make_async_copy(acc.at[c], out_ref.at[c], c_sem.at[c])

    for c in range(acc.shape[0]):
        stage[c] = 0

    def meanwhile():
        touched(0, lambda c: fetched(c).start())
        touched(1, lambda c: fetched(c).wait())

    multiply_listed(list_ref, a_ref, b_refs, acc, *buffers, meanwhile)
    touched(2, lambda c: stored(c).start())
    touched(3, lambda c: stored(c).wait())


def sent_kernel(parts, list_ref, a_ref, *rest):
    add_listed(list_ref, a_ref, rest[:parts], *rest[parts:])


def rest_kernel(parts, me_ref, info_ref, a_ref, *rest):
    b_refs, (total_ref, out_ref, rest_list, *buffers) = rest[:parts], rest[parts:]
    extract(entries_of(info_ref, me_ref[0])[2], rest_list)
    add_listed(rest_list, a_ref, b_refs, total_ref, out_ref, *buffers)


def products(kernel, leading, a_all, b_parts, total, slots, own_list=False):
    size = a_all.shape[-1]
    smem = pl.BlockSpec(memory_space=pltpu.SMEM)
    vmem = pl.BlockSpec(memory_space=pltpu.VMEM)
    hbm = pl.BlockSpec(memory_space=pltpu.HBM)
    operands = [*leading, a_all, *b_parts] + ([] if total is None else [total])
    return pl.pallas_call(
        functools.partial(kernel, len(b_parts)),
        in_specs=[smem if x.ndim == 1 else vmem for x in leading]
        + [pl.BlockSpec(memory_space=pl.ANY)] * (1 + len(b_parts))
        + ([] if total is None else [hbm]),
        out_specs=hbm,
        out_shape=jax.ShapeDtypeStruct((slots, size, size), jnp.float32),
        scratch_shapes=([pltpu.SMEM((LIST + 1,), jnp.int32)] if own_list else [])
        + [
            pltpu.VMEM((slots, size, size), jnp.float32),
            pltpu.SemaphoreType.DMA((slots,)),
            pltpu.SMEM((slots,), jnp.int32),
            pltpu.VMEM((AHEAD, size, size), jnp.float32),
            pltpu.VMEM((AHEAD, size, size), jnp.float32),
            pltpu.SemaphoreType.DMA((AHEAD,)),
            pltpu.SemaphoreType.DMA((AHEAD,)),
        ],
        input_output_aliases={} if total is None else {len(operands) - 1: 0},
        compiler_params=pltpu.CompilerParams(vmem_limit_bytes=16 << 20),
        cost_estimate=pl.CostEstimate(
            flops=8 * 3 * 2 * size**3, bytes_accessed=24 * size * size * 4, transcendentals=0
        ),
        name="products",
    )(*operands)


def to_row(block, rows, there):
    return lax.ppermute(block, "row", [(i, there(i)) for i in range(rows)])


def everywhere(mine, rows, columns):
    axes = ("row", *COL)
    me = lax.axis_index("row") * columns + lax.axis_index(COL)
    held = mine
    for bits in ((3, 4), (5, 6), (1, 2), (0,)):
        group = jnp.zeros((2 ** len(bits),) + held.shape, held.dtype)
        for move in range(2 ** len(bits)):
            flip = sum(((move >> n) & 1) << bit for n, bit in enumerate(bits))
            got = held
            if move:
                got = lax.ppermute(held, axes, [(i ^ flip, i) for i in range(rows * columns)])
            spot = sum((((me ^ flip) >> bit) & 1) << n for n, bit in enumerate(bits))
            group = lax.dynamic_update_index_in_dim(group, got, spot, 0)
        held = group
    return held.reshape(rows * columns, mine.shape[0])


def per_device(a_blocks, a_index, b_blocks, b_index, c_index):
    rows = lax.axis_size("row")
    columns = lax.axis_size(COL)
    row = lax.axis_index("row")
    me = jnp.stack([row, lax.axis_index(COL)])
    hold = columns // rows
    sa, sb, sc = a_blocks.shape[2], b_blocks.shape[3], c_index.shape[2]
    held = hold * sb
    size = a_blocks.shape[-1]

    a_all = lax.all_gather(a_blocks[0, 0], COL).reshape(columns * sa, size, size)

    own = b_blocks[0, 0].reshape(held, size, size)
    near = [own, to_row(own, rows, lambda i: i ^ 1)]

    blank = jnp.full((8 - sa,), -1, jnp.int32)
    mine = jnp.concatenate([a_index[0, 0], blank, b_index[0, 0].reshape(-1), c_index[0, 0]])
    spots = everywhere(jnp.pad(mine, (0, 128 - mine.shape[0])), rows, columns)

    sends = [
        (1, lambda i: (i - 2) & 7),
        (2, lambda i: (i + 4) & 7),
        (3, lambda i: (i + 2) & 7),
    ]
    pack_list, own_list, sent_list, info, maps = plan(me, spots, sends)
    packed = pack(pack_list, near, sends)
    arrived = [to_row(block, rows, there) for block, (_, there) in zip(packed, sends)]

    total = products(own_kernel, [own_list], a_all, near, None, sc)
    total = products(sent_kernel, [sent_list], a_all, arrived, total, sc)

    trips = overflow(spots, maps)[0]

    def trip(state):
        done, total = state
        whole = lax.all_gather(own, "row").reshape(rows * held, size, size)
        rest = products(rest_kernel, [me, info], a_all, [whole], total, sc, own_list=True)
        return done + 1, rest

    _, total = lax.while_loop(lambda state: state[0] < trips, trip, (jnp.int32(0), total))
    return total[None, None]


def solution(mesh):
    rows, columns = mesh.devices.shape
    mesh = Mesh(mesh.devices.reshape(rows, 2, columns // 4, 2), ("row", *COL))
    in_specs = (
        P("row", COL, None, None, None),
        P("row", COL, None),
        P("row", COL, None, None, None, None),
        P("row", COL, None, None),
        P("row", COL, None),
    )
    out_specs = P("row", COL, None, None, None)
    return jax.shard_map(
        per_device, mesh=mesh, in_specs=in_specs, out_specs=out_specs, check_vma=False
    )
```

```python
import functools

import jax
import jax.numpy as jnp
from jax import lax
from jax.experimental import pallas as pl
from jax.experimental.pallas import tpu as pltpu
from jax.sharding import Mesh
from jax.sharding import PartitionSpec as P

SA = 4
PK = 8
NBD = 8
NEAR = 6
FAR = 3
COL = ("x_lo", "z", "core")
A_PARTS = 10
LIST = 512
AHEAD = 8


def matmul(a, b):
    return jnp.dot(a.astype(jnp.bfloat16), b, preferred_element_type=jnp.float32)


def lands_at(a_line, b):
    meet = (a_line >= 0) & (b >= 0) & ((a_line & (PK - 1)) == (b >> 3))
    return jnp.where(meet, (a_line >> 3) * NBD + (b & (NBD - 1)), -2)


def needed(a, b, c):
    need = jnp.zeros(b.shape, jnp.bool_)
    for s in range(SA):
        lands = lands_at(a[s : s + 1], b)
        for n in range(c.shape[0]):
            need = need | (lands == c[n : n + 1])
    return need


def lane_facts(shape, axis=1):
    lane = lax.broadcasted_iota(jnp.int32, shape, axis)
    r, p = lane >> 4, lane & 15
    owner = p >> 1
    far = (((owner >> 1) - (r >> 1)) & 3) == 2
    way = ((owner ^ r) & 1) + jnp.where(far, 2, 0)
    return r, p, owner, way


def code(a_slot, part, at, c_slot):
    return ((a_slot * 16 + part) * 128 + at) * 16 + c_slot


def a_of(word):
    return word >> 15


def part_of(word):
    return (word >> 11) & 15


def at_of(word):
    return (word >> 4) & 127


def c_of(word):
    return word & 15


def fetch_a(word, a_refs, dst, sem):
    a = a_of(word)
    fetch_block(a >> 3, a & 7, a_refs, dst, sem)


def fetch_block(part, at, refs, dst, sem):
    for i, ref in enumerate(refs):

        def start(ref=ref):
            pltpu.make_async_copy(ref.at[at], dst, sem).start()

        if len(refs) == 1:
            start()
        else:
            pl.when(part == i)(start)


def make_maps(maps_ref):
    shape = maps_ref.shape[1:]
    lane = lax.broadcasted_iota(jnp.int32, shape, 1)
    down = lax.broadcasted_iota(jnp.int32, shape, 0)
    r, p, owner, way = lane_facts(shape)
    r_down, p_down, _, way_down = lane_facts(shape, 0)
    holder = (p_down == 0) & (r_down == owner)
    alike = (r == r_down) & (way == way_down)
    y, xh, xl, z, core = lane >> 5, (lane >> 4) & 1, (lane >> 3) & 1, (lane >> 1) & 3, lane & 1
    listed_at = (((core * 4 + z) * 2 + xh) * 2 + xl) * 4 + y
    for n, flags in enumerate(
        [
            holder & ((p & 1) == 0),
            holder & ((p & 1) == 1),
            (p_down == 0) & (r == r_down),
            alike,
            alike & (down < lane),
            down == listed_at,
        ]
    ):
        maps_ref[n] = jnp.where(flags, 1.0, 0.0).astype(jnp.bfloat16)


def positions(spots_ref, maps_ref):
    spots = spots_ref[...].astype(jnp.float32).astype(jnp.bfloat16)
    return lax.dot_general(
        spots, maps_ref[5], (((0,), (0,)), ((), ())), preferred_element_type=jnp.float32
    )


def plan_kernel(sends, me_ref, spots_ref, pack_list, own_list, sent_list, info_ref, maps_ref):
    row, column = me_ref[0], me_ref[1]
    make_maps(maps_ref)
    held = positions(spots_ref, maps_ref)
    a = held[:8].astype(jnp.int32)
    turned = pltpu.roll(held[8:40], (128 - column) & 127, 1)
    b = matmul(turned[:8], maps_ref[0]) + matmul(turned[8:16], maps_ref[1])
    b = b.astype(jnp.int32)
    c = matmul(turned[16:32], maps_ref[2]).astype(jnp.int32)
    need = needed(a, b, c)

    r, p, owner, way = lane_facts(b.shape)
    t = lax.broadcasted_iota(jnp.int32, b.shape, 0)
    flags = jnp.where(need, 1.0, 0.0)
    alike = matmul(flags, maps_ref[3])
    upto = alike
    for step in (1, 2, 4):
        upto = upto + jnp.where(t >= step, pltpu.roll(upto, step, 0), 0.0)
    rank = (upto - alike + matmul(flags, maps_ref[4])).astype(jnp.int32)
    order = jnp.where(need, way * 128 + rank, -1)

    steps = ((owner >> 1) - (row >> 1)) & 3
    part = jnp.where(steps == 0, 0, jnp.where(steps == 3, 1, 2))
    word = (part * 16 + (p & 1) * 8 + t).astype(jnp.float32)
    n = 0
    for slots, which, there in sends:
        for e in range(slots):
            hit = (order == which * 128 + e) & (r == there(row))
            pack_list[n] = jnp.max(jnp.where(hit, word, -1.0)).astype(jnp.int32)
            n += 1

    info_ref[0:8] = a
    info_ref[8:16] = b
    info_ref[16:32] = c
    info_ref[32:40] = order
    here, sent, _ = entries_of(info_ref, me_ref)
    extract(here, own_list)
    extract(sent, sent_list)


def plan(me, spots, sends):
    smem = pl.BlockSpec(memory_space=pltpu.SMEM)
    vmem = pl.BlockSpec(memory_space=pltpu.VMEM)
    return pl.pallas_call(
        functools.partial(plan_kernel, sends),
        in_specs=[smem, vmem],
        out_specs=[smem, smem, smem, vmem, vmem],
        out_shape=[
            jax.ShapeDtypeStruct((sum(n for n, *_ in sends),), jnp.int32),
            jax.ShapeDtypeStruct((LIST + 1,), jnp.int32),
            jax.ShapeDtypeStruct((LIST + 1,), jnp.int32),
            jax.ShapeDtypeStruct((40, 128), jnp.int32),
            jax.ShapeDtypeStruct((6, 128, 128), jnp.bfloat16),
        ],
        compiler_params=pltpu.CompilerParams(vmem_limit_bytes=16 << 20),
        name="plan",
    )(me, spots)


def pack_kernel(sizes, list_ref, *rest):
    near, packed, sems = rest[:3], rest[3:-1], rest[-1]
    places = [(i, e) for i, size in enumerate(sizes) for e in range(size)]
    for n, (i, e) in enumerate(places):
        word = list_ref[n]

        @pl.when(word >= 0)
        def _():
            fetch_block(word >> 4, word & 15, near, packed[i].at[e], sems.at[n])

    for n, (i, e) in enumerate(places):

        @pl.when(list_ref[n] >= 0)
        def _():
            pltpu.make_async_copy(near[0].at[0], packed[i].at[e], sems.at[n]).wait()


def pack(listing, near, sizes):
    size = near[0].shape[-1]
    return pl.pallas_call(
        functools.partial(pack_kernel, sizes),
        in_specs=[pl.BlockSpec(memory_space=pltpu.SMEM)]
        + [pl.BlockSpec(memory_space=pl.ANY)] * 3,
        out_specs=[pl.BlockSpec(memory_space=pltpu.VMEM)] * len(sizes),
        scratch_shapes=[pltpu.SemaphoreType.DMA((sum(sizes),))],
        out_shape=[jax.ShapeDtypeStruct((n, size, size), jnp.float32) for n in sizes],
        compiler_params=pltpu.CompilerParams(vmem_limit_bytes=16 << 20),
        name="pack",
    )(listing, *near)


def overflow_kernel(spots_ref, maps_ref, over_ref):
    held = positions(spots_ref, maps_ref)
    a = held[:8].astype(jnp.int32)
    turned = [held[8:40]] + [pltpu.roll(held[8:40], 128 - q, 1) for q in range(1, 16)]
    b = matmul(jnp.concatenate([x[:8] for x in turned]), maps_ref[0])
    b = b + matmul(jnp.concatenate([x[8:16] for x in turned]), maps_ref[1])
    b = b.astype(jnp.int32)
    c = matmul(jnp.concatenate([x[16:32] for x in turned]), maps_ref[2]).astype(jnp.int32)
    flags = [
        jnp.where(needed(a, b[q * 8 : q * 8 + 8], c[q * 16 : q * 16 + 16]), 1.0, 0.0)
        for q in range(16)
    ]
    alike = matmul(jnp.concatenate(flags), maps_ref[3])
    most = jnp.sum(alike[:8], axis=0, keepdims=True)
    for q in range(1, 16):
        most = jnp.maximum(most, jnp.sum(alike[q * 8 : q * 8 + 8], axis=0, keepdims=True))
    *_, way = lane_facts(most.shape)
    slots = jnp.where(way == 0, 128, jnp.where(way == 1, NEAR, FAR))
    over_ref[0] = jnp.max(jnp.where(most > slots.astype(jnp.float32), 1.0, 0.0)).astype(jnp.int32)


def overflow(spots, maps):
    vmem = pl.BlockSpec(memory_space=pltpu.VMEM)
    return pl.pallas_call(
        overflow_kernel,
        in_specs=[vmem] * 2,
        out_specs=pl.BlockSpec(memory_space=pltpu.SMEM),
        out_shape=jax.ShapeDtypeStruct((1,), jnp.int32),
        compiler_params=pltpu.CompilerParams(vmem_limit_bytes=16 << 20),
        cost_estimate=pl.CostEstimate(flops=10**9, bytes_accessed=10**5, transcendentals=0),
        name="overflow",
    )(spots, maps)


def halves(x):
    high = x.astype(jnp.bfloat16)
    return high, (x - high.astype(jnp.float32)).astype(jnp.bfloat16)


def block_product(a, b):
    a_high, a_low = halves(a)
    b_high, b_low = halves(b)
    dot = functools.partial(jnp.dot, preferred_element_type=jnp.float32)
    return dot(a_high, b_high) + (dot(a_high, b_low) + dot(a_low, b_high))


def extract(entries, list_ref):
    def more(state):
        n, word, left = state
        list_ref[n] = word.astype(jnp.int32)
        left = jnp.where(left == word, -1.0, left)
        return n + 1, jnp.max(left), left

    n, *_ = lax.while_loop(
        lambda state: state[1] >= 0, more, (jnp.int32(0), jnp.max(entries), entries)
    )
    list_ref[LIST] = n


def entries_of(info_ref, me_ref):
    row, column = me_ref[0], me_ref[1]
    b, c, order = info_ref[8:16], info_ref[16:32], info_ref[32:40]
    r, p, owner, way = lane_facts(b.shape)
    t = lax.broadcasted_iota(jnp.int32, b.shape, 0)
    rank = order & 127
    steps = ((owner >> 1) - (row >> 1)) & 3
    part = jnp.where(steps == 0, 0, jnp.where(steps == 3, 1, 2))
    sent = (way > 0) & (rank < jnp.where(way == 1, NEAR, FAR))
    along = ((p >> 1) - (column >> 1)) & 3
    beside = ((p ^ column) >> 3) & 1
    a_part = jnp.where(along == 0, 0, jnp.where(along == 3, 1, jnp.where(along == 1, 2, 3 + beside)))
    a_at = (a_part + 5 * ((p ^ column) & 1)) * 8 + jnp.where(along == 2, 0, beside * SA)
    found = [[], [], []]
    for s in range(SA):
        lands = lands_at(info_ref[s : s + 1], b)
        c_slot = jnp.full(b.shape, -1, jnp.int32)
        for n in range(c.shape[0]):
            c_slot = jnp.where(lands == c[n : n + 1], n, c_slot)
        live = (c_slot >= 0) & (r == row)
        a_slot = a_at + s
        for found_in, mine, code_of in (
            (found[0], way == 0, code(a_slot, part, (p & 1) * 8 + t, c_slot)),
            (found[1], sent, code(a_slot, (way - 1) & 3, rank, c_slot)),
            (found[2], (way > 0) & ~sent, code(a_slot, owner ^ row, (p & 1) * 8 + t, c_slot)),
        ):
            found_in.append(jnp.where(live & mine, code_of, -1).astype(jnp.float32))
    return [jnp.concatenate(x) for x in found]


def multiply_listed(list_ref, a_refs, b_refs, out_ref, a_buf, b_buf, a_sem, b_sem, meanwhile):
    count = list_ref[LIST]

    def fetch(n):
        slot = n % AHEAD
        word = list_ref[n]
        fetch_a(word, a_refs, a_buf.at[slot], a_sem.at[slot])
        fetch_block(part_of(word), at_of(word), b_refs, b_buf.at[slot], b_sem.at[slot])

    for n in range(AHEAD):

        @pl.when(n < count)
        def _():
            fetch(n)

    meanwhile()

    def step(n, carry):
        slot = n % AHEAD
        pltpu.make_async_copy(a_refs[0].at[0], a_buf.at[slot], a_sem.at[slot]).wait()
        pltpu.make_async_copy(b_refs[0].at[0], b_buf.at[slot], b_sem.at[slot]).wait()
        out_ref[c_of(list_ref[n])] += block_product(a_buf[slot], b_buf[slot])

        @pl.when(n + AHEAD < count)
        def _():
            fetch(n + AHEAD)

        return carry

    lax.fori_loop(0, count, step, 0)


def own_kernel(parts, list_ref, *rest):
    a_refs, b_refs, (out_ref, *buffers) = rest[:A_PARTS], rest[A_PARTS:parts], rest[parts:]

    def meanwhile():
        out_ref[...] = jnp.zeros_like(out_ref)

    multiply_listed(list_ref, a_refs, b_refs, out_ref, *buffers, meanwhile)


def sent_kernel(parts, list_ref, *rest):
    a_refs, b_refs = rest[:A_PARTS], rest[A_PARTS:parts]
    total_ref, out_ref, *buffers = rest[parts:]

    def meanwhile():
        out_ref[...] = total_ref[...]

    multiply_listed(list_ref, a_refs, b_refs, out_ref, *buffers, meanwhile)


def rest_kernel(parts, me_ref, info_ref, *rest):
    a_refs, b_refs = rest[:A_PARTS], rest[A_PARTS:parts]
    total_ref, out_ref, rest_list, *buffers = rest[parts:]
    extract(entries_of(info_ref, me_ref)[2], rest_list)

    def meanwhile():
        out_ref[...] = total_ref[...]

    multiply_listed(rest_list, a_refs, b_refs, out_ref, *buffers, meanwhile)


def products(kernel, leading, a_parts, b_parts, total, slots, own_list=False):
    size = a_parts[0].shape[-1]
    parts = len(a_parts) + len(b_parts)
    smem = pl.BlockSpec(memory_space=pltpu.SMEM)
    vmem = pl.BlockSpec(memory_space=pltpu.VMEM)
    operands = [*leading, *a_parts, *b_parts] + ([] if total is None else [total])
    return pl.pallas_call(
        functools.partial(kernel, parts),
        in_specs=[smem if x.ndim == 1 else vmem for x in leading]
        + [pl.BlockSpec(memory_space=pl.ANY)] * parts
        + ([] if total is None else [vmem]),
        out_specs=vmem,
        out_shape=jax.ShapeDtypeStruct((slots, size, size), jnp.float32),
        scratch_shapes=([pltpu.SMEM((LIST + 1,), jnp.int32)] if own_list else [])
        + [
            pltpu.VMEM((AHEAD, size, size), jnp.float32),
            pltpu.VMEM((AHEAD, size, size), jnp.float32),
            pltpu.SemaphoreType.DMA((AHEAD,)),
            pltpu.SemaphoreType.DMA((AHEAD,)),
        ],
        input_output_aliases={} if total is None else {len(operands) - 1: 0},
        compiler_params=pltpu.CompilerParams(vmem_limit_bytes=16 << 20),
        cost_estimate=pl.CostEstimate(
            flops=8 * 3 * 2 * size**3, bytes_accessed=24 * size * size * 4, transcendentals=0
        ),
        name="products",
    )(*operands)


def to_row(block, rows, there):
    return lax.ppermute(block, "row", [(i, there(i)) for i in range(rows)])


def tiles(tile, columns):
    def moved(block, there):
        return lax.ppermute(block, COL, [(i, there(i)) for i in range(columns)])

    def on(i):
        return (i & 9) | ((i + 2) & 6)

    def back(i):
        return (i & 9) | ((i - 2) & 6)

    n = tile.shape[0]
    pair = jnp.concatenate([tile, moved(tile, lambda i: i ^ 8)])
    behind, ahead = moved(pair, on), moved(pair, back)
    mine = [pair, behind, ahead, moved(behind[:n], on), moved(ahead[n:], back)]
    return mine + [moved(block, lambda i: i ^ 1) for block in mine]


def everywhere(mine, rows, columns):
    axes = ("row", *COL)
    me = lax.axis_index("row") * columns + lax.axis_index(COL)
    held = mine
    for bits in ((5, 6), (3, 4), (1, 2), (0,)):
        group = jnp.zeros((2 ** len(bits),) + held.shape, held.dtype)
        for move in range(2 ** len(bits)):
            flip = sum(((move >> n) & 1) << bit for n, bit in enumerate(bits))
            got = held
            if move:
                got = lax.ppermute(held, axes, [(i ^ flip, i) for i in range(rows * columns)])
            spot = sum((((me ^ flip) >> bit) & 1) << n for n, bit in enumerate(bits))
            group = lax.dynamic_update_index_in_dim(group, got, spot, 0)
        held = group
    return held.reshape(rows * columns, mine.shape[0])


def per_device(a_blocks, a_index, b_blocks, b_index, c_index):
    rows = lax.axis_size("row")
    columns = lax.axis_size(COL)
    row = lax.axis_index("row")
    me = jnp.stack([row, lax.axis_index(COL)])
    hold = columns // rows
    sa, sb, sc = a_blocks.shape[2], b_blocks.shape[3], c_index.shape[2]
    held = hold * sb
    size = a_blocks.shape[-1]

    a_parts = tiles(a_blocks[0, 0], columns)

    own = b_blocks[0, 0].reshape(held, size, size)
    behind = to_row(own, rows, lambda i: (i + 2) % rows)
    ahead = to_row(own, rows, lambda i: (i - 2) % rows)
    near = [own, behind, ahead]

    blank = jnp.full((8 - sa,), -1, jnp.int32)
    mine = jnp.concatenate([a_index[0, 0], blank, b_index[0, 0].reshape(-1), c_index[0, 0]])
    spots = everywhere(jnp.pad(mine, (0, 128 - mine.shape[0])), rows, columns)

    sends = [
        (FAR, 2, lambda i: (i + 2) & 7),
        (FAR, 3, lambda i: ((i + 2) & 7) ^ 1),
        (NEAR, 1, lambda i: i ^ 1),
    ]
    pack_list, own_list, sent_list, info, maps = plan(me, spots, sends)
    packed = pack(pack_list, near, [n for n, *_ in sends])
    far_own, far_other, cross = [
        to_row(block, rows, there) for block, (*_, there) in zip(packed, sends)
    ]

    total = products(own_kernel, [own_list], a_parts, near, None, sc)
    total = products(
        sent_kernel, [sent_list], a_parts, [cross, far_own, far_other], total, sc
    )

    trips = overflow(spots, maps)[0]

    def trip(state):
        done, total = state
        sent = jnp.where(done >= 0, own, 0)
        whole = [own] + [to_row(sent, rows, lambda i, n=n: i ^ n) for n in range(1, rows)]
        rest = products(rest_kernel, [me, info], a_parts, whole, total, sc, own_list=True)
        return done + 1, rest

    _, total = lax.while_loop(lambda state: state[0] < trips, trip, (jnp.int32(0), total))
    return total[None, None]


def solution(mesh):
    rows, columns = mesh.devices.shape
    mesh = Mesh(mesh.devices.reshape(rows, 2, columns // 4, 2), ("row", *COL))
    in_specs = (
        P("row", COL, None, None, None),
        P("row", COL, None),
        P("row", COL, None, None, None, None),
        P("row", COL, None, None),
        P("row", COL, None),
    )
    out_specs = P("row", COL, None, None, None)
    return jax.shard_map(
        per_device, mesh=mesh, in_specs=in_specs, out_specs=out_specs, check_vma=False
    )
```

```python
import functools

import jax
import jax.numpy as jnp
from jax import lax
from jax.experimental import pallas as pl
from jax.experimental.pallas import tpu as pltpu
from jax.sharding import Mesh
from jax.sharding import PartitionSpec as P

SA = 4
PK = 8
NBD = 8
NEAR = 6
FAR = 3
COL = ("x_lo", "z", "core")
VMEM_LIMIT = 16 << 20
A_PARTS = 10
LIST = 512
AHEAD = 8


def matmul(a, b):
    return jnp.dot(a.astype(jnp.bfloat16), b, preferred_element_type=jnp.float32)


def lands_at(a_line, b):
    meet = (a_line >= 0) & (b >= 0) & ((a_line & (PK - 1)) == (b >> 3))
    return jnp.where(meet, (a_line >> 3) * NBD + (b & (NBD - 1)), -2)


def needed(a, b, c):
    need = jnp.zeros(b.shape, jnp.bool_)
    for s in range(SA):
        lands = lands_at(a[s : s + 1], b)
        for n in range(c.shape[0]):
            need = need | (lands == c[n : n + 1])
    return need


def lane_facts(shape, axis=1):
    lane = lax.broadcasted_iota(jnp.int32, shape, axis)
    r, p = lane >> 4, lane & 15
    owner = p >> 1
    far = (((owner >> 1) - (r >> 1)) & 3) == 2
    way = ((owner ^ r) & 1) + jnp.where(far, 2, 0)
    return r, p, owner, way


def code(a_slot, part, at, c_slot):
    return ((a_slot * 16 + part) * 128 + at) * 16 + c_slot


def a_of(word):
    return word >> 15


def part_of(word):
    return (word >> 11) & 15


def at_of(word):
    return (word >> 4) & 127


def c_of(word):
    return word & 15


def fetch_a(word, a_refs, dst, sem):
    a = a_of(word)
    fetch_block(a >> 3, a & 7, a_refs, dst, sem)


def fetch_block(part, at, refs, dst, sem):
    for i, ref in enumerate(refs):

        def start(ref=ref):
            pltpu.make_async_copy(ref.at[at], dst, sem).start()

        if len(refs) == 1:
            start()
        else:
            pl.when(part == i)(start)


def make_maps(maps_ref):
    shape = maps_ref.shape[1:]
    lane = lax.broadcasted_iota(jnp.int32, shape, 1)
    down = lax.broadcasted_iota(jnp.int32, shape, 0)
    r, p, owner, way = lane_facts(shape)
    r_down, p_down, _, way_down = lane_facts(shape, 0)
    holder = (p_down == 0) & (r_down == owner)
    alike = (r == r_down) & (way == way_down)
    y, xh, xl, z, core = lane >> 5, (lane >> 4) & 1, (lane >> 3) & 1, (lane >> 1) & 3, lane & 1
    listed_at = (((core * 2 + xh) * 2 + xl) * 4 + z) * 4 + y
    for n, flags in enumerate(
        [
            holder & ((p & 1) == 0),
            holder & ((p & 1) == 1),
            (p_down == 0) & (r == r_down),
            alike,
            alike & (down < lane),
            down == listed_at,
        ]
    ):
        maps_ref[n] = jnp.where(flags, 1.0, 0.0).astype(jnp.bfloat16)


def positions(spots_ref, maps_ref):
    spots = spots_ref[...].astype(jnp.float32).astype(jnp.bfloat16)
    return lax.dot_general(
        spots, maps_ref[5], (((0,), (0,)), ((), ())), preferred_element_type=jnp.float32
    )


def plan_kernel(sends, me_ref, spots_ref, pack_list, own_list, sent_list, info_ref, maps_ref):
    row, column = me_ref[0], me_ref[1]
    make_maps(maps_ref)
    held = positions(spots_ref, maps_ref)
    a = held[:8].astype(jnp.int32)
    turned = pltpu.roll(held[8:40], (128 - column) & 127, 1)
    b = matmul(turned[:8], maps_ref[0]) + matmul(turned[8:16], maps_ref[1])
    b = b.astype(jnp.int32)
    c = matmul(turned[16:32], maps_ref[2]).astype(jnp.int32)
    need = needed(a, b, c)

    r, p, owner, way = lane_facts(b.shape)
    t = lax.broadcasted_iota(jnp.int32, b.shape, 0)
    flags = jnp.where(need, 1.0, 0.0)
    alike = matmul(flags, maps_ref[3])
    upto = alike
    for step in (1, 2, 4):
        upto = upto + jnp.where(t >= step, pltpu.roll(upto, step, 0), 0.0)
    rank = (upto - alike + matmul(flags, maps_ref[4])).astype(jnp.int32)
    order = jnp.where(need, way * 128 + rank, -1)

    steps = ((owner >> 1) - (row >> 1)) & 3
    part = jnp.where(steps == 0, 0, jnp.where(steps == 3, 1, 2))
    word = (part * 16 + (p & 1) * 8 + t).astype(jnp.float32)
    n = 0
    for slots, which, there in sends:
        for e in range(slots):
            hit = (order == which * 128 + e) & (r == there(row))
            pack_list[n] = jnp.max(jnp.where(hit, word, -1.0)).astype(jnp.int32)
            n += 1

    info_ref[0:8] = a
    info_ref[8:16] = b
    info_ref[16:32] = c
    info_ref[32:40] = order
    here, sent, _ = entries_of(info_ref, me_ref)
    extract(here, own_list)
    extract(sent, sent_list)


def plan(me, spots, sends):
    smem = pl.BlockSpec(memory_space=pltpu.SMEM)
    vmem = pl.BlockSpec(memory_space=pltpu.VMEM)
    return pl.pallas_call(
        functools.partial(plan_kernel, sends),
        in_specs=[smem, vmem],
        out_specs=[smem, smem, smem, vmem, vmem],
        out_shape=[
            jax.ShapeDtypeStruct((sum(n for n, *_ in sends),), jnp.int32),
            jax.ShapeDtypeStruct((LIST + 1,), jnp.int32),
            jax.ShapeDtypeStruct((LIST + 1,), jnp.int32),
            jax.ShapeDtypeStruct((40, 128), jnp.int32),
            jax.ShapeDtypeStruct((6, 128, 128), jnp.bfloat16),
        ],
        compiler_params=pltpu.CompilerParams(vmem_limit_bytes=16 << 20),
        name="plan",
    )(me, spots)


def pack_kernel(sizes, list_ref, *rest):
    near, packed, sems = rest[:3], rest[3:-1], rest[-1]
    places = [(i, e) for i, size in enumerate(sizes) for e in range(size)]
    for n, (i, e) in enumerate(places):
        word = list_ref[n]

        @pl.when(word >= 0)
        def _():
            fetch_block(word >> 4, word & 15, near, packed[i].at[e], sems.at[n])

    for n, (i, e) in enumerate(places):

        @pl.when(list_ref[n] >= 0)
        def _():
            pltpu.make_async_copy(near[0].at[0], packed[i].at[e], sems.at[n]).wait()


def pack(listing, near, sizes):
    size = near[0].shape[-1]
    return pl.pallas_call(
        functools.partial(pack_kernel, sizes),
        in_specs=[pl.BlockSpec(memory_space=pltpu.SMEM)]
        + [pl.BlockSpec(memory_space=pl.ANY)] * 3,
        out_specs=[pl.BlockSpec(memory_space=pltpu.VMEM)] * len(sizes),
        scratch_shapes=[pltpu.SemaphoreType.DMA((sum(sizes),))],
        out_shape=[jax.ShapeDtypeStruct((n, size, size), jnp.float32) for n in sizes],
        compiler_params=pltpu.CompilerParams(vmem_limit_bytes=16 << 20),
        name="pack",
    )(listing, *near)


def overflow_kernel(spots_ref, maps_ref, over_ref):
    held = positions(spots_ref, maps_ref)
    a = held[:8].astype(jnp.int32)
    turned = [held[8:40]] + [pltpu.roll(held[8:40], 128 - q, 1) for q in range(1, 16)]
    b = matmul(jnp.concatenate([x[:8] for x in turned]), maps_ref[0])
    b = b + matmul(jnp.concatenate([x[8:16] for x in turned]), maps_ref[1])
    b = b.astype(jnp.int32)
    c = matmul(jnp.concatenate([x[16:32] for x in turned]), maps_ref[2]).astype(jnp.int32)
    flags = [
        jnp.where(needed(a, b[q * 8 : q * 8 + 8], c[q * 16 : q * 16 + 16]), 1.0, 0.0)
        for q in range(16)
    ]
    alike = matmul(jnp.concatenate(flags), maps_ref[3])
    most = jnp.sum(alike[:8], axis=0, keepdims=True)
    for q in range(1, 16):
        most = jnp.maximum(most, jnp.sum(alike[q * 8 : q * 8 + 8], axis=0, keepdims=True))
    *_, way = lane_facts(most.shape)
    slots = jnp.where(way == 0, 128, jnp.where(way == 1, NEAR, FAR))
    over_ref[0] = jnp.max(jnp.where(most > slots.astype(jnp.float32), 1.0, 0.0)).astype(jnp.int32)


def overflow(spots, maps):
    vmem = pl.BlockSpec(memory_space=pltpu.VMEM)
    return pl.pallas_call(
        overflow_kernel,
        in_specs=[vmem] * 2,
        out_specs=pl.BlockSpec(memory_space=pltpu.SMEM),
        out_shape=jax.ShapeDtypeStruct((1,), jnp.int32),
        compiler_params=pltpu.CompilerParams(vmem_limit_bytes=16 << 20),
        cost_estimate=pl.CostEstimate(flops=10**9, bytes_accessed=10**5, transcendentals=0),
        name="overflow",
    )(spots, maps)


def halves(x):
    high = x.astype(jnp.bfloat16)
    return high, (x - high.astype(jnp.float32)).astype(jnp.bfloat16)


def block_product(a, b):
    a_high, a_low = halves(a)
    b_high, b_low = halves(b)
    dot = functools.partial(jnp.dot, preferred_element_type=jnp.float32)
    return dot(a_high, b_high) + (dot(a_high, b_low) + dot(a_low, b_high))


def extract(entries, list_ref):
    def more(state):
        n, word, left = state
        list_ref[n] = word.astype(jnp.int32)
        left = jnp.where(left == word, -1.0, left)
        return n + 1, jnp.max(left), left

    n, *_ = lax.while_loop(
        lambda state: state[1] >= 0, more, (jnp.int32(0), jnp.max(entries), entries)
    )
    list_ref[LIST] = n


def entries_of(info_ref, me_ref):
    row, column = me_ref[0], me_ref[1]
    b, c, order = info_ref[8:16], info_ref[16:32], info_ref[32:40]
    r, p, owner, way = lane_facts(b.shape)
    t = lax.broadcasted_iota(jnp.int32, b.shape, 0)
    rank = order & 127
    steps = ((owner >> 1) - (row >> 1)) & 3
    part = jnp.where(steps == 0, 0, jnp.where(steps == 3, 1, 2))
    sent = (way > 0) & (rank < jnp.where(way == 1, NEAR, FAR))
    along = ((p >> 1) - (column >> 1)) & 3
    beside = ((p ^ column) >> 3) & 1
    a_part = jnp.where(along == 0, 0, jnp.where(along == 3, 1, jnp.where(along == 1, 2, 3 + beside)))
    a_at = (a_part + 5 * ((p ^ column) & 1)) * 8 + jnp.where(along == 2, 0, beside * SA)
    found = [[], [], []]
    for s in range(SA):
        lands = lands_at(info_ref[s : s + 1], b)
        c_slot = jnp.full(b.shape, -1, jnp.int32)
        for n in range(c.shape[0]):
            c_slot = jnp.where(lands == c[n : n + 1], n, c_slot)
        live = (c_slot >= 0) & (r == row)
        a_slot = a_at + s
        for found_in, mine, code_of in (
            (found[0], way == 0, code(a_slot, part, (p & 1) * 8 + t, c_slot)),
            (found[1], sent, code(a_slot, (way - 1) & 3, rank, c_slot)),
            (found[2], (way > 0) & ~sent, code(a_slot, owner ^ row, (p & 1) * 8 + t, c_slot)),
        ):
            found_in.append(jnp.where(live & mine, code_of, -1).astype(jnp.float32))
    return [jnp.concatenate(x) for x in found]


def multiply_listed(list_ref, a_refs, b_refs, acc, a_buf, b_buf, a_sem, b_sem, meanwhile):
    count = list_ref[LIST]

    def fetch(n):
        slot = n % AHEAD
        word = list_ref[n]
        fetch_a(word, a_refs, a_buf.at[slot], a_sem.at[slot])
        fetch_block(part_of(word), at_of(word), b_refs, b_buf.at[slot], b_sem.at[slot])

    for n in range(AHEAD):

        @pl.when(n < count)
        def _():
            fetch(n)

    meanwhile()

    def step(n, carry):
        slot = n % AHEAD
        pltpu.make_async_copy(a_refs[0].at[0], a_buf.at[slot], a_sem.at[slot]).wait()
        pltpu.make_async_copy(b_refs[0].at[0], b_buf.at[slot], b_sem.at[slot]).wait()
        acc[c_of(list_ref[n])] += block_product(a_buf[slot], b_buf[slot])

        @pl.when(n + AHEAD < count)
        def _():
            fetch(n + AHEAD)

        return carry

    lax.fori_loop(0, count, step, 0)


def own_kernel(parts, list_ref, *rest):
    a_refs, b_refs = rest[:A_PARTS], rest[A_PARTS:parts]
    out_ref, acc, c_sem, _, *buffers = rest[parts:]

    def meanwhile():
        acc[...] = jnp.zeros_like(acc)

    multiply_listed(list_ref, a_refs, b_refs, acc, *buffers, meanwhile)
    copy = pltpu.make_async_copy(acc, out_ref, c_sem.at[0])
    copy.start()
    copy.wait()


def add_listed(list_ref, a_refs, b_refs, total_ref, out_ref, acc, c_sem, stage, *buffers):
    count = list_ref[LIST]

    def touched(was, act):
        def step(n, carry):
            c = c_of(list_ref[n])

            @pl.when(stage[c] == was)
            def _():
                stage[c] = was + 1
                act(c)

            return carry

        lax.fori_loop(0, count, step, 0)

    def fetched(c):
        return pltpu.make_async_copy(total_ref.at[c], acc.at[c], c_sem.at[c])

    def stored(c):
        return pltpu.make_async_copy(acc.at[c], out_ref.at[c], c_sem.at[c])

    for c in range(acc.shape[0]):
        stage[c] = 0

    def meanwhile():
        touched(0, lambda c: fetched(c).start())
        touched(1, lambda c: fetched(c).wait())

    multiply_listed(list_ref, a_refs, b_refs, acc, *buffers, meanwhile)
    touched(2, lambda c: stored(c).start())
    touched(3, lambda c: stored(c).wait())


def sent_kernel(parts, list_ref, *rest):
    add_listed(list_ref, rest[:A_PARTS], rest[A_PARTS:parts], *rest[parts:])


def rest_kernel(parts, me_ref, info_ref, *rest):
    a_refs, b_refs = rest[:A_PARTS], rest[A_PARTS:parts]
    total_ref, out_ref, rest_list, *buffers = rest[parts:]
    extract(entries_of(info_ref, me_ref)[2], rest_list)
    add_listed(rest_list, a_refs, b_refs, total_ref, out_ref, *buffers)


def products(kernel, leading, a_parts, b_parts, total, slots, own_list=False):
    size = a_parts[0].shape[-1]
    parts = len(a_parts) + len(b_parts)
    smem = pl.BlockSpec(memory_space=pltpu.SMEM)
    vmem = pl.BlockSpec(memory_space=pltpu.VMEM)
    hbm = pl.BlockSpec(memory_space=pltpu.HBM)
    operands = [*leading, *a_parts, *b_parts] + ([] if total is None else [total])
    return pl.pallas_call(
        functools.partial(kernel, parts),
        in_specs=[smem if x.ndim == 1 else vmem for x in leading]
        + [pl.BlockSpec(memory_space=pl.ANY)] * parts
        + ([] if total is None else [hbm]),
        out_specs=hbm,
        out_shape=jax.ShapeDtypeStruct((slots, size, size), jnp.float32),
        scratch_shapes=([pltpu.SMEM((LIST + 1,), jnp.int32)] if own_list else [])
        + [
            pltpu.VMEM((slots, size, size), jnp.float32),
            pltpu.SemaphoreType.DMA((slots,)),
            pltpu.SMEM((slots,), jnp.int32),
            pltpu.VMEM((AHEAD, size, size), jnp.float32),
            pltpu.VMEM((AHEAD, size, size), jnp.float32),
            pltpu.SemaphoreType.DMA((AHEAD,)),
            pltpu.SemaphoreType.DMA((AHEAD,)),
        ],
        input_output_aliases={} if total is None else {len(operands) - 1: 0},
        compiler_params=pltpu.CompilerParams(vmem_limit_bytes=VMEM_LIMIT),
        cost_estimate=pl.CostEstimate(
            flops=8 * 3 * 2 * size**3, bytes_accessed=24 * size * size * 4, transcendentals=0
        ),
        name="products",
    )(*operands)


def to_row(block, rows, there):
    return lax.ppermute(block, "row", [(i, there(i)) for i in range(rows)])


def on_z(i):
    return (i & 9) | ((i + 2) & 6)


def back_z(i):
    return (i & 9) | ((i - 2) & 6)


def moved(block, there, columns):
    return lax.ppermute(block, COL, [(i, there(i)) for i in range(columns)])


def pair_kernel(tile_ref, beside_ref, _, pair_ref, sems):
    n = tile_ref.shape[0]
    copies = [
        pltpu.make_async_copy(tile_ref, pair_ref.at[pl.ds(0, n)], sems.at[0]),
        pltpu.make_async_copy(beside_ref, pair_ref.at[pl.ds(n, n)], sems.at[1]),
    ]
    for copy in copies:
        copy.start()
    for copy in copies:
        copy.wait()


def paired(tile, beside, later):
    n, size = tile.shape[0], tile.shape[-1]
    return pl.pallas_call(
        pair_kernel,
        in_specs=[pl.BlockSpec(memory_space=pl.ANY)] * 3,
        out_specs=pl.BlockSpec(memory_space=pltpu.VMEM),
        out_shape=jax.ShapeDtypeStruct((2 * n, size, size), tile.dtype),
        scratch_shapes=[pltpu.SemaphoreType.DMA((2,))],
        compiler_params=pltpu.CompilerParams(vmem_limit_bytes=16 << 20),
        name="pair",
    )(tile, beside, later)


def onward_kernel(behind_ref, ahead_ref, _, behind_out, ahead_out, first_ref, second_ref, sems):
    n = first_ref.shape[0]
    copies = [
        pltpu.make_async_copy(behind_ref.at[pl.ds(0, n)], first_ref, sems.at[0]),
        pltpu.make_async_copy(ahead_ref.at[pl.ds(n, n)], second_ref, sems.at[1]),
    ]
    for copy in copies:
        copy.start()
    for copy in copies:
        copy.wait()


def onward(behind, ahead, later):
    n, size = behind.shape[0] // 2, behind.shape[-1]
    anywhere = pl.BlockSpec(memory_space=pl.ANY)
    tile = jax.ShapeDtypeStruct((n, size, size), behind.dtype)
    pair = jax.ShapeDtypeStruct(behind.shape, behind.dtype)
    return pl.pallas_call(
        onward_kernel,
        in_specs=[anywhere] * 3,
        out_specs=[anywhere] * 2 + [pl.BlockSpec(memory_space=pltpu.VMEM)] * 2,
        out_shape=[pair, pair, tile, tile],
        scratch_shapes=[pltpu.SemaphoreType.DMA((2,))],
        input_output_aliases={0: 0, 1: 1},
        compiler_params=pltpu.CompilerParams(vmem_limit_bytes=16 << 20),
        name="onward",
    )(behind, ahead, later)


def hold_kernel(first_ref, second_ref, _, first_out, second_out):
    pass


def held_for(first, second, later):
    anywhere = pl.BlockSpec(memory_space=pl.ANY)
    return pl.pallas_call(
        hold_kernel,
        in_specs=[anywhere] * 3,
        out_specs=[anywhere] * 2,
        out_shape=[jax.ShapeDtypeStruct(x.shape, x.dtype) for x in (first, second)],
        input_output_aliases={0: 0, 1: 1},
        name="hold",
    )(first, second, later)


def everywhere(mine, rows, columns):
    axes = ("row", *COL)
    me = lax.axis_index("row") * columns + lax.axis_index(COL)
    held = mine
    for bits in ((5, 6), (1, 2), (3, 4), (0,)):
        group = jnp.zeros((2 ** len(bits),) + held.shape, held.dtype)
        for move in range(2 ** len(bits)):
            flip = sum(((move >> n) & 1) << bit for n, bit in enumerate(bits))
            got = held
            if move:
                got = lax.ppermute(held, axes, [(i ^ flip, i) for i in range(rows * columns)])
            spot = sum((((me ^ flip) >> bit) & 1) << n for n, bit in enumerate(bits))
            group = lax.dynamic_update_index_in_dim(group, got, spot, 0)
        held = group
        if bits == (1, 2):
            midway = held
    return held.reshape(rows * columns, mine.shape[0]), midway


def per_device(a_blocks, a_index, b_blocks, b_index, c_index):
    rows = lax.axis_size("row")
    columns = lax.axis_size(COL)
    row = lax.axis_index("row")
    me = jnp.stack([row, lax.axis_index(COL)])
    hold = columns // rows
    sa, sb, sc = a_blocks.shape[2], b_blocks.shape[3], c_index.shape[2]
    held = hold * sb
    size = a_blocks.shape[-1]

    own = b_blocks[0, 0].reshape(held, size, size)
    behind = to_row(own, rows, lambda i: (i + 2) % rows)
    ahead = to_row(own, rows, lambda i: (i - 2) % rows)
    near = [own, behind, ahead]

    blank = jnp.full((8 - sa,), -1, jnp.int32)
    mine = jnp.concatenate([a_index[0, 0], blank, b_index[0, 0].reshape(-1), c_index[0, 0]])
    spots, midway = everywhere(jnp.pad(mine, (0, 128 - mine.shape[0])), rows, columns)

    tile = a_blocks[0, 0]
    pair = paired(tile, moved(tile, lambda i: i ^ 8, columns), midway)
    a_behind = moved(pair, on_z, columns)
    a_ahead = moved(pair, back_z, columns)

    sends = [
        (FAR, 2, lambda i: (i + 2) & 7),
        (FAR, 3, lambda i: ((i + 2) & 7) ^ 1),
        (NEAR, 1, lambda i: i ^ 1),
    ]
    pack_list, own_list, sent_list, info, maps = plan(me, spots, sends)
    packed = pack(pack_list, near, [n for n, *_ in sends])

    far_own, far_other, cross = [
        to_row(block, rows, there) for block, (*_, there) in zip(packed, sends)
    ]

    a_behind, a_ahead, first, second = onward(a_behind, a_ahead, info)
    first, second = moved(first, on_z, columns), moved(second, back_z, columns)
    first, second = held_for(first, second, packed[0])
    a_mine = [pair, a_behind, a_ahead, first, second]
    a_parts = a_mine + [moved(block, lambda i: i ^ 1, columns) for block in a_mine]

    total = products(own_kernel, [own_list], a_parts, near, None, sc)
    total = products(
        sent_kernel, [sent_list], a_parts, [cross, far_own, far_other], total, sc
    )

    trips = overflow(spots, maps)[0]

    def trip(state):
        done, total = state
        sent = jnp.where(done >= 0, own, 0)
        whole = [own] + [to_row(sent, rows, lambda i, n=n: i ^ n) for n in range(1, rows)]
        rest = products(rest_kernel, [me, info], a_parts, whole, total, sc, own_list=True)
        return done + 1, rest

    _, total = lax.while_loop(lambda state: state[0] < trips, trip, (jnp.int32(0), total))
    return total[None, None]


def solution(mesh):
    rows, columns = mesh.devices.shape
    mesh = Mesh(mesh.devices.reshape(rows, 2, columns // 4, 2), ("row", *COL))
    in_specs = (
        P("row", COL, None, None, None),
        P("row", COL, None),
        P("row", COL, None, None, None, None),
        P("row", COL, None, None),
        P("row", COL, None),
    )
    out_specs = P("row", COL, None, None, None)
    return jax.shard_map(
        per_device, mesh=mesh, in_specs=in_specs, out_specs=out_specs, check_vma=False
    )
```

```python
import functools

import jax
import jax.numpy as jnp
from jax import lax
from jax.experimental import pallas as pl
from jax.experimental.pallas import tpu as pltpu
from jax.sharding import Mesh
from jax.sharding import PartitionSpec as P

SA = 4
PK = 8
NBD = 8
NEAR = 6
FAR = 3
COL = ("x_lo", "z", "core")
VMEM_LIMIT = 16 << 20
A_PARTS = 8
LIST = 512
AHEAD = 8


def matmul(a, b):
    return jnp.dot(a.astype(jnp.bfloat16), b, preferred_element_type=jnp.float32)


def lands_at(a_line, b):
    meet = (a_line >= 0) & (b >= 0) & ((a_line & (PK - 1)) == (b >> 3))
    return jnp.where(meet, (a_line >> 3) * NBD + (b & (NBD - 1)), -2)


def needed(a, b, c):
    need = jnp.zeros(b.shape, jnp.bool_)
    for s in range(SA):
        lands = lands_at(a[s : s + 1], b)
        for n in range(c.shape[0]):
            need = need | (lands == c[n : n + 1])
    return need


def lane_facts(shape, axis=1):
    lane = lax.broadcasted_iota(jnp.int32, shape, axis)
    r, p = lane >> 4, lane & 15
    owner = p >> 1
    far = (((owner >> 1) - (r >> 1)) & 3) == 2
    way = ((owner ^ r) & 1) + jnp.where(far, 2, 0)
    return r, p, owner, way


def code(a_slot, part, at, c_slot):
    return ((a_slot * 16 + part) * 128 + at) * 16 + c_slot


def a_of(word):
    return word >> 15


def part_of(word):
    return (word >> 11) & 15


def at_of(word):
    return (word >> 4) & 127


def c_of(word):
    return word & 15


def fetch_a(word, a_refs, dst, sem):
    a = a_of(word)
    fetch_block(a >> 3, a & 7, a_refs, dst, sem)


def fetch_block(part, at, refs, dst, sem):
    for i, ref in enumerate(refs):

        def start(ref=ref):
            pltpu.make_async_copy(ref.at[at], dst, sem).start()

        if len(refs) == 1:
            start()
        else:
            pl.when(part == i)(start)


def make_maps(maps_ref):
    shape = maps_ref.shape[1:]
    lane = lax.broadcasted_iota(jnp.int32, shape, 1)
    down = lax.broadcasted_iota(jnp.int32, shape, 0)
    r, p, owner, way = lane_facts(shape)
    r_down, p_down, _, way_down = lane_facts(shape, 0)
    holder = (p_down == 0) & (r_down == owner)
    alike = (r == r_down) & (way == way_down)
    y, xh, xl, z, core = lane >> 5, (lane >> 4) & 1, (lane >> 3) & 1, (lane >> 1) & 3, lane & 1
    listed_at = (((core * 2 + xh) * 2 + xl) * 4 + z) * 4 + y
    for n, flags in enumerate(
        [
            holder & ((p & 1) == 0),
            holder & ((p & 1) == 1),
            (p_down == 0) & (r == r_down),
            alike,
            alike & (down < lane),
            down == listed_at,
        ]
    ):
        maps_ref[n] = jnp.where(flags, 1.0, 0.0).astype(jnp.bfloat16)


def positions(spots_ref, maps_ref):
    spots = spots_ref[...].astype(jnp.float32).astype(jnp.bfloat16)
    return lax.dot_general(
        spots, maps_ref[5], (((0,), (0,)), ((), ())), preferred_element_type=jnp.float32
    )


def plan_kernel(sends, me_ref, spots_ref, pack_list, product_list, info_ref, maps_ref):
    row, column = me_ref[0], me_ref[1]
    make_maps(maps_ref)
    held = positions(spots_ref, maps_ref)
    a = held[:8].astype(jnp.int32)
    turned = pltpu.roll(held[8:40], (128 - column) & 127, 1)
    b = matmul(turned[:8], maps_ref[0]) + matmul(turned[8:16], maps_ref[1])
    b = b.astype(jnp.int32)
    c = matmul(turned[16:32], maps_ref[2]).astype(jnp.int32)
    need = needed(a, b, c)

    r, p, owner, way = lane_facts(b.shape)
    t = lax.broadcasted_iota(jnp.int32, b.shape, 0)
    flags = jnp.where(need, 1.0, 0.0)
    alike = matmul(flags, maps_ref[3])
    upto = alike
    for step in (1, 2, 4):
        upto = upto + jnp.where(t >= step, pltpu.roll(upto, step, 0), 0.0)
    rank = (upto - alike + matmul(flags, maps_ref[4])).astype(jnp.int32)
    order = jnp.where(need, way * 128 + rank, -1)

    steps = ((owner >> 1) - (row >> 1)) & 3
    part = jnp.where(steps == 0, 0, jnp.where(steps == 3, 1, 2))
    word = (part * 16 + (p & 1) * 8 + t).astype(jnp.float32)
    n = 0
    for slots, which, there in sends:
        for e in range(slots):
            hit = (order == which * 128 + e) & (r == there(row))
            pack_list[n] = jnp.max(jnp.where(hit, word, -1.0)).astype(jnp.int32)
            n += 1

    info_ref[0:8] = a
    info_ref[8:16] = b
    info_ref[16:32] = c
    info_ref[32:40] = order
    extract(entries_of(info_ref, me_ref)[0], product_list)


def plan(me, spots, sends):
    smem = pl.BlockSpec(memory_space=pltpu.SMEM)
    vmem = pl.BlockSpec(memory_space=pltpu.VMEM)
    return pl.pallas_call(
        functools.partial(plan_kernel, sends),
        in_specs=[smem, vmem],
        out_specs=[smem, smem, vmem, vmem],
        out_shape=[
            jax.ShapeDtypeStruct((sum(n for n, *_ in sends),), jnp.int32),
            jax.ShapeDtypeStruct((LIST + 1,), jnp.int32),
            jax.ShapeDtypeStruct((40, 128), jnp.int32),
            jax.ShapeDtypeStruct((6, 128, 128), jnp.bfloat16),
        ],
        compiler_params=pltpu.CompilerParams(vmem_limit_bytes=16 << 20),
        name="plan",
    )(me, spots)


def pack_kernel(sizes, list_ref, *rest):
    near, packed, sems = rest[:3], rest[3:-1], rest[-1]
    places = [(i, e) for i, size in enumerate(sizes) for e in range(size)]
    for n, (i, e) in enumerate(places):
        word = list_ref[n]

        @pl.when(word >= 0)
        def _():
            fetch_block(word >> 4, word & 15, near, packed[i].at[e], sems.at[n])

    for n, (i, e) in enumerate(places):

        @pl.when(list_ref[n] >= 0)
        def _():
            pltpu.make_async_copy(near[0].at[0], packed[i].at[e], sems.at[n]).wait()


def pack(listing, near, sizes):
    size = near[0].shape[-1]
    return pl.pallas_call(
        functools.partial(pack_kernel, sizes),
        in_specs=[pl.BlockSpec(memory_space=pltpu.SMEM)]
        + [pl.BlockSpec(memory_space=pl.ANY)] * 3,
        out_specs=[pl.BlockSpec(memory_space=pltpu.VMEM)] * len(sizes),
        scratch_shapes=[pltpu.SemaphoreType.DMA((sum(sizes),))],
        out_shape=[jax.ShapeDtypeStruct((n, size, size), jnp.float32) for n in sizes],
        compiler_params=pltpu.CompilerParams(vmem_limit_bytes=16 << 20),
        name="pack",
    )(listing, *near)


def overflow_kernel(spots_ref, maps_ref, over_ref):
    held = positions(spots_ref, maps_ref)
    a = held[:8].astype(jnp.int32)
    turned = [held[8:40]] + [pltpu.roll(held[8:40], 128 - q, 1) for q in range(1, 16)]
    b = matmul(jnp.concatenate([x[:8] for x in turned]), maps_ref[0])
    b = b + matmul(jnp.concatenate([x[8:16] for x in turned]), maps_ref[1])
    b = b.astype(jnp.int32)
    c = matmul(jnp.concatenate([x[16:32] for x in turned]), maps_ref[2]).astype(jnp.int32)
    flags = [
        jnp.where(needed(a, b[q * 8 : q * 8 + 8], c[q * 16 : q * 16 + 16]), 1.0, 0.0)
        for q in range(16)
    ]
    alike = matmul(jnp.concatenate(flags), maps_ref[3])
    most = jnp.sum(alike[:8], axis=0, keepdims=True)
    for q in range(1, 16):
        most = jnp.maximum(most, jnp.sum(alike[q * 8 : q * 8 + 8], axis=0, keepdims=True))
    *_, way = lane_facts(most.shape)
    slots = jnp.where(way == 0, 128, jnp.where(way == 1, NEAR, FAR))
    over_ref[0] = jnp.max(jnp.where(most > slots.astype(jnp.float32), 1.0, 0.0)).astype(jnp.int32)


def overflow(spots, maps):
    vmem = pl.BlockSpec(memory_space=pltpu.VMEM)
    return pl.pallas_call(
        overflow_kernel,
        in_specs=[vmem] * 2,
        out_specs=pl.BlockSpec(memory_space=pltpu.SMEM),
        out_shape=jax.ShapeDtypeStruct((1,), jnp.int32),
        compiler_params=pltpu.CompilerParams(vmem_limit_bytes=16 << 20),
        cost_estimate=pl.CostEstimate(flops=10**9, bytes_accessed=10**5, transcendentals=0),
        name="overflow",
    )(spots, maps)


def halves(x):
    high = x.astype(jnp.bfloat16)
    return high, (x - high.astype(jnp.float32)).astype(jnp.bfloat16)


def block_product(a, b):
    a_high, a_low = halves(a)
    b_high, b_low = halves(b)
    dot = functools.partial(jnp.dot, preferred_element_type=jnp.float32)
    return dot(a_high, b_high) + (dot(a_high, b_low) + dot(a_low, b_high))


def extract(entries, list_ref):
    def more(state):
        n, word, left = state
        list_ref[n] = word.astype(jnp.int32)
        left = jnp.where(left == word, -1.0, left)
        return n + 1, jnp.max(left), left

    n, *_ = lax.while_loop(
        lambda state: state[1] >= 0, more, (jnp.int32(0), jnp.max(entries), entries)
    )
    list_ref[LIST] = n


def entries_of(info_ref, me_ref):
    row, column = me_ref[0], me_ref[1]
    b, c, order = info_ref[8:16], info_ref[16:32], info_ref[32:40]
    r, p, owner, way = lane_facts(b.shape)
    t = lax.broadcasted_iota(jnp.int32, b.shape, 0)
    rank = order & 127
    steps = ((owner >> 1) - (row >> 1)) & 3
    part = jnp.where(steps == 0, 0, jnp.where(steps == 3, 1, 2))
    sent = (way > 0) & (rank < jnp.where(way == 1, NEAR, FAR))
    along = ((p >> 1) - (column >> 1)) & 3
    beside = ((p ^ column) >> 3) & 1
    a_part = jnp.where(along == 0, 0, jnp.where(along == 3, 1, jnp.where(along == 1, 2, 3)))
    a_at = (a_part + 4 * ((p ^ column) & 1)) * 8 + beside * SA
    found = [[], []]
    for s in range(SA):
        lands = lands_at(info_ref[s : s + 1], b)
        c_slot = jnp.full(b.shape, -1, jnp.int32)
        for n in range(c.shape[0]):
            c_slot = jnp.where(lands == c[n : n + 1], n, c_slot)
        live = (c_slot >= 0) & (r == row)
        a_slot = a_at + s
        at_hand = jnp.where(
            way == 0,
            code(a_slot, part, (p & 1) * 8 + t, c_slot),
            code(a_slot, 2 + way, rank, c_slot),
        )
        elsewhere = code(a_slot, owner ^ row, (p & 1) * 8 + t, c_slot)
        found[0].append(jnp.where(live & ((way == 0) | sent), at_hand, -1).astype(jnp.float32))
        found[1].append(jnp.where(live & (way > 0) & ~sent, elsewhere, -1).astype(jnp.float32))
    return [jnp.concatenate(x) for x in found]


def multiply_listed(list_ref, a_refs, b_refs, acc, a_buf, b_buf, a_sem, b_sem, meanwhile):
    count = list_ref[LIST]

    def fetch(n):
        slot = n % AHEAD
        word = list_ref[n]
        fetch_a(word, a_refs, a_buf.at[slot], a_sem.at[slot])
        fetch_block(part_of(word), at_of(word), b_refs, b_buf.at[slot], b_sem.at[slot])

    for n in range(AHEAD):

        @pl.when(n < count)
        def _():
            fetch(n)

    meanwhile()

    def step(n, carry):
        slot = n % AHEAD
        pltpu.make_async_copy(a_refs[0].at[0], a_buf.at[slot], a_sem.at[slot]).wait()
        pltpu.make_async_copy(b_refs[0].at[0], b_buf.at[slot], b_sem.at[slot]).wait()
        acc[c_of(list_ref[n])] += block_product(a_buf[slot], b_buf[slot])

        @pl.when(n + AHEAD < count)
        def _():
            fetch(n + AHEAD)

        return carry

    lax.fori_loop(0, count, step, 0)


def all_kernel(parts, list_ref, *rest):
    a_refs, b_refs = rest[:A_PARTS], rest[A_PARTS:parts]
    out_ref, acc, c_sem, _, *buffers = rest[parts:]

    def meanwhile():
        acc[...] = jnp.zeros_like(acc)

    multiply_listed(list_ref, a_refs, b_refs, acc, *buffers, meanwhile)
    copy = pltpu.make_async_copy(acc, out_ref, c_sem.at[0])
    copy.start()
    copy.wait()


def add_listed(list_ref, a_refs, b_refs, total_ref, out_ref, acc, c_sem, stage, *buffers):
    count = list_ref[LIST]

    def touched(was, act):
        def step(n, carry):
            c = c_of(list_ref[n])

            @pl.when(stage[c] == was)
            def _():
                stage[c] = was + 1
                act(c)

            return carry

        lax.fori_loop(0, count, step, 0)

    def fetched(c):
        return pltpu.make_async_copy(total_ref.at[c], acc.at[c], c_sem.at[c])

    def stored(c):
        return pltpu.make_async_copy(acc.at[c], out_ref.at[c], c_sem.at[c])

    for c in range(acc.shape[0]):
        stage[c] = 0

    def meanwhile():
        touched(0, lambda c: fetched(c).start())
        touched(1, lambda c: fetched(c).wait())

    multiply_listed(list_ref, a_refs, b_refs, acc, *buffers, meanwhile)
    touched(2, lambda c: stored(c).start())
    touched(3, lambda c: stored(c).wait())


def rest_kernel(parts, me_ref, info_ref, *rest):
    a_refs, b_refs = rest[:A_PARTS], rest[A_PARTS:parts]
    total_ref, out_ref, rest_list, *buffers = rest[parts:]
    extract(entries_of(info_ref, me_ref)[1], rest_list)
    add_listed(rest_list, a_refs, b_refs, total_ref, out_ref, *buffers)


def products(kernel, leading, a_parts, b_parts, total, slots, own_list=False):
    size = a_parts[0].shape[-1]
    parts = len(a_parts) + len(b_parts)
    smem = pl.BlockSpec(memory_space=pltpu.SMEM)
    vmem = pl.BlockSpec(memory_space=pltpu.VMEM)
    hbm = pl.BlockSpec(memory_space=pltpu.HBM)
    operands = [*leading, *a_parts, *b_parts] + ([] if total is None else [total])
    return pl.pallas_call(
        functools.partial(kernel, parts),
        in_specs=[smem if x.ndim == 1 else vmem for x in leading]
        + [pl.BlockSpec(memory_space=pl.ANY)] * parts
        + ([] if total is None else [hbm]),
        out_specs=hbm,
        out_shape=jax.ShapeDtypeStruct((slots, size, size), jnp.float32),
        scratch_shapes=([pltpu.SMEM((LIST + 1,), jnp.int32)] if own_list else [])
        + [
            pltpu.VMEM((slots, size, size), jnp.float32),
            pltpu.SemaphoreType.DMA((slots,)),
            pltpu.SMEM((slots,), jnp.int32),
            pltpu.VMEM((AHEAD, size, size), jnp.float32),
            pltpu.VMEM((AHEAD, size, size), jnp.float32),
            pltpu.SemaphoreType.DMA((AHEAD,)),
            pltpu.SemaphoreType.DMA((AHEAD,)),
        ],
        input_output_aliases={} if total is None else {len(operands) - 1: 0},
        compiler_params=pltpu.CompilerParams(vmem_limit_bytes=VMEM_LIMIT),
        cost_estimate=pl.CostEstimate(
            flops=8 * 3 * 2 * size**3, bytes_accessed=24 * size * size * 4, transcendentals=0
        ),
        name="products",
    )(*operands)


def to_row(block, rows, there):
    return lax.ppermute(block, "row", [(i, there(i)) for i in range(rows)])


def on_z(i):
    return (i & 9) | ((i + 2) & 6)


def back_z(i):
    return (i & 9) | ((i - 2) & 6)


def moved(block, there, columns):
    return lax.ppermute(block, COL, [(i, there(i)) for i in range(columns)])


def pair_kernel(tile_ref, beside_ref, _, pair_ref, __, sems):
    n = tile_ref.shape[0]
    copies = [
        pltpu.make_async_copy(tile_ref, pair_ref.at[pl.ds(0, n)], sems.at[0]),
        pltpu.make_async_copy(beside_ref, pair_ref.at[pl.ds(n, n)], sems.at[1]),
    ]
    for copy in copies:
        copy.start()
    for copy in copies:
        copy.wait()


def paired(tile, beside, passing):
    n, size = tile.shape[0], tile.shape[-1]
    anywhere = pl.BlockSpec(memory_space=pl.ANY)
    return pl.pallas_call(
        pair_kernel,
        in_specs=[anywhere] * 3,
        out_specs=[pl.BlockSpec(memory_space=pltpu.VMEM), anywhere],
        out_shape=[
            jax.ShapeDtypeStruct((2 * n, size, size), tile.dtype),
            jax.ShapeDtypeStruct(passing.shape, passing.dtype),
        ],
        scratch_shapes=[pltpu.SemaphoreType.DMA((2,))],
        input_output_aliases={2: 1},
        compiler_params=pltpu.CompilerParams(vmem_limit_bytes=16 << 20),
        name="pair",
    )(tile, beside, passing)


def hold_kernel(*refs):
    pass


def held_for(arrays, later):
    anywhere = pl.BlockSpec(memory_space=pl.ANY)
    return pl.pallas_call(
        hold_kernel,
        in_specs=[anywhere] * (len(arrays) + len(later)),
        out_specs=[anywhere] * len(arrays),
        out_shape=[jax.ShapeDtypeStruct(x.shape, x.dtype) for x in arrays],
        input_output_aliases={i: i for i in range(len(arrays))},
        name="hold",
    )(*arrays, *later)


def among(held, bits, rows, columns):
    me = lax.axis_index("row") * columns + lax.axis_index(COL)
    group = jnp.zeros((2 ** len(bits),) + held.shape, held.dtype)
    for move in range(2 ** len(bits)):
        flip = sum(((move >> n) & 1) << bit for n, bit in enumerate(bits))
        got = held
        if move:
            pairs = [(i ^ flip, i) for i in range(rows * columns)]
            got = lax.ppermute(held, ("row", *COL), pairs)
        spot = sum((((me ^ flip) >> bit) & 1) << n for n, bit in enumerate(bits))
        group = lax.dynamic_update_index_in_dim(group, got, spot, 0)
    return group


def per_device(a_blocks, a_index, b_blocks, b_index, c_index):
    rows = lax.axis_size("row")
    columns = lax.axis_size(COL)
    row = lax.axis_index("row")
    me = jnp.stack([row, lax.axis_index(COL)])
    hold = columns // rows
    sa, sb, sc = a_blocks.shape[2], b_blocks.shape[3], c_index.shape[2]
    held = hold * sb
    size = a_blocks.shape[-1]

    own = b_blocks[0, 0].reshape(held, size, size)
    behind = to_row(own, rows, lambda i: (i + 2) % rows)
    ahead = to_row(own, rows, lambda i: (i - 2) % rows)
    near = [own, behind, ahead]

    blank = jnp.full((8 - sa,), -1, jnp.int32)
    mine = jnp.concatenate([a_index[0, 0], blank, b_index[0, 0].reshape(-1), c_index[0, 0]])
    spots = among(jnp.pad(mine, (0, 128 - mine.shape[0])), (5, 6), rows, columns)
    spots = among(spots, (1, 2), rows, columns)
    tile = a_blocks[0, 0]
    pair, spots = paired(tile, moved(tile, lambda i: i ^ 8, columns), spots)
    spots = among(spots, (3,), rows, columns)
    spots = among(spots, (4,), rows, columns)
    spots = among(spots, (0,), rows, columns).reshape(rows * columns, 128)
    a_behind = moved(pair, on_z, columns)
    a_ahead = moved(pair, back_z, columns)

    sends = [
        (FAR, 2, lambda i: (i + 2) & 7),
        (FAR, 3, lambda i: ((i + 2) & 7) ^ 1),
        (NEAR, 1, lambda i: i ^ 1),
    ]
    pack_list, product_list, info, maps = plan(me, spots, sends)
    packed = pack(pack_list, near, [n for n, *_ in sends])

    far_own, far_other, cross = [
        to_row(block, rows, there) for block, (*_, there) in zip(packed, sends)
    ]

    (a_far,) = held_for([moved(a_behind, on_z, columns)], [far_own, far_other, cross])
    a_mine = [pair, a_behind, a_ahead, a_far]
    a_parts = a_mine + [moved(block, lambda i: i ^ 1, columns) for block in a_mine]

    b_parts = near + [cross, far_own, far_other]
    total = products(all_kernel, [product_list], a_parts, b_parts, None, sc)

    trips = overflow(spots, maps)[0]

    def trip(state):
        done, total = state
        sent = jnp.where(done >= 0, own, 0)
        whole = [own] + [to_row(sent, rows, lambda i, n=n: i ^ n) for n in range(1, rows)]
        rest = products(rest_kernel, [me, info], a_parts, whole, total, sc, own_list=True)
        return done + 1, rest

    _, total = lax.while_loop(lambda state: state[0] < trips, trip, (jnp.int32(0), total))
    return total[None, None]


def solution(mesh):
    rows, columns = mesh.devices.shape
    mesh = Mesh(mesh.devices.reshape(rows, 2, columns // 4, 2), ("row", *COL))
    in_specs = (
        P("row", COL, None, None, None),
        P("row", COL, None),
        P("row", COL, None, None, None, None),
        P("row", COL, None, None),
        P("row", COL, None),
    )
    out_specs = P("row", COL, None, None, None)
    return jax.shard_map(
        per_device, mesh=mesh, in_specs=in_specs, out_specs=out_specs, check_vma=False
    )
```

```python
import functools

import jax
import jax.numpy as jnp
from jax import lax
from jax.experimental import pallas as pl
from jax.experimental.pallas import tpu as pltpu
from jax.sharding import Mesh
from jax.sharding import PartitionSpec as P

SA = 4
PK = 8
NBD = 8
NEAR = 6
FAR = 3
COL = ("x_lo", "z", "core")
VMEM_LIMIT = 16 << 20
A_PARTS = 8
LIST = 512
AHEAD = 8


def matmul(a, b):
    return jnp.dot(a.astype(jnp.bfloat16), b, preferred_element_type=jnp.float32)


def lands_at(a_line, b):
    meet = (a_line >= 0) & (b >= 0) & ((a_line & (PK - 1)) == (b >> 3))
    return jnp.where(meet, (a_line >> 3) * NBD + (b & (NBD - 1)), -2)


def needed(a, b, c):
    need = jnp.zeros(b.shape, jnp.bool_)
    for s in range(SA):
        lands = lands_at(a[s : s + 1], b)
        for n in range(c.shape[0]):
            need = need | (lands == c[n : n + 1])
    return need


def lane_facts(shape, axis=1):
    lane = lax.broadcasted_iota(jnp.int32, shape, axis)
    r, p = lane >> 4, lane & 15
    owner = p >> 1
    far = (((owner >> 1) - (r >> 1)) & 3) == 2
    way = ((owner ^ r) & 1) + jnp.where(far, 2, 0)
    return r, p, owner, way


def code(a_slot, part, at, c_slot):
    return ((a_slot * 16 + part) * 128 + at) * 16 + c_slot


def a_of(word):
    return word >> 15


def part_of(word):
    return (word >> 11) & 15


def at_of(word):
    return (word >> 4) & 127


def c_of(word):
    return word & 15


def fetch_a(word, a_refs, dst, sem):
    a = a_of(word)
    fetch_block(a >> 3, a & 7, a_refs, dst, sem)


def fetch_block(part, at, refs, dst, sem):
    for i, ref in enumerate(refs):

        def start(ref=ref):
            pltpu.make_async_copy(ref.at[at], dst, sem).start()

        if len(refs) == 1:
            start()
        else:
            pl.when(part == i)(start)


def make_maps(maps_ref):
    shape = maps_ref.shape[1:]
    lane = lax.broadcasted_iota(jnp.int32, shape, 1)
    down = lax.broadcasted_iota(jnp.int32, shape, 0)
    r, p, owner, way = lane_facts(shape)
    r_down, p_down, _, way_down = lane_facts(shape, 0)
    holder = (p_down == 0) & (r_down == owner)
    alike = (r == r_down) & (way == way_down)
    y, xh, xl, z, core = lane >> 5, (lane >> 4) & 1, (lane >> 3) & 1, (lane >> 1) & 3, lane & 1
    listed_at = (((core * 2 + xh) * 2 + xl) * 4 + z) * 4 + y
    for n, flags in enumerate(
        [
            holder & ((p & 1) == 0),
            holder & ((p & 1) == 1),
            (p_down == 0) & (r == r_down),
            alike,
            alike & (down < lane),
            down == listed_at,
        ]
    ):
        maps_ref[n] = jnp.where(flags, 1.0, 0.0).astype(jnp.bfloat16)


def positions(spots_ref, maps_ref):
    spots = spots_ref[...].astype(jnp.float32).astype(jnp.bfloat16)
    return lax.dot_general(
        spots, maps_ref[5], (((0,), (0,)), ((), ())), preferred_element_type=jnp.float32
    )


def plan_kernel(sends, me_ref, spots_ref, pack_list, info_ref, maps_ref):
    row, column = me_ref[0], me_ref[1]
    make_maps(maps_ref)
    held = positions(spots_ref, maps_ref)
    a = held[:8].astype(jnp.int32)
    turned = pltpu.roll(held[8:40], (128 - column) & 127, 1)
    b = matmul(turned[:8], maps_ref[0]) + matmul(turned[8:16], maps_ref[1])
    b = b.astype(jnp.int32)
    c = matmul(turned[16:32], maps_ref[2]).astype(jnp.int32)
    need = needed(a, b, c)

    r, p, owner, way = lane_facts(b.shape)
    t = lax.broadcasted_iota(jnp.int32, b.shape, 0)
    flags = jnp.where(need, 1.0, 0.0)
    alike = matmul(flags, maps_ref[3])
    upto = alike
    for step in (1, 2, 4):
        upto = upto + jnp.where(t >= step, pltpu.roll(upto, step, 0), 0.0)
    rank = (upto - alike + matmul(flags, maps_ref[4])).astype(jnp.int32)
    order = jnp.where(need, way * 128 + rank, -1)

    steps = ((owner >> 1) - (row >> 1)) & 3
    part = jnp.where(steps == 0, 0, jnp.where(steps == 3, 1, 2))
    word = (part * 16 + (p & 1) * 8 + t).astype(jnp.float32)
    n = 0
    for slots, which, there in sends:
        for e in range(slots):
            hit = (order == which * 128 + e) & (r == there(row))
            pack_list[n] = jnp.max(jnp.where(hit, word, -1.0)).astype(jnp.int32)
            n += 1

    info_ref[0:8] = a
    info_ref[8:16] = b
    info_ref[16:32] = c
    info_ref[32:40] = order


def plan(me, spots, sends):
    smem = pl.BlockSpec(memory_space=pltpu.SMEM)
    vmem = pl.BlockSpec(memory_space=pltpu.VMEM)
    return pl.pallas_call(
        functools.partial(plan_kernel, sends),
        in_specs=[smem, vmem],
        out_specs=[smem, vmem, vmem],
        out_shape=[
            jax.ShapeDtypeStruct((sum(n for n, *_ in sends),), jnp.int32),
            jax.ShapeDtypeStruct((40, 128), jnp.int32),
            jax.ShapeDtypeStruct((6, 128, 128), jnp.bfloat16),
        ],
        compiler_params=pltpu.CompilerParams(vmem_limit_bytes=16 << 20),
        name="plan",
    )(me, spots)


def pack_kernel(sizes, list_ref, *rest):
    near, packed, sems = rest[:3], rest[3:-1], rest[-1]
    places = [(i, e) for i, size in enumerate(sizes) for e in range(size)]
    for n, (i, e) in enumerate(places):
        word = list_ref[n]

        @pl.when(word >= 0)
        def _():
            fetch_block(word >> 4, word & 15, near, packed[i].at[e], sems.at[n])

    for n, (i, e) in enumerate(places):

        @pl.when(list_ref[n] >= 0)
        def _():
            pltpu.make_async_copy(near[0].at[0], packed[i].at[e], sems.at[n]).wait()


def pack(listing, near, sizes):
    size = near[0].shape[-1]
    return pl.pallas_call(
        functools.partial(pack_kernel, sizes),
        in_specs=[pl.BlockSpec(memory_space=pltpu.SMEM)]
        + [pl.BlockSpec(memory_space=pl.ANY)] * 3,
        out_specs=[pl.BlockSpec(memory_space=pltpu.VMEM)] * len(sizes),
        scratch_shapes=[pltpu.SemaphoreType.DMA((sum(sizes),))],
        out_shape=[jax.ShapeDtypeStruct((n, size, size), jnp.float32) for n in sizes],
        compiler_params=pltpu.CompilerParams(vmem_limit_bytes=16 << 20),
        name="pack",
    )(listing, *near)


def overflow_kernel(me_ref, info_ref, spots_ref, maps_ref, over_ref, product_list):
    extract(entries_of(info_ref, me_ref)[0], product_list)
    held = positions(spots_ref, maps_ref)
    a = held[:8].astype(jnp.int32)
    turned = [held[8:40]] + [pltpu.roll(held[8:40], 128 - q, 1) for q in range(1, 16)]
    b = matmul(jnp.concatenate([x[:8] for x in turned]), maps_ref[0])
    b = b + matmul(jnp.concatenate([x[8:16] for x in turned]), maps_ref[1])
    b = b.astype(jnp.int32)
    c = matmul(jnp.concatenate([x[16:32] for x in turned]), maps_ref[2]).astype(jnp.int32)
    flags = [
        jnp.where(needed(a, b[q * 8 : q * 8 + 8], c[q * 16 : q * 16 + 16]), 1.0, 0.0)
        for q in range(16)
    ]
    alike = matmul(jnp.concatenate(flags), maps_ref[3])
    most = jnp.sum(alike[:8], axis=0, keepdims=True)
    for q in range(1, 16):
        most = jnp.maximum(most, jnp.sum(alike[q * 8 : q * 8 + 8], axis=0, keepdims=True))
    *_, way = lane_facts(most.shape)
    slots = jnp.where(way == 0, 128, jnp.where(way == 1, NEAR, FAR))
    over_ref[0] = jnp.max(jnp.where(most > slots.astype(jnp.float32), 1.0, 0.0)).astype(jnp.int32)


def overflow(me, info, spots, maps):
    smem = pl.BlockSpec(memory_space=pltpu.SMEM)
    vmem = pl.BlockSpec(memory_space=pltpu.VMEM)
    return pl.pallas_call(
        overflow_kernel,
        in_specs=[smem, vmem, vmem, vmem],
        out_specs=[smem, smem],
        out_shape=[
            jax.ShapeDtypeStruct((1,), jnp.int32),
            jax.ShapeDtypeStruct((LIST + 1,), jnp.int32),
        ],
        compiler_params=pltpu.CompilerParams(vmem_limit_bytes=16 << 20),
        cost_estimate=pl.CostEstimate(flops=10**9, bytes_accessed=10**5, transcendentals=0),
        name="overflow",
    )(me, info, spots, maps)


def halves(x):
    high = x.astype(jnp.bfloat16)
    return high, (x - high.astype(jnp.float32)).astype(jnp.bfloat16)


def block_product(a, b):
    a_high, a_low = halves(a)
    b_high, b_low = halves(b)
    dot = functools.partial(jnp.dot, preferred_element_type=jnp.float32)
    return dot(a_high, b_high) + (dot(a_high, b_low) + dot(a_low, b_high))


def extract(entries, list_ref):
    def more(state):
        n, word, left = state
        list_ref[n] = word.astype(jnp.int32)
        left = jnp.where(left == word, -1.0, left)
        return n + 1, jnp.max(left), left

    n, *_ = lax.while_loop(
        lambda state: state[1] >= 0, more, (jnp.int32(0), jnp.max(entries), entries)
    )
    list_ref[LIST] = n


def entries_of(info_ref, me_ref):
    row, column = me_ref[0], me_ref[1]
    b, c, order = info_ref[8:16], info_ref[16:32], info_ref[32:40]
    r, p, owner, way = lane_facts(b.shape)
    t = lax.broadcasted_iota(jnp.int32, b.shape, 0)
    rank = order & 127
    steps = ((owner >> 1) - (row >> 1)) & 3
    part = jnp.where(steps == 0, 0, jnp.where(steps == 3, 1, 2))
    sent = (way > 0) & (rank < jnp.where(way == 1, NEAR, FAR))
    along = ((p >> 1) - (column >> 1)) & 3
    beside = ((p ^ column) >> 3) & 1
    a_part = jnp.where(along == 0, 0, jnp.where(along == 3, 1, jnp.where(along == 1, 2, 3)))
    a_at = (a_part + 4 * ((p ^ column) & 1)) * 8 + beside * SA
    found = [[], []]
    for s in range(SA):
        lands = lands_at(info_ref[s : s + 1], b)
        c_slot = jnp.full(b.shape, -1, jnp.int32)
        for n in range(c.shape[0]):
            c_slot = jnp.where(lands == c[n : n + 1], n, c_slot)
        live = (c_slot >= 0) & (r == row)
        a_slot = a_at + s
        at_hand = jnp.where(
            way == 0,
            code(a_slot, part, (p & 1) * 8 + t, c_slot),
            code(a_slot, 2 + way, rank, c_slot),
        )
        elsewhere = code(a_slot, owner ^ row, (p & 1) * 8 + t, c_slot)
        found[0].append(jnp.where(live & ((way == 0) | sent), at_hand, -1).astype(jnp.float32))
        found[1].append(jnp.where(live & (way > 0) & ~sent, elsewhere, -1).astype(jnp.float32))
    return [jnp.concatenate(x) for x in found]


def multiply_listed(list_ref, a_refs, b_refs, acc, a_buf, b_buf, a_sem, b_sem, meanwhile):
    count = list_ref[LIST]

    def fetch(n):
        slot = n % AHEAD
        word = list_ref[n]
        fetch_a(word, a_refs, a_buf.at[slot], a_sem.at[slot])
        fetch_block(part_of(word), at_of(word), b_refs, b_buf.at[slot], b_sem.at[slot])

    for n in range(AHEAD):

        @pl.when(n < count)
        def _():
            fetch(n)

    meanwhile()

    def step(n, carry):
        slot = n % AHEAD
        pltpu.make_async_copy(a_refs[0].at[0], a_buf.at[slot], a_sem.at[slot]).wait()
        pltpu.make_async_copy(b_refs[0].at[0], b_buf.at[slot], b_sem.at[slot]).wait()
        acc[c_of(list_ref[n])] += block_product(a_buf[slot], b_buf[slot])

        @pl.when(n + AHEAD < count)
        def _():
            fetch(n + AHEAD)

        return carry

    lax.fori_loop(0, count, step, 0)


def all_kernel(parts, list_ref, *rest):
    a_refs, b_refs = rest[:A_PARTS], rest[A_PARTS:parts]
    out_ref, acc, c_sem, touched, *buffers = rest[parts:]
    slots = acc.shape[0]

    def stored(c):
        return pltpu.make_async_copy(acc.at[c], out_ref.at[c], c_sem.at[c])

    def meanwhile():
        for c in range(slots):
            touched[c] = 0

        def mark(n, carry):
            touched[c_of(list_ref[n])] = 1
            return carry

        lax.fori_loop(0, list_ref[LIST], mark, 0)
        acc[...] = jnp.zeros_like(acc)
        for c in range(slots):
            pl.when(touched[c] == 0)(lambda c=c: stored(c).start())

    multiply_listed(list_ref, a_refs, b_refs, acc, *buffers, meanwhile)
    for c in range(slots):
        pl.when(touched[c] == 1)(lambda c=c: stored(c).start())
    for c in range(slots):
        stored(c).wait()


def add_listed(list_ref, a_refs, b_refs, total_ref, out_ref, acc, c_sem, stage, *buffers):
    count = list_ref[LIST]

    def touched(was, act):
        def step(n, carry):
            c = c_of(list_ref[n])

            @pl.when(stage[c] == was)
            def _():
                stage[c] = was + 1
                act(c)

            return carry

        lax.fori_loop(0, count, step, 0)

    def fetched(c):
        return pltpu.make_async_copy(total_ref.at[c], acc.at[c], c_sem.at[c])

    def stored(c):
        return pltpu.make_async_copy(acc.at[c], out_ref.at[c], c_sem.at[c])

    for c in range(acc.shape[0]):
        stage[c] = 0

    def meanwhile():
        touched(0, lambda c: fetched(c).start())
        touched(1, lambda c: fetched(c).wait())

    multiply_listed(list_ref, a_refs, b_refs, acc, *buffers, meanwhile)
    touched(2, lambda c: stored(c).start())
    touched(3, lambda c: stored(c).wait())


def rest_kernel(parts, me_ref, info_ref, *rest):
    a_refs, b_refs = rest[:A_PARTS], rest[A_PARTS:parts]
    total_ref, out_ref, rest_list, *buffers = rest[parts:]
    extract(entries_of(info_ref, me_ref)[1], rest_list)
    add_listed(rest_list, a_refs, b_refs, total_ref, out_ref, *buffers)


def products(kernel, leading, a_parts, b_parts, total, slots, own_list=False):
    size = a_parts[0].shape[-1]
    parts = len(a_parts) + len(b_parts)
    smem = pl.BlockSpec(memory_space=pltpu.SMEM)
    vmem = pl.BlockSpec(memory_space=pltpu.VMEM)
    hbm = pl.BlockSpec(memory_space=pltpu.HBM)
    operands = [*leading, *a_parts, *b_parts] + ([] if total is None else [total])
    return pl.pallas_call(
        functools.partial(kernel, parts),
        in_specs=[smem if x.ndim == 1 else vmem for x in leading]
        + [pl.BlockSpec(memory_space=pl.ANY)] * parts
        + ([] if total is None else [hbm]),
        out_specs=hbm,
        out_shape=jax.ShapeDtypeStruct((slots, size, size), jnp.float32),
        scratch_shapes=([pltpu.SMEM((LIST + 1,), jnp.int32)] if own_list else [])
        + [
            pltpu.VMEM((slots, size, size), jnp.float32),
            pltpu.SemaphoreType.DMA((slots,)),
            pltpu.SMEM((slots,), jnp.int32),
            pltpu.VMEM((AHEAD, size, size), jnp.float32),
            pltpu.VMEM((AHEAD, size, size), jnp.float32),
            pltpu.SemaphoreType.DMA((AHEAD,)),
            pltpu.SemaphoreType.DMA((AHEAD,)),
        ],
        input_output_aliases={} if total is None else {len(operands) - 1: 0},
        compiler_params=pltpu.CompilerParams(vmem_limit_bytes=VMEM_LIMIT),
        cost_estimate=pl.CostEstimate(
            flops=8 * 3 * 2 * size**3, bytes_accessed=24 * size * size * 4, transcendentals=0
        ),
        name="products",
    )(*operands)


def to_row(block, rows, there):
    return lax.ppermute(block, "row", [(i, there(i)) for i in range(rows)])


def on_z(i):
    return (i & 9) | ((i + 2) & 6)


def back_z(i):
    return (i & 9) | ((i - 2) & 6)


def moved(block, there, columns):
    return lax.ppermute(block, COL, [(i, there(i)) for i in range(columns)])


def pair_kernel(tile_ref, beside_ref, _, pair_ref, __, sems):
    n = tile_ref.shape[0]
    copies = [
        pltpu.make_async_copy(tile_ref, pair_ref.at[pl.ds(0, n)], sems.at[0]),
        pltpu.make_async_copy(beside_ref, pair_ref.at[pl.ds(n, n)], sems.at[1]),
    ]
    for copy in copies:
        copy.start()
    for copy in copies:
        copy.wait()


def paired(tile, beside, passing):
    n, size = tile.shape[0], tile.shape[-1]
    anywhere = pl.BlockSpec(memory_space=pl.ANY)
    return pl.pallas_call(
        pair_kernel,
        in_specs=[anywhere] * 3,
        out_specs=[pl.BlockSpec(memory_space=pltpu.VMEM), anywhere],
        out_shape=[
            jax.ShapeDtypeStruct((2 * n, size, size), tile.dtype),
            jax.ShapeDtypeStruct(passing.shape, passing.dtype),
        ],
        scratch_shapes=[pltpu.SemaphoreType.DMA((2,))],
        input_output_aliases={2: 1},
        compiler_params=pltpu.CompilerParams(vmem_limit_bytes=16 << 20),
        name="pair",
    )(tile, beside, passing)


def hold_kernel(*refs):
    pass


def held_for(arrays, later):
    anywhere = pl.BlockSpec(memory_space=pl.ANY)
    return pl.pallas_call(
        hold_kernel,
        in_specs=[anywhere] * (len(arrays) + len(later)),
        out_specs=[anywhere] * len(arrays),
        out_shape=[jax.ShapeDtypeStruct(x.shape, x.dtype) for x in arrays],
        input_output_aliases={i: i for i in range(len(arrays))},
        name="hold",
    )(*arrays, *later)


def among(held, bits, rows, columns):
    me = lax.axis_index("row") * columns + lax.axis_index(COL)
    group = jnp.zeros((2 ** len(bits),) + held.shape, held.dtype)
    for move in range(2 ** len(bits)):
        flip = sum(((move >> n) & 1) << bit for n, bit in enumerate(bits))
        got = held
        if move:
            pairs = [(i ^ flip, i) for i in range(rows * columns)]
            got = lax.ppermute(held, ("row", *COL), pairs)
        spot = sum((((me ^ flip) >> bit) & 1) << n for n, bit in enumerate(bits))
        group = lax.dynamic_update_index_in_dim(group, got, spot, 0)
    return group


def per_device(a_blocks, a_index, b_blocks, b_index, c_index):
    rows = lax.axis_size("row")
    columns = lax.axis_size(COL)
    row = lax.axis_index("row")
    me = jnp.stack([row, lax.axis_index(COL)])
    hold = columns // rows
    sa, sb, sc = a_blocks.shape[2], b_blocks.shape[3], c_index.shape[2]
    held = hold * sb
    size = a_blocks.shape[-1]

    own = b_blocks[0, 0].reshape(held, size, size)
    behind = to_row(own, rows, lambda i: (i + 2) % rows)
    ahead = to_row(own, rows, lambda i: (i - 2) % rows)
    near = [own, behind, ahead]

    blank = jnp.full((8 - sa,), -1, jnp.int32)
    mine = jnp.concatenate([a_index[0, 0], blank, b_index[0, 0].reshape(-1), c_index[0, 0]])
    spots = among(jnp.pad(mine, (0, 128 - mine.shape[0])), (5, 6), rows, columns)
    spots = among(spots, (1, 2), rows, columns)
    tile = a_blocks[0, 0]
    pair, spots = paired(tile, moved(tile, lambda i: i ^ 8, columns), spots)
    spots = among(spots, (3,), rows, columns)
    spots = among(spots, (4,), rows, columns)
    spots = among(spots, (0,), rows, columns).reshape(rows * columns, 128)
    a_behind = moved(pair, on_z, columns)
    a_ahead = moved(pair, back_z, columns)

    sends = [
        (FAR, 2, lambda i: (i - 2) & 7),
        (FAR, 3, lambda i: ((i + 2) & 7) ^ 1),
        (NEAR, 1, lambda i: i ^ 1),
    ]
    pack_list, info, maps = plan(me, spots, sends)
    packed = pack(pack_list, near, [n for n, *_ in sends])

    far_own, far_other, cross = [
        to_row(block, rows, there) for block, (*_, there) in zip(packed, sends)
    ]

    over, product_list = overflow(me, info, spots, maps)
    (a_behind,) = held_for([a_behind], [info])
    a_far = moved(a_behind, on_z, columns)
    (a_far,) = held_for([a_far], [far_own, far_other, cross, over])
    a_mine = [pair, a_behind, a_ahead, a_far]
    a_parts = a_mine + [moved(block, lambda i: i ^ 1, columns) for block in a_mine]

    b_parts = near + [cross, far_own, far_other]
    total = products(all_kernel, [product_list], a_parts, b_parts, None, sc)

    trips = over[0]

    def trip(state):
        done, total = state
        sent = jnp.where(done >= 0, own, 0)
        whole = [own] + [to_row(sent, rows, lambda i, n=n: i ^ n) for n in range(1, rows)]
        rest = products(rest_kernel, [me, info], a_parts, whole, total, sc, own_list=True)
        return done + 1, rest

    _, total = lax.while_loop(lambda state: state[0] < trips, trip, (jnp.int32(0), total))
    return total[None, None]


def solution(mesh):
    rows, columns = mesh.devices.shape
    mesh = Mesh(mesh.devices.reshape(rows, 2, columns // 4, 2), ("row", *COL))
    in_specs = (
        P("row", COL, None, None, None),
        P("row", COL, None),
        P("row", COL, None, None, None, None),
        P("row", COL, None, None),
        P("row", COL, None),
    )
    out_specs = P("row", COL, None, None, None)
    return jax.shard_map(
        per_device, mesh=mesh, in_specs=in_specs, out_specs=out_specs, check_vma=False
    )
```

```python
import functools

import jax
import jax.numpy as jnp
from jax import lax
from jax.experimental import pallas as pl
from jax.experimental.pallas import tpu as pltpu
from jax.sharding import Mesh
from jax.sharding import PartitionSpec as P

SA = 4
PK = 8
NBD = 8
NEAR = 6
FAR = 3
COL = ("x_lo", "z", "core")
VMEM_LIMIT = 8 << 20
A_PARTS = 8
LIST = 512
AHEAD = 8


def matmul(a, b):
    return jnp.dot(a.astype(jnp.bfloat16), b, preferred_element_type=jnp.float32)


def lands_at(a_line, b):
    meet = (a_line >= 0) & (b >= 0) & ((a_line & (PK - 1)) == (b >> 3))
    return jnp.where(meet, (a_line >> 3) * NBD + (b & (NBD - 1)), -2)


def needed(a, b, c):
    need = jnp.zeros(b.shape, jnp.bool_)
    for s in range(SA):
        lands = lands_at(a[s : s + 1], b)
        for n in range(c.shape[0]):
            need = need | (lands == c[n : n + 1])
    return need


def lane_facts(shape, axis=1):
    lane = lax.broadcasted_iota(jnp.int32, shape, axis)
    r, p = lane >> 4, lane & 15
    owner = p >> 1
    far = (((owner >> 1) - (r >> 1)) & 3) == 2
    way = ((owner ^ r) & 1) + jnp.where(far, 2, 0)
    return r, p, owner, way


def code(a_slot, part, at, c_slot):
    return ((a_slot * 16 + part) * 128 + at) * 16 + c_slot


def a_of(word):
    return word >> 15


def part_of(word):
    return (word >> 11) & 15


def at_of(word):
    return (word >> 4) & 127


def c_of(word):
    return word & 15


def fetch_a(word, a_refs, dst, sem):
    a = a_of(word)
    fetch_block(a >> 3, a & 7, a_refs, dst, sem)


def fetch_block(part, at, refs, dst, sem):
    for i, ref in enumerate(refs):

        def start(ref=ref):
            pltpu.make_async_copy(ref.at[at], dst, sem).start()

        if len(refs) == 1:
            start()
        else:
            pl.when(part == i)(start)


def make_maps(maps_ref):
    shape = maps_ref.shape[1:]
    lane = lax.broadcasted_iota(jnp.int32, shape, 1)
    down = lax.broadcasted_iota(jnp.int32, shape, 0)
    r, p, owner, way = lane_facts(shape)
    r_down, p_down, _, way_down = lane_facts(shape, 0)
    holder = (p_down == 0) & (r_down == owner)
    alike = (r == r_down) & (way == way_down)
    y, xh, xl, z, core = lane >> 5, (lane >> 4) & 1, (lane >> 3) & 1, (lane >> 1) & 3, lane & 1
    listed_at = (((core * 2 + xh) * 2 + xl) * 4 + z) * 4 + y
    for n, flags in enumerate(
        [
            holder & ((p & 1) == 0),
            holder & ((p & 1) == 1),
            (p_down == 0) & (r == r_down),
            alike,
            alike & (down < lane),
            down == listed_at,
        ]
    ):
        maps_ref[n] = jnp.where(flags, 1.0, 0.0).astype(jnp.bfloat16)


def positions(spots_ref, maps_ref):
    spots = spots_ref[...].astype(jnp.float32).astype(jnp.bfloat16)
    return lax.dot_general(
        spots, maps_ref[5], (((0,), (0,)), ((), ())), preferred_element_type=jnp.float32
    )


def plan_kernel(sends, me_ref, spots_ref, pack_list, info_ref, maps_ref):
    row, column = me_ref[0], me_ref[1]
    make_maps(maps_ref)
    held = positions(spots_ref, maps_ref)
    a = held[:8].astype(jnp.int32)
    turned = pltpu.roll(held[8:40], (128 - column) & 127, 1)
    b = matmul(turned[:8], maps_ref[0]) + matmul(turned[8:16], maps_ref[1])
    b = b.astype(jnp.int32)
    c = matmul(turned[16:32], maps_ref[2]).astype(jnp.int32)
    need = needed(a, b, c)

    r, p, owner, way = lane_facts(b.shape)
    t = lax.broadcasted_iota(jnp.int32, b.shape, 0)
    flags = jnp.where(need, 1.0, 0.0)
    alike = matmul(flags, maps_ref[3])
    upto = alike
    for step in (1, 2, 4):
        upto = upto + jnp.where(t >= step, pltpu.roll(upto, step, 0), 0.0)
    rank = (upto - alike + matmul(flags, maps_ref[4])).astype(jnp.int32)
    order = jnp.where(need, way * 128 + rank, -1)

    steps = ((owner >> 1) - (row >> 1)) & 3
    part = jnp.where(steps == 0, 0, jnp.where(steps == 3, 1, 2))
    word = (part * 16 + (p & 1) * 8 + t).astype(jnp.float32)
    n = 0
    for slots, which, there in sends:
        for e in range(slots):
            hit = (order == which * 128 + e) & (r == there(row))
            pack_list[n] = jnp.max(jnp.where(hit, word, -1.0)).astype(jnp.int32)
            n += 1

    info_ref[0:8] = a
    info_ref[8:16] = b
    info_ref[16:32] = c
    info_ref[32:40] = order


def plan(me, spots, sends):
    smem = pl.BlockSpec(memory_space=pltpu.SMEM)
    vmem = pl.BlockSpec(memory_space=pltpu.VMEM)
    return pl.pallas_call(
        functools.partial(plan_kernel, sends),
        in_specs=[smem, vmem],
        out_specs=[smem, vmem, vmem],
        out_shape=[
            jax.ShapeDtypeStruct((sum(n for n, *_ in sends),), jnp.int32),
            jax.ShapeDtypeStruct((40, 128), jnp.int32),
            jax.ShapeDtypeStruct((6, 128, 128), jnp.bfloat16),
        ],
        compiler_params=pltpu.CompilerParams(vmem_limit_bytes=4 << 20),
        name="plan",
    )(me, spots)


def pack_kernel(sizes, list_ref, *rest):
    near, packed, sems = rest[:3], rest[3:-1], rest[-1]
    places = [(i, e) for i, size in enumerate(sizes) for e in range(size)]
    for n, (i, e) in enumerate(places):
        word = list_ref[n]

        @pl.when(word >= 0)
        def _():
            fetch_block(word >> 4, word & 15, near, packed[i].at[e], sems.at[n])

    for n, (i, e) in enumerate(places):

        @pl.when(list_ref[n] >= 0)
        def _():
            pltpu.make_async_copy(near[0].at[0], packed[i].at[e], sems.at[n]).wait()


def pack(listing, near, sizes):
    size = near[0].shape[-1]
    return pl.pallas_call(
        functools.partial(pack_kernel, sizes),
        in_specs=[pl.BlockSpec(memory_space=pltpu.SMEM)]
        + [pl.BlockSpec(memory_space=pl.ANY)] * 3,
        out_specs=[pl.BlockSpec(memory_space=pltpu.VMEM)] * len(sizes),
        scratch_shapes=[pltpu.SemaphoreType.DMA((sum(sizes),))],
        out_shape=[jax.ShapeDtypeStruct((n, size, size), jnp.float32) for n in sizes],
        compiler_params=pltpu.CompilerParams(vmem_limit_bytes=4 << 20),
        name="pack",
    )(listing, *near)


def overflow_kernel(me_ref, info_ref, spots_ref, maps_ref, over_ref, product_list):
    extract(entries_of(info_ref, me_ref)[0], product_list)
    held = positions(spots_ref, maps_ref)
    a = held[:8].astype(jnp.int32)
    turned = [held[8:40]] + [pltpu.roll(held[8:40], 128 - q, 1) for q in range(1, 16)]
    b = matmul(jnp.concatenate([x[:8] for x in turned]), maps_ref[0])
    b = b + matmul(jnp.concatenate([x[8:16] for x in turned]), maps_ref[1])
    b = b.astype(jnp.int32)
    c = matmul(jnp.concatenate([x[16:32] for x in turned]), maps_ref[2]).astype(jnp.int32)
    flags = [
        jnp.where(needed(a, b[q * 8 : q * 8 + 8], c[q * 16 : q * 16 + 16]), 1.0, 0.0)
        for q in range(16)
    ]
    alike = matmul(jnp.concatenate(flags), maps_ref[3])
    most = jnp.sum(alike[:8], axis=0, keepdims=True)
    for q in range(1, 16):
        most = jnp.maximum(most, jnp.sum(alike[q * 8 : q * 8 + 8], axis=0, keepdims=True))
    *_, way = lane_facts(most.shape)
    slots = jnp.where(way == 0, 128, jnp.where(way == 1, NEAR, FAR))
    over_ref[0] = jnp.max(jnp.where(most > slots.astype(jnp.float32), 1.0, 0.0)).astype(jnp.int32)


def overflow(me, info, spots, maps):
    smem = pl.BlockSpec(memory_space=pltpu.SMEM)
    vmem = pl.BlockSpec(memory_space=pltpu.VMEM)
    return pl.pallas_call(
        overflow_kernel,
        in_specs=[smem, vmem, vmem, vmem],
        out_specs=[smem, smem],
        out_shape=[
            jax.ShapeDtypeStruct((1,), jnp.int32),
            jax.ShapeDtypeStruct((LIST + 1,), jnp.int32),
        ],
        compiler_params=pltpu.CompilerParams(vmem_limit_bytes=4 << 20),
        cost_estimate=pl.CostEstimate(flops=10**9, bytes_accessed=10**5, transcendentals=0),
        name="overflow",
    )(me, info, spots, maps)


def halves(x):
    high = x.astype(jnp.bfloat16)
    return high, (x - high.astype(jnp.float32)).astype(jnp.bfloat16)


def block_product(a, b):
    a_high, a_low = halves(a)
    b_high, b_low = halves(b)
    dot = functools.partial(jnp.dot, preferred_element_type=jnp.float32)
    return dot(a_high, b_high) + (dot(a_high, b_low) + dot(a_low, b_high))


def extract(entries, list_ref):
    def more(state):
        n, word, left = state
        list_ref[n] = word.astype(jnp.int32)
        left = jnp.where(left == word, -1.0, left)
        return n + 1, jnp.max(left), left

    n, *_ = lax.while_loop(
        lambda state: state[1] >= 0, more, (jnp.int32(0), jnp.max(entries), entries)
    )
    list_ref[LIST] = n


def entries_of(info_ref, me_ref):
    row, column = me_ref[0], me_ref[1]
    b, c, order = info_ref[8:16], info_ref[16:32], info_ref[32:40]
    r, p, owner, way = lane_facts(b.shape)
    t = lax.broadcasted_iota(jnp.int32, b.shape, 0)
    rank = order & 127
    steps = ((owner >> 1) - (row >> 1)) & 3
    part = jnp.where(steps == 0, 0, jnp.where(steps == 3, 1, 2))
    sent = (way > 0) & (rank < jnp.where(way == 1, NEAR, FAR))
    along = ((p >> 1) - (column >> 1)) & 3
    beside = ((p ^ column) >> 3) & 1
    a_part = jnp.where(along == 0, 0, jnp.where(along == 3, 1, jnp.where(along == 1, 2, 3)))
    a_at = (a_part + 4 * ((p ^ column) & 1)) * 8 + beside * SA
    found = [[], []]
    for s in range(SA):
        lands = lands_at(info_ref[s : s + 1], b)
        c_slot = jnp.full(b.shape, -1, jnp.int32)
        for n in range(c.shape[0]):
            c_slot = jnp.where(lands == c[n : n + 1], n, c_slot)
        live = (c_slot >= 0) & (r == row)
        a_slot = a_at + s
        at_hand = jnp.where(
            way == 0,
            code(a_slot, part, (p & 1) * 8 + t, c_slot),
            code(a_slot, 2 + way, rank, c_slot),
        )
        elsewhere = code(a_slot, owner ^ row, (p & 1) * 8 + t, c_slot)
        found[0].append(jnp.where(live & ((way == 0) | sent), at_hand, -1).astype(jnp.float32))
        found[1].append(jnp.where(live & (way > 0) & ~sent, elsewhere, -1).astype(jnp.float32))
    return [jnp.concatenate(x) for x in found]


def multiply_listed(list_ref, a_refs, b_refs, acc, a_buf, b_buf, a_sem, b_sem, meanwhile):
    count = list_ref[LIST]

    def fetch(n):
        slot = n % AHEAD
        word = list_ref[n]
        fetch_a(word, a_refs, a_buf.at[slot], a_sem.at[slot])
        fetch_block(part_of(word), at_of(word), b_refs, b_buf.at[slot], b_sem.at[slot])

    for n in range(AHEAD):

        @pl.when(n < count)
        def _():
            fetch(n)

    meanwhile()

    def step(n, carry):
        slot = n % AHEAD
        pltpu.make_async_copy(a_refs[0].at[0], a_buf.at[slot], a_sem.at[slot]).wait()
        pltpu.make_async_copy(b_refs[0].at[0], b_buf.at[slot], b_sem.at[slot]).wait()
        acc[c_of(list_ref[n])] += block_product(a_buf[slot], b_buf[slot])

        @pl.when(n + AHEAD < count)
        def _():
            fetch(n + AHEAD)

        return carry

    lax.fori_loop(0, count, step, 0)


def all_kernel(parts, list_ref, *rest):
    a_refs, b_refs = rest[:A_PARTS], rest[A_PARTS:parts]
    out_ref, acc, c_sem, touched, *buffers = rest[parts:]
    slots = acc.shape[0]

    def stored(c):
        return pltpu.make_async_copy(acc.at[c], out_ref.at[c], c_sem.at[c])

    def meanwhile():
        for c in range(slots):
            touched[c] = 0

        def mark(n, carry):
            touched[c_of(list_ref[n])] = 1
            return carry

        lax.fori_loop(0, list_ref[LIST], mark, 0)
        acc[...] = jnp.zeros_like(acc)
        for c in range(slots):
            pl.when(touched[c] == 0)(lambda c=c: stored(c).start())

    multiply_listed(list_ref, a_refs, b_refs, acc, *buffers, meanwhile)
    for c in range(slots):
        pl.when(touched[c] == 1)(lambda c=c: stored(c).start())
    for c in range(slots):
        stored(c).wait()


def add_listed(list_ref, a_refs, b_refs, total_ref, out_ref, acc, c_sem, stage, *buffers):
    count = list_ref[LIST]

    def touched(was, act):
        def step(n, carry):
            c = c_of(list_ref[n])

            @pl.when(stage[c] == was)
            def _():
                stage[c] = was + 1
                act(c)

            return carry

        lax.fori_loop(0, count, step, 0)

    def fetched(c):
        return pltpu.make_async_copy(total_ref.at[c], acc.at[c], c_sem.at[c])

    def stored(c):
        return pltpu.make_async_copy(acc.at[c], out_ref.at[c], c_sem.at[c])

    for c in range(acc.shape[0]):
        stage[c] = 0

    def meanwhile():
        touched(0, lambda c: fetched(c).start())
        touched(1, lambda c: fetched(c).wait())

    multiply_listed(list_ref, a_refs, b_refs, acc, *buffers, meanwhile)
    touched(2, lambda c: stored(c).start())
    touched(3, lambda c: stored(c).wait())


def rest_kernel(parts, me_ref, info_ref, *rest):
    a_refs, b_refs = rest[:A_PARTS], rest[A_PARTS:parts]
    total_ref, out_ref, rest_list, *buffers = rest[parts:]
    extract(entries_of(info_ref, me_ref)[1], rest_list)
    add_listed(rest_list, a_refs, b_refs, total_ref, out_ref, *buffers)


def products(kernel, leading, a_parts, b_parts, total, slots, own_list=False):
    size = a_parts[0].shape[-1]
    parts = len(a_parts) + len(b_parts)
    smem = pl.BlockSpec(memory_space=pltpu.SMEM)
    vmem = pl.BlockSpec(memory_space=pltpu.VMEM)
    hbm = pl.BlockSpec(memory_space=pltpu.HBM)
    operands = [*leading, *a_parts, *b_parts] + ([] if total is None else [total])
    return pl.pallas_call(
        functools.partial(kernel, parts),
        in_specs=[smem if x.ndim == 1 else vmem for x in leading]
        + [pl.BlockSpec(memory_space=pl.ANY)] * parts
        + ([] if total is None else [hbm]),
        out_specs=hbm,
        out_shape=jax.ShapeDtypeStruct((slots, size, size), jnp.float32),
        scratch_shapes=([pltpu.SMEM((LIST + 1,), jnp.int32)] if own_list else [])
        + [
            pltpu.VMEM((slots, size, size), jnp.float32),
            pltpu.SemaphoreType.DMA((slots,)),
            pltpu.SMEM((slots,), jnp.int32),
            pltpu.VMEM((AHEAD, size, size), jnp.float32),
            pltpu.VMEM((AHEAD, size, size), jnp.float32),
            pltpu.SemaphoreType.DMA((AHEAD,)),
            pltpu.SemaphoreType.DMA((AHEAD,)),
        ],
        input_output_aliases={} if total is None else {len(operands) - 1: 0},
        compiler_params=pltpu.CompilerParams(vmem_limit_bytes=VMEM_LIMIT),
        cost_estimate=pl.CostEstimate(
            flops=8 * 3 * 2 * size**3, bytes_accessed=24 * size * size * 4, transcendentals=0
        ),
        name="products",
    )(*operands)


def to_row(block, rows, there):
    return lax.ppermute(block, "row", [(i, there(i)) for i in range(rows)])


def on_z(i):
    return (i & 9) | ((i + 2) & 6)


def back_z(i):
    return (i & 9) | ((i - 2) & 6)


def moved(block, there, columns):
    return lax.ppermute(block, COL, [(i, there(i)) for i in range(columns)])


def pair_kernel(tile_ref, beside_ref, _, pair_ref, __, sems):
    n = tile_ref.shape[0]
    copies = [
        pltpu.make_async_copy(tile_ref, pair_ref.at[pl.ds(0, n)], sems.at[0]),
        pltpu.make_async_copy(beside_ref, pair_ref.at[pl.ds(n, n)], sems.at[1]),
    ]
    for copy in copies:
        copy.start()
    for copy in copies:
        copy.wait()


def paired(tile, beside, passing):
    n, size = tile.shape[0], tile.shape[-1]
    anywhere = pl.BlockSpec(memory_space=pl.ANY)
    return pl.pallas_call(
        pair_kernel,
        in_specs=[anywhere] * 3,
        out_specs=[pl.BlockSpec(memory_space=pltpu.VMEM), anywhere],
        out_shape=[
            jax.ShapeDtypeStruct((2 * n, size, size), tile.dtype),
            jax.ShapeDtypeStruct(passing.shape, passing.dtype),
        ],
        scratch_shapes=[pltpu.SemaphoreType.DMA((2,))],
        input_output_aliases={2: 1},
        compiler_params=pltpu.CompilerParams(vmem_limit_bytes=4 << 20),
        name="pair",
    )(tile, beside, passing)


def hold_kernel(*refs):
    pass


def held_for(arrays, later):
    anywhere = pl.BlockSpec(memory_space=pl.ANY)
    return pl.pallas_call(
        hold_kernel,
        in_specs=[anywhere] * (len(arrays) + len(later)),
        out_specs=[anywhere] * len(arrays),
        out_shape=[jax.ShapeDtypeStruct(x.shape, x.dtype) for x in arrays],
        input_output_aliases={i: i for i in range(len(arrays))},
        compiler_params=pltpu.CompilerParams(vmem_limit_bytes=1 << 20),
        name="hold",
    )(*arrays, *later)


def among(held, bits, rows, columns):
    me = lax.axis_index("row") * columns + lax.axis_index(COL)
    group = jnp.zeros((2 ** len(bits),) + held.shape, held.dtype)
    for move in range(2 ** len(bits)):
        flip = sum(((move >> n) & 1) << bit for n, bit in enumerate(bits))
        got = held
        if move:
            pairs = [(i ^ flip, i) for i in range(rows * columns)]
            got = lax.ppermute(held, ("row", *COL), pairs)
        spot = sum((((me ^ flip) >> bit) & 1) << n for n, bit in enumerate(bits))
        group = lax.dynamic_update_index_in_dim(group, got, spot, 0)
    return group


def per_device(a_blocks, a_index, b_blocks, b_index, c_index):
    rows = lax.axis_size("row")
    columns = lax.axis_size(COL)
    row = lax.axis_index("row")
    me = jnp.stack([row, lax.axis_index(COL)])
    hold = columns // rows
    sa, sb, sc = a_blocks.shape[2], b_blocks.shape[3], c_index.shape[2]
    held = hold * sb
    size = a_blocks.shape[-1]

    own = b_blocks[0, 0].reshape(held, size, size)
    behind = to_row(own, rows, lambda i: (i + 2) % rows)
    ahead = to_row(own, rows, lambda i: (i - 2) % rows)
    near = [own, behind, ahead]

    blank = jnp.full((8 - sa,), -1, jnp.int32)
    mine = jnp.concatenate([a_index[0, 0], blank, b_index[0, 0].reshape(-1), c_index[0, 0]])
    spots = among(jnp.pad(mine, (0, 128 - mine.shape[0])), (5, 6), rows, columns)
    spots = among(spots, (1, 2), rows, columns)
    tile = a_blocks[0, 0]
    pair, spots = paired(tile, moved(tile, lambda i: i ^ 8, columns), spots)
    spots = among(spots, (3,), rows, columns)
    spots = among(spots, (4,), rows, columns)
    spots = among(spots, (0,), rows, columns).reshape(rows * columns, 128)
    a_behind = moved(pair, on_z, columns)
    a_ahead = moved(pair, back_z, columns)

    sends = [
        (FAR, 2, lambda i: (i - 2) & 7),
        (FAR, 3, lambda i: ((i + 2) & 7) ^ 1),
        (NEAR, 1, lambda i: i ^ 1),
    ]
    pack_list, info, maps = plan(me, spots, sends)
    packed = pack(pack_list, near, [n for n, *_ in sends])

    far_own, far_other, cross = [
        to_row(block, rows, there) for block, (*_, there) in zip(packed, sends)
    ]

    over, product_list = overflow(me, info, spots, maps)
    (a_behind,) = held_for([a_behind], [info])
    a_far = moved(a_behind, on_z, columns)
    (a_far,) = held_for([a_far], [far_own, far_other, cross, over])
    a_mine = [pair, a_behind, a_ahead, a_far]
    a_parts = a_mine + [moved(block, lambda i: i ^ 1, columns) for block in a_mine]

    b_parts = near + [cross, far_own, far_other]
    total = products(all_kernel, [product_list], a_parts, b_parts, None, sc)

    trips = over[0]

    def trip(state):
        done, total = state
        sent = jnp.where(done >= 0, own, 0)
        whole = [own] + [to_row(sent, rows, lambda i, n=n: i ^ n) for n in range(1, rows)]
        rest = products(rest_kernel, [me, info], a_parts, whole, total, sc, own_list=True)
        return done + 1, rest

    _, total = lax.while_loop(lambda state: state[0] < trips, trip, (jnp.int32(0), total))
    return total[None, None]


def solution(mesh):
    rows, columns = mesh.devices.shape
    mesh = Mesh(mesh.devices.reshape(rows, 2, columns // 4, 2), ("row", *COL))
    in_specs = (
        P("row", COL, None, None, None),
        P("row", COL, None),
        P("row", COL, None, None, None, None),
        P("row", COL, None, None),
        P("row", COL, None),
    )
    out_specs = P("row", COL, None, None, None)
    return jax.shard_map(
        per_device, mesh=mesh, in_specs=in_specs, out_specs=out_specs, check_vma=False
    )
```

```python
import functools

import jax
import jax.numpy as jnp
from jax import lax
from jax.experimental import pallas as pl
from jax.experimental.pallas import tpu as pltpu
from jax.sharding import Mesh
from jax.sharding import PartitionSpec as P

SA = 4
PK = 8
NBD = 8
NEAR = 6
FAR = 3
COL = ("x_lo", "z", "core")
VMEM_LIMIT = 8 << 20
A_PARTS = 8
LIST = 512
AHEAD = 8


def matmul(a, b):
    return jnp.dot(a.astype(jnp.bfloat16), b, preferred_element_type=jnp.float32)


def lands_at(a_line, b):
    meet = (a_line >= 0) & (b >= 0) & ((a_line & (PK - 1)) == (b >> 3))
    return jnp.where(meet, (a_line >> 3) * NBD + (b & (NBD - 1)), -2)


def needed(a, b, c):
    need = jnp.zeros(b.shape, jnp.bool_)
    for s in range(SA):
        lands = lands_at(a[s : s + 1], b)
        for n in range(c.shape[0]):
            need = need | (lands == c[n : n + 1])
    return need


def lane_facts(shape, axis=1):
    lane = lax.broadcasted_iota(jnp.int32, shape, axis)
    r, p = lane >> 4, lane & 15
    owner = p >> 1
    far = (((owner >> 1) - (r >> 1)) & 3) == 2
    way = ((owner ^ r) & 1) + jnp.where(far, 2, 0)
    return r, p, owner, way


def code(a_slot, part, at, c_slot):
    return ((a_slot * 16 + part) * 128 + at) * 16 + c_slot


def a_of(word):
    return word >> 15


def part_of(word):
    return (word >> 11) & 15


def at_of(word):
    return (word >> 4) & 127


def c_of(word):
    return word & 15


def fetch_a(word, a_refs, dst, sem):
    a = a_of(word)
    fetch_block(a >> 3, a & 7, a_refs, dst, sem)


def fetch_block(part, at, refs, dst, sem):
    for i, ref in enumerate(refs):

        def start(ref=ref):
            pltpu.make_async_copy(ref.at[at], dst, sem).start()

        if len(refs) == 1:
            start()
        else:
            pl.when(part == i)(start)


def make_maps(maps_ref):
    shape = maps_ref.shape[1:]
    lane = lax.broadcasted_iota(jnp.int32, shape, 1)
    down = lax.broadcasted_iota(jnp.int32, shape, 0)
    r, p, owner, way = lane_facts(shape)
    r_down, p_down, _, way_down = lane_facts(shape, 0)
    holder = (p_down == 0) & (r_down == owner)
    alike = (r == r_down) & (way == way_down)
    y, xh, xl, z, core = lane >> 5, (lane >> 4) & 1, (lane >> 3) & 1, (lane >> 1) & 3, lane & 1
    listed_at = (((core * 2 + xh) * 2 + xl) * 4 + z) * 4 + y
    for n, flags in enumerate(
        [
            holder & ((p & 1) == 0),
            holder & ((p & 1) == 1),
            (p_down == 0) & (r == r_down),
            alike,
            alike & (down < lane),
            down == listed_at,
        ]
    ):
        maps_ref[n] = jnp.where(flags, 1.0, 0.0).astype(jnp.bfloat16)


def positions(spots_ref, maps_ref):
    spots = spots_ref[...].astype(jnp.float32).astype(jnp.bfloat16)
    return lax.dot_general(
        spots, maps_ref[5], (((0,), (0,)), ((), ())), preferred_element_type=jnp.float32
    )


def plan_kernel(sends, me_ref, spots_ref, pack_list, info_ref, maps_ref):
    row, column = me_ref[0], me_ref[1]
    make_maps(maps_ref)
    held = positions(spots_ref, maps_ref)
    a = held[:8].astype(jnp.int32)
    turned = pltpu.roll(held[8:40], (128 - column) & 127, 1)
    b = matmul(turned[:8], maps_ref[0]) + matmul(turned[8:16], maps_ref[1])
    b = b.astype(jnp.int32)
    c = matmul(turned[16:32], maps_ref[2]).astype(jnp.int32)
    need = needed(a, b, c)

    r, p, owner, way = lane_facts(b.shape)
    t = lax.broadcasted_iota(jnp.int32, b.shape, 0)
    flags = jnp.where(need, 1.0, 0.0)
    alike = matmul(flags, maps_ref[3])
    upto = alike
    for step in (1, 2, 4):
        upto = upto + jnp.where(t >= step, pltpu.roll(upto, step, 0), 0.0)
    rank = (upto - alike + matmul(flags, maps_ref[4])).astype(jnp.int32)
    order = jnp.where(need, way * 128 + rank, -1)

    steps = ((owner >> 1) - (row >> 1)) & 3
    part = jnp.where(steps == 0, 0, jnp.where(steps == 3, 1, 2))
    word = (part * 16 + (p & 1) * 8 + t).astype(jnp.float32)
    n = 0
    for slots, which, there in sends:
        for e in range(slots):
            hit = (order == which * 128 + e) & (r == there(row))
            pack_list[n] = jnp.max(jnp.where(hit, word, -1.0)).astype(jnp.int32)
            n += 1

    info_ref[0:8] = a
    info_ref[8:16] = b
    info_ref[16:32] = c
    info_ref[32:40] = order


def plan(me, spots, sends):
    smem = pl.BlockSpec(memory_space=pltpu.SMEM)
    vmem = pl.BlockSpec(memory_space=pltpu.VMEM)
    return pl.pallas_call(
        functools.partial(plan_kernel, sends),
        in_specs=[smem, vmem],
        out_specs=[smem, vmem, vmem],
        out_shape=[
            jax.ShapeDtypeStruct((sum(n for n, *_ in sends),), jnp.int32),
            jax.ShapeDtypeStruct((40, 128), jnp.int32),
            jax.ShapeDtypeStruct((6, 128, 128), jnp.bfloat16),
        ],
        compiler_params=pltpu.CompilerParams(vmem_limit_bytes=4 << 20),
        name="plan",
    )(me, spots)


def pack_kernel(sizes, list_ref, *rest):
    near, packed, sems = rest[:3], rest[3:-1], rest[-1]
    places = [(i, e) for i, size in enumerate(sizes) for e in range(size)]
    for n, (i, e) in enumerate(places):
        word = list_ref[n]

        @pl.when(word >= 0)
        def _():
            fetch_block(word >> 4, word & 15, near, packed[i].at[e], sems.at[n])

    for n, (i, e) in enumerate(places):

        @pl.when(list_ref[n] >= 0)
        def _():
            pltpu.make_async_copy(near[0].at[0], packed[i].at[e], sems.at[n]).wait()


def pack(listing, near, sizes):
    size = near[0].shape[-1]
    return pl.pallas_call(
        functools.partial(pack_kernel, sizes),
        in_specs=[pl.BlockSpec(memory_space=pltpu.SMEM)]
        + [pl.BlockSpec(memory_space=pl.ANY)] * 3,
        out_specs=[pl.BlockSpec(memory_space=pltpu.VMEM)] * len(sizes),
        scratch_shapes=[pltpu.SemaphoreType.DMA((sum(sizes),))],
        out_shape=[jax.ShapeDtypeStruct((n, size, size), jnp.float32) for n in sizes],
        compiler_params=pltpu.CompilerParams(vmem_limit_bytes=4 << 20),
        name="pack",
    )(listing, *near)


def overflow_kernel(
    me_ref, info_ref, spots_ref, maps_ref, over_ref, product_list, zeros_ref, zero, sem
):
    zero[...] = jnp.zeros_like(zero)
    stores = [pltpu.make_async_copy(zero, zeros_ref.at[c], sem.at[c]) for c in range(sem.shape[0])]
    for store in stores:
        store.start()
    extract(entries_of(info_ref, me_ref)[0], product_list)
    held = positions(spots_ref, maps_ref)
    a = held[:8].astype(jnp.int32)
    turned = [held[8:40]] + [pltpu.roll(held[8:40], 128 - q, 1) for q in range(1, 16)]
    b = matmul(jnp.concatenate([x[:8] for x in turned]), maps_ref[0])
    b = b + matmul(jnp.concatenate([x[8:16] for x in turned]), maps_ref[1])
    b = b.astype(jnp.int32)
    c = matmul(jnp.concatenate([x[16:32] for x in turned]), maps_ref[2]).astype(jnp.int32)
    flags = [
        jnp.where(needed(a, b[q * 8 : q * 8 + 8], c[q * 16 : q * 16 + 16]), 1.0, 0.0)
        for q in range(16)
    ]
    alike = matmul(jnp.concatenate(flags), maps_ref[3])
    most = jnp.sum(alike[:8], axis=0, keepdims=True)
    for q in range(1, 16):
        most = jnp.maximum(most, jnp.sum(alike[q * 8 : q * 8 + 8], axis=0, keepdims=True))
    *_, way = lane_facts(most.shape)
    slots = jnp.where(way == 0, 128, jnp.where(way == 1, NEAR, FAR))
    over_ref[0] = jnp.max(jnp.where(most > slots.astype(jnp.float32), 1.0, 0.0)).astype(jnp.int32)
    for store in stores:
        store.wait()


def overflow(me, info, spots, maps, slots, size):
    smem = pl.BlockSpec(memory_space=pltpu.SMEM)
    vmem = pl.BlockSpec(memory_space=pltpu.VMEM)
    return pl.pallas_call(
        overflow_kernel,
        in_specs=[smem, vmem, vmem, vmem],
        out_specs=[smem, smem, pl.BlockSpec(memory_space=pltpu.HBM)],
        out_shape=[
            jax.ShapeDtypeStruct((1,), jnp.int32),
            jax.ShapeDtypeStruct((LIST + 1,), jnp.int32),
            jax.ShapeDtypeStruct((slots, size, size), jnp.float32),
        ],
        scratch_shapes=[pltpu.VMEM((size, size), jnp.float32), pltpu.SemaphoreType.DMA((slots,))],
        compiler_params=pltpu.CompilerParams(vmem_limit_bytes=4 << 20),
        cost_estimate=pl.CostEstimate(flops=10**9, bytes_accessed=10**5, transcendentals=0),
        name="overflow",
    )(me, info, spots, maps)


def halves(x):
    high = x.astype(jnp.bfloat16)
    return high, (x - high.astype(jnp.float32)).astype(jnp.bfloat16)


def block_product(a, b):
    a_high, a_low = halves(a)
    b_high, b_low = halves(b)
    dot = functools.partial(jnp.dot, preferred_element_type=jnp.float32)
    return dot(a_high, b_high) + (dot(a_high, b_low) + dot(a_low, b_high))


def extract(entries, list_ref):
    def more(state):
        n, word, left = state
        list_ref[n] = word.astype(jnp.int32)
        left = jnp.where(left == word, -1.0, left)
        return n + 1, jnp.max(left), left

    n, *_ = lax.while_loop(
        lambda state: state[1] >= 0, more, (jnp.int32(0), jnp.max(entries), entries)
    )
    list_ref[LIST] = n


def entries_of(info_ref, me_ref):
    row, column = me_ref[0], me_ref[1]
    b, c, order = info_ref[8:16], info_ref[16:32], info_ref[32:40]
    r, p, owner, way = lane_facts(b.shape)
    t = lax.broadcasted_iota(jnp.int32, b.shape, 0)
    rank = order & 127
    steps = ((owner >> 1) - (row >> 1)) & 3
    part = jnp.where(steps == 0, 0, jnp.where(steps == 3, 1, 2))
    sent = (way > 0) & (rank < jnp.where(way == 1, NEAR, FAR))
    along = ((p >> 1) - (column >> 1)) & 3
    beside = ((p ^ column) >> 3) & 1
    a_part = jnp.where(along == 0, 0, jnp.where(along == 3, 1, jnp.where(along == 1, 2, 3)))
    a_at = (a_part + 4 * ((p ^ column) & 1)) * 8 + beside * SA
    found = [[], []]
    for s in range(SA):
        lands = lands_at(info_ref[s : s + 1], b)
        c_slot = jnp.full(b.shape, -1, jnp.int32)
        for n in range(c.shape[0]):
            c_slot = jnp.where(lands == c[n : n + 1], n, c_slot)
        live = (c_slot >= 0) & (r == row)
        a_slot = a_at + s
        at_hand = jnp.where(
            way == 0,
            code(a_slot, part, (p & 1) * 8 + t, c_slot),
            code(a_slot, 2 + way, rank, c_slot),
        )
        elsewhere = code(a_slot, owner ^ row, (p & 1) * 8 + t, c_slot)
        found[0].append(jnp.where(live & ((way == 0) | sent), at_hand, -1).astype(jnp.float32))
        found[1].append(jnp.where(live & (way > 0) & ~sent, elsewhere, -1).astype(jnp.float32))
    return [jnp.concatenate(x) for x in found]


def multiply_listed(list_ref, a_refs, b_refs, acc, a_buf, b_buf, a_sem, b_sem, meanwhile):
    count = list_ref[LIST]

    def fetch(n):
        slot = n % AHEAD
        word = list_ref[n]
        fetch_a(word, a_refs, a_buf.at[slot], a_sem.at[slot])
        fetch_block(part_of(word), at_of(word), b_refs, b_buf.at[slot], b_sem.at[slot])

    for n in range(AHEAD):

        @pl.when(n < count)
        def _():
            fetch(n)

    meanwhile()

    def step(n, carry):
        slot = n % AHEAD
        pltpu.make_async_copy(a_refs[0].at[0], a_buf.at[slot], a_sem.at[slot]).wait()
        pltpu.make_async_copy(b_refs[0].at[0], b_buf.at[slot], b_sem.at[slot]).wait()
        acc[c_of(list_ref[n])] += block_product(a_buf[slot], b_buf[slot])

        @pl.when(n + AHEAD < count)
        def _():
            fetch(n + AHEAD)

        return carry

    lax.fori_loop(0, count, step, 0)


def all_kernel(parts, list_ref, *rest):
    a_refs, b_refs = rest[:A_PARTS], rest[A_PARTS:parts]
    _, out_ref, acc, c_sem, touched, *buffers = rest[parts:]
    slots = acc.shape[0]

    def stored(c):
        return pltpu.make_async_copy(acc.at[c], out_ref.at[c], c_sem.at[c])

    def meanwhile():
        for c in range(slots):
            touched[c] = 0

        def mark(n, carry):
            touched[c_of(list_ref[n])] = 1
            return carry

        lax.fori_loop(0, list_ref[LIST], mark, 0)
        acc[...] = jnp.zeros_like(acc)

    multiply_listed(list_ref, a_refs, b_refs, acc, *buffers, meanwhile)
    for c in range(slots):
        pl.when(touched[c] == 1)(lambda c=c: stored(c).start())
    for c in range(slots):
        pl.when(touched[c] == 1)(lambda c=c: stored(c).wait())


def add_listed(list_ref, a_refs, b_refs, total_ref, out_ref, acc, c_sem, stage, *buffers):
    count = list_ref[LIST]

    def touched(was, act):
        def step(n, carry):
            c = c_of(list_ref[n])

            @pl.when(stage[c] == was)
            def _():
                stage[c] = was + 1
                act(c)

            return carry

        lax.fori_loop(0, count, step, 0)

    def fetched(c):
        return pltpu.make_async_copy(total_ref.at[c], acc.at[c], c_sem.at[c])

    def stored(c):
        return pltpu.make_async_copy(acc.at[c], out_ref.at[c], c_sem.at[c])

    for c in range(acc.shape[0]):
        stage[c] = 0

    def meanwhile():
        touched(0, lambda c: fetched(c).start())
        touched(1, lambda c: fetched(c).wait())

    multiply_listed(list_ref, a_refs, b_refs, acc, *buffers, meanwhile)
    touched(2, lambda c: stored(c).start())
    touched(3, lambda c: stored(c).wait())


def rest_kernel(parts, me_ref, info_ref, *rest):
    a_refs, b_refs = rest[:A_PARTS], rest[A_PARTS:parts]
    total_ref, out_ref, rest_list, *buffers = rest[parts:]
    extract(entries_of(info_ref, me_ref)[1], rest_list)
    add_listed(rest_list, a_refs, b_refs, total_ref, out_ref, *buffers)


def products(kernel, leading, a_parts, b_parts, total, slots, own_list=False):
    size = a_parts[0].shape[-1]
    parts = len(a_parts) + len(b_parts)
    smem = pl.BlockSpec(memory_space=pltpu.SMEM)
    vmem = pl.BlockSpec(memory_space=pltpu.VMEM)
    hbm = pl.BlockSpec(memory_space=pltpu.HBM)
    operands = [*leading, *a_parts, *b_parts] + ([] if total is None else [total])
    return pl.pallas_call(
        functools.partial(kernel, parts),
        in_specs=[smem if x.ndim == 1 else vmem for x in leading]
        + [pl.BlockSpec(memory_space=pl.ANY)] * parts
        + ([] if total is None else [hbm]),
        out_specs=hbm,
        out_shape=jax.ShapeDtypeStruct((slots, size, size), jnp.float32),
        scratch_shapes=([pltpu.SMEM((LIST + 1,), jnp.int32)] if own_list else [])
        + [
            pltpu.VMEM((slots, size, size), jnp.float32),
            pltpu.SemaphoreType.DMA((slots,)),
            pltpu.SMEM((slots,), jnp.int32),
            pltpu.VMEM((AHEAD, size, size), jnp.float32),
            pltpu.VMEM((AHEAD, size, size), jnp.float32),
            pltpu.SemaphoreType.DMA((AHEAD,)),
            pltpu.SemaphoreType.DMA((AHEAD,)),
        ],
        input_output_aliases={} if total is None else {len(operands) - 1: 0},
        compiler_params=pltpu.CompilerParams(vmem_limit_bytes=VMEM_LIMIT),
        cost_estimate=pl.CostEstimate(
            flops=8 * 3 * 2 * size**3, bytes_accessed=24 * size * size * 4, transcendentals=0
        ),
        name="products",
    )(*operands)


def to_row(block, rows, there):
    return lax.ppermute(block, "row", [(i, there(i)) for i in range(rows)])


def on_z(i):
    return (i & 9) | ((i + 2) & 6)


def back_z(i):
    return (i & 9) | ((i - 2) & 6)


def moved(block, there, columns):
    return lax.ppermute(block, COL, [(i, there(i)) for i in range(columns)])


def pair_kernel(tile_ref, beside_ref, _, pair_ref, __, sems):
    n = tile_ref.shape[0]
    copies = [
        pltpu.make_async_copy(tile_ref, pair_ref.at[pl.ds(0, n)], sems.at[0]),
        pltpu.make_async_copy(beside_ref, pair_ref.at[pl.ds(n, n)], sems.at[1]),
    ]
    for copy in copies:
        copy.start()
    for copy in copies:
        copy.wait()


def paired(tile, beside, passing):
    n, size = tile.shape[0], tile.shape[-1]
    anywhere = pl.BlockSpec(memory_space=pl.ANY)
    return pl.pallas_call(
        pair_kernel,
        in_specs=[anywhere] * 3,
        out_specs=[pl.BlockSpec(memory_space=pltpu.VMEM), anywhere],
        out_shape=[
            jax.ShapeDtypeStruct((2 * n, size, size), tile.dtype),
            jax.ShapeDtypeStruct(passing.shape, passing.dtype),
        ],
        scratch_shapes=[pltpu.SemaphoreType.DMA((2,))],
        input_output_aliases={2: 1},
        compiler_params=pltpu.CompilerParams(vmem_limit_bytes=4 << 20),
        name="pair",
    )(tile, beside, passing)


def hold_kernel(*refs):
    pass


def held_for(arrays, later):
    anywhere = pl.BlockSpec(memory_space=pl.ANY)
    return pl.pallas_call(
        hold_kernel,
        in_specs=[anywhere] * (len(arrays) + len(later)),
        out_specs=[anywhere] * len(arrays),
        out_shape=[jax.ShapeDtypeStruct(x.shape, x.dtype) for x in arrays],
        input_output_aliases={i: i for i in range(len(arrays))},
        compiler_params=pltpu.CompilerParams(vmem_limit_bytes=1 << 20),
        name="hold",
    )(*arrays, *later)


def among(held, bits, rows, columns):
    me = lax.axis_index("row") * columns + lax.axis_index(COL)
    group = jnp.zeros((2 ** len(bits),) + held.shape, held.dtype)
    for move in range(2 ** len(bits)):
        flip = sum(((move >> n) & 1) << bit for n, bit in enumerate(bits))
        got = held
        if move:
            pairs = [(i ^ flip, i) for i in range(rows * columns)]
            got = lax.ppermute(held, ("row", *COL), pairs)
        spot = sum((((me ^ flip) >> bit) & 1) << n for n, bit in enumerate(bits))
        group = lax.dynamic_update_index_in_dim(group, got, spot, 0)
    return group


def per_device(a_blocks, a_index, b_blocks, b_index, c_index):
    rows = lax.axis_size("row")
    columns = lax.axis_size(COL)
    row = lax.axis_index("row")
    me = jnp.stack([row, lax.axis_index(COL)])
    hold = columns // rows
    sa, sb, sc = a_blocks.shape[2], b_blocks.shape[3], c_index.shape[2]
    held = hold * sb
    size = a_blocks.shape[-1]

    own = b_blocks[0, 0].reshape(held, size, size)
    behind = to_row(own, rows, lambda i: (i + 2) % rows)
    ahead = to_row(own, rows, lambda i: (i - 2) % rows)
    near = [own, behind, ahead]

    blank = jnp.full((8 - sa,), -1, jnp.int32)
    mine = jnp.concatenate([a_index[0, 0], blank, b_index[0, 0].reshape(-1), c_index[0, 0]])
    spots = among(jnp.pad(mine, (0, 128 - mine.shape[0])), (5, 6), rows, columns)
    tile = a_blocks[0, 0]
    pair, spots = paired(tile, moved(tile, lambda i: i ^ 8, columns), spots)
    spots = among(spots, (1, 2), rows, columns)
    spots = among(spots, (3,), rows, columns)
    spots = among(spots, (4,), rows, columns)
    spots = among(spots, (0,), rows, columns).reshape(rows * columns, 128)
    a_behind = moved(pair, on_z, columns)
    a_ahead = moved(pair, back_z, columns)

    sends = [
        (FAR, 3, lambda i: ((i + 2) & 7) ^ 1),
        (FAR, 2, lambda i: (i - 2) & 7),
        (NEAR, 1, lambda i: i ^ 1),
    ]
    pack_list, info, maps = plan(me, spots, sends)
    packed = pack(pack_list, near, [n for n, *_ in sends])

    far_other, far_own, cross = [
        to_row(block, rows, there) for block, (*_, there) in zip(packed, sends)
    ]

    over, product_list, zeros = overflow(me, info, spots, maps, sc, size)
    (a_behind,) = held_for([a_behind], [info])
    a_far = moved(a_behind, on_z, columns)
    (a_far,) = held_for([a_far], [far_other, far_own, cross, over])
    a_mine = [pair, a_behind, a_ahead, a_far]
    a_parts = a_mine + [moved(block, lambda i: i ^ 1, columns) for block in a_mine]

    b_parts = near + [cross, far_own, far_other]
    total = products(all_kernel, [product_list], a_parts, b_parts, zeros, sc)

    trips = over[0]

    def trip(state):
        done, total = state
        sent = jnp.where(done >= 0, own, 0)
        whole = [own] + [to_row(sent, rows, lambda i, n=n: i ^ n) for n in range(1, rows)]
        rest = products(rest_kernel, [me, info], a_parts, whole, total, sc, own_list=True)
        return done + 1, rest

    _, total = lax.while_loop(lambda state: state[0] < trips, trip, (jnp.int32(0), total))
    return total[None, None]


def solution(mesh):
    rows, columns = mesh.devices.shape
    mesh = Mesh(mesh.devices.reshape(rows, 2, columns // 4, 2), ("row", *COL))
    in_specs = (
        P("row", COL, None, None, None),
        P("row", COL, None),
        P("row", COL, None, None, None, None),
        P("row", COL, None, None),
        P("row", COL, None),
    )
    out_specs = P("row", COL, None, None, None)
    return jax.shard_map(
        per_device, mesh=mesh, in_specs=in_specs, out_specs=out_specs, check_vma=False
    )
```

```python
import functools

import jax
import jax.numpy as jnp
from jax import lax
from jax.experimental import pallas as pl
from jax.experimental.pallas import tpu as pltpu
from jax.sharding import Mesh
from jax.sharding import PartitionSpec as P

SA = 4
PK = 8
NBD = 8
NEAR = 6
FAR = 3
COL = ("x_lo", "z", "core")
VMEM_LIMIT = 8 << 20
A_PARTS = 8
LIST = 512
AHEAD = 8


def matmul(a, b):
    return jnp.dot(a.astype(jnp.bfloat16), b, preferred_element_type=jnp.float32)


def lands_at(a_line, b):
    meet = (a_line >= 0) & (b >= 0) & ((a_line & (PK - 1)) == (b >> 3))
    return jnp.where(meet, (a_line >> 3) * NBD + (b & (NBD - 1)), -2)


def needed(a, b, c):
    need = jnp.zeros(b.shape, jnp.bool_)
    for s in range(SA):
        lands = lands_at(a[s : s + 1], b)
        for n in range(c.shape[0]):
            need = need | (lands == c[n : n + 1])
    return need


def lane_facts(shape, axis=1):
    lane = lax.broadcasted_iota(jnp.int32, shape, axis)
    r, p = lane >> 4, lane & 15
    owner = p >> 1
    far = (((owner >> 1) - (r >> 1)) & 3) == 2
    way = ((owner ^ r) & 1) + jnp.where(far, 2, 0)
    return r, p, owner, way


def code(a_slot, part, at, c_slot):
    return ((a_slot * 16 + part) * 128 + at) * 16 + c_slot


def a_of(word):
    return word >> 15


def part_of(word):
    return (word >> 11) & 15


def at_of(word):
    return (word >> 4) & 127


def c_of(word):
    return word & 15


def fetch_a(word, a_refs, dst, sem):
    a = a_of(word)
    fetch_block(a >> 3, a & 7, a_refs, dst, sem)


def fetch_block(part, at, refs, dst, sem):
    for i, ref in enumerate(refs):

        def start(ref=ref):
            pltpu.make_async_copy(ref.at[at], dst, sem).start()

        if len(refs) == 1:
            start()
        else:
            pl.when(part == i)(start)


def make_maps(maps_ref):
    shape = maps_ref.shape[1:]
    lane = lax.broadcasted_iota(jnp.int32, shape, 1)
    down = lax.broadcasted_iota(jnp.int32, shape, 0)
    r, p, owner, way = lane_facts(shape)
    r_down, p_down, _, way_down = lane_facts(shape, 0)
    holder = (p_down == 0) & (r_down == owner)
    alike = (r == r_down) & (way == way_down)
    y, xh, xl, z, core = lane >> 5, (lane >> 4) & 1, (lane >> 3) & 1, (lane >> 1) & 3, lane & 1
    listed_at = (((core * 2 + xh) * 2 + xl) * 4 + z) * 4 + y
    for n, flags in enumerate(
        [
            holder & ((p & 1) == 0),
            holder & ((p & 1) == 1),
            (p_down == 0) & (r == r_down),
            alike,
            alike & (down < lane),
            down == listed_at,
        ]
    ):
        maps_ref[n] = jnp.where(flags, 1.0, 0.0).astype(jnp.bfloat16)


def positions(spots_ref, maps_ref):
    spots = spots_ref[...].astype(jnp.float32).astype(jnp.bfloat16)
    return lax.dot_general(
        spots, maps_ref[5], (((0,), (0,)), ((), ())), preferred_element_type=jnp.float32
    )


def list_sends(sends, row, order, turn, pack_list):
    r, p, owner, _ = lane_facts(order.shape)
    t = lax.broadcasted_iota(jnp.int32, order.shape, 0)
    steps = ((owner >> 1) - (row >> 1)) & 3
    part = jnp.where(steps == 0, 0, jnp.where(steps == 3, 1, 2))
    word = (part * 16 + (p & 1) * 8 + t).astype(jnp.float32)
    n = 0
    for slots, which, there in sends:
        for e in range(slots):
            hit = (order == which * 128 + turn * slots + e) & (r == there(row))
            pack_list[n] = jnp.max(jnp.where(hit, word, -1.0)).astype(jnp.int32)
            n += 1


def relist_kernel(sends, me_ref, turn_ref, info_ref, pack_list):
    list_sends(sends, me_ref[0], info_ref[32:40], turn_ref[0], pack_list)


def relist(me, turn, info, sends):
    smem = pl.BlockSpec(memory_space=pltpu.SMEM)
    return pl.pallas_call(
        functools.partial(relist_kernel, sends),
        in_specs=[smem, smem, pl.BlockSpec(memory_space=pltpu.VMEM)],
        out_specs=smem,
        out_shape=jax.ShapeDtypeStruct((sum(n for n, *_ in sends),), jnp.int32),
        compiler_params=pltpu.CompilerParams(vmem_limit_bytes=4 << 20),
        name="relist",
    )(me, turn, info)


def plan_kernel(sends, me_ref, spots_ref, pack_list, info_ref, maps_ref):
    row, column = me_ref[0], me_ref[1]
    make_maps(maps_ref)
    held = positions(spots_ref, maps_ref)
    a = held[:8].astype(jnp.int32)
    turned = pltpu.roll(held[8:40], (128 - column) & 127, 1)
    b = matmul(turned[:8], maps_ref[0]) + matmul(turned[8:16], maps_ref[1])
    b = b.astype(jnp.int32)
    c = matmul(turned[16:32], maps_ref[2]).astype(jnp.int32)
    need = needed(a, b, c)

    r, p, owner, way = lane_facts(b.shape)
    t = lax.broadcasted_iota(jnp.int32, b.shape, 0)
    flags = jnp.where(need, 1.0, 0.0)
    alike = matmul(flags, maps_ref[3])
    upto = alike
    for step in (1, 2, 4):
        upto = upto + jnp.where(t >= step, pltpu.roll(upto, step, 0), 0.0)
    rank = (upto - alike + matmul(flags, maps_ref[4])).astype(jnp.int32)
    order = jnp.where(need, way * 128 + rank, -1)

    list_sends(sends, row, order, 0, pack_list)
    info_ref[0:8] = a
    info_ref[8:16] = b
    info_ref[16:32] = c
    info_ref[32:40] = order


def plan(me, spots, sends):
    smem = pl.BlockSpec(memory_space=pltpu.SMEM)
    vmem = pl.BlockSpec(memory_space=pltpu.VMEM)
    return pl.pallas_call(
        functools.partial(plan_kernel, sends),
        in_specs=[smem, vmem],
        out_specs=[smem, vmem, vmem],
        out_shape=[
            jax.ShapeDtypeStruct((sum(n for n, *_ in sends),), jnp.int32),
            jax.ShapeDtypeStruct((40, 128), jnp.int32),
            jax.ShapeDtypeStruct((6, 128, 128), jnp.bfloat16),
        ],
        compiler_params=pltpu.CompilerParams(vmem_limit_bytes=4 << 20),
        name="plan",
    )(me, spots)


def pack_kernel(sizes, list_ref, *rest):
    near, packed, sems = rest[:3], rest[3:-1], rest[-1]
    places = [(i, e) for i, size in enumerate(sizes) for e in range(size)]
    for n, (i, e) in enumerate(places):
        word = list_ref[n]

        @pl.when(word >= 0)
        def _():
            fetch_block(word >> 4, word & 15, near, packed[i].at[e], sems.at[n])

    for n, (i, e) in enumerate(places):

        @pl.when(list_ref[n] >= 0)
        def _():
            pltpu.make_async_copy(near[0].at[0], packed[i].at[e], sems.at[n]).wait()


def pack(listing, near, sizes):
    size = near[0].shape[-1]
    return pl.pallas_call(
        functools.partial(pack_kernel, sizes),
        in_specs=[pl.BlockSpec(memory_space=pltpu.SMEM)]
        + [pl.BlockSpec(memory_space=pl.ANY)] * 3,
        out_specs=[pl.BlockSpec(memory_space=pltpu.VMEM)] * len(sizes),
        scratch_shapes=[pltpu.SemaphoreType.DMA((sum(sizes),))],
        out_shape=[jax.ShapeDtypeStruct((n, size, size), jnp.float32) for n in sizes],
        compiler_params=pltpu.CompilerParams(vmem_limit_bytes=4 << 20),
        name="pack",
    )(listing, *near)


def overflow_kernel(
    me_ref, info_ref, spots_ref, maps_ref, over_ref, product_list, zeros_ref, zero, sem
):
    zero[...] = jnp.zeros_like(zero)
    stores = [pltpu.make_async_copy(zero, zeros_ref.at[c], sem.at[c]) for c in range(sem.shape[0])]
    for store in stores:
        store.start()
    extract(entries_of(info_ref, me_ref)[0], product_list)
    held = positions(spots_ref, maps_ref)
    a = held[:8].astype(jnp.int32)
    turned = [held[8:40]] + [pltpu.roll(held[8:40], 128 - q, 1) for q in range(1, 16)]
    b = matmul(jnp.concatenate([x[:8] for x in turned]), maps_ref[0])
    b = b + matmul(jnp.concatenate([x[8:16] for x in turned]), maps_ref[1])
    b = b.astype(jnp.int32)
    c = matmul(jnp.concatenate([x[16:32] for x in turned]), maps_ref[2]).astype(jnp.int32)
    flags = [
        jnp.where(needed(a, b[q * 8 : q * 8 + 8], c[q * 16 : q * 16 + 16]), 1.0, 0.0)
        for q in range(16)
    ]
    alike = matmul(jnp.concatenate(flags), maps_ref[3])
    most = jnp.sum(alike[:8], axis=0, keepdims=True)
    for q in range(1, 16):
        most = jnp.maximum(most, jnp.sum(alike[q * 8 : q * 8 + 8], axis=0, keepdims=True))
    *_, way = lane_facts(most.shape)
    slots = jnp.where(way == 0, 128, jnp.where(way == 1, NEAR, FAR))
    slots = slots.astype(jnp.float32)
    turns = sum(jnp.where(most > k * slots, 1.0, 0.0) for k in range(1, 17))
    over_ref[0] = jnp.max(turns).astype(jnp.int32)
    for store in stores:
        store.wait()


def overflow(me, info, spots, maps, slots, size):
    smem = pl.BlockSpec(memory_space=pltpu.SMEM)
    vmem = pl.BlockSpec(memory_space=pltpu.VMEM)
    return pl.pallas_call(
        overflow_kernel,
        in_specs=[smem, vmem, vmem, vmem],
        out_specs=[smem, smem, pl.BlockSpec(memory_space=pltpu.HBM)],
        out_shape=[
            jax.ShapeDtypeStruct((1,), jnp.int32),
            jax.ShapeDtypeStruct((LIST + 1,), jnp.int32),
            jax.ShapeDtypeStruct((slots, size, size), jnp.float32),
        ],
        scratch_shapes=[pltpu.VMEM((size, size), jnp.float32), pltpu.SemaphoreType.DMA((slots,))],
        compiler_params=pltpu.CompilerParams(vmem_limit_bytes=4 << 20),
        cost_estimate=pl.CostEstimate(flops=10**9, bytes_accessed=10**5, transcendentals=0),
        name="overflow",
    )(me, info, spots, maps)


def halves(x):
    high = x.astype(jnp.bfloat16)
    return high, (x - high.astype(jnp.float32)).astype(jnp.bfloat16)


def block_product(a, b):
    a_high, a_low = halves(a)
    b_high, b_low = halves(b)
    dot = functools.partial(jnp.dot, preferred_element_type=jnp.float32)
    return dot(a_high, b_high) + (dot(a_high, b_low) + dot(a_low, b_high))


def extract(entries, list_ref):
    def more(state):
        n, word, left = state
        list_ref[n] = word.astype(jnp.int32)
        left = jnp.where(left == word, -1.0, left)
        return n + 1, jnp.max(left), left

    n, *_ = lax.while_loop(
        lambda state: state[1] >= 0, more, (jnp.int32(0), jnp.max(entries), entries)
    )
    list_ref[LIST] = n


def entries_of(info_ref, me_ref, turn=1):
    row, column = me_ref[0], me_ref[1]
    b, c, order = info_ref[8:16], info_ref[16:32], info_ref[32:40]
    r, p, owner, way = lane_facts(b.shape)
    t = lax.broadcasted_iota(jnp.int32, b.shape, 0)
    rank = order & 127
    steps = ((owner >> 1) - (row >> 1)) & 3
    part = jnp.where(steps == 0, 0, jnp.where(steps == 3, 1, 2))
    slots = jnp.where(way == 1, NEAR, FAR)
    sent = (way > 0) & (rank < slots)
    at = rank - turn * slots
    later = (way > 0) & (at >= 0) & (at < slots)
    along = ((p >> 1) - (column >> 1)) & 3
    beside = ((p ^ column) >> 3) & 1
    a_part = jnp.where(along == 0, 0, jnp.where(along == 3, 1, jnp.where(along == 1, 2, 3)))
    a_at = (a_part + 4 * ((p ^ column) & 1)) * 8 + beside * SA
    found = [[], []]
    for s in range(SA):
        lands = lands_at(info_ref[s : s + 1], b)
        c_slot = jnp.full(b.shape, -1, jnp.int32)
        for n in range(c.shape[0]):
            c_slot = jnp.where(lands == c[n : n + 1], n, c_slot)
        live = (c_slot >= 0) & (r == row)
        a_slot = a_at + s
        at_hand = jnp.where(
            way == 0,
            code(a_slot, part, (p & 1) * 8 + t, c_slot),
            code(a_slot, 2 + way, rank, c_slot),
        )
        in_turn = code(a_slot, (way - 1) & 3, at, c_slot)
        found[0].append(jnp.where(live & ((way == 0) | sent), at_hand, -1).astype(jnp.float32))
        found[1].append(jnp.where(live & later, in_turn, -1).astype(jnp.float32))
    return [jnp.concatenate(x) for x in found]


def multiply_listed(list_ref, a_refs, b_refs, acc, a_buf, b_buf, a_sem, b_sem, meanwhile):
    count = list_ref[LIST]

    def fetch(n):
        slot = n % AHEAD
        word = list_ref[n]
        fetch_a(word, a_refs, a_buf.at[slot], a_sem.at[slot])
        fetch_block(part_of(word), at_of(word), b_refs, b_buf.at[slot], b_sem.at[slot])

    for n in range(AHEAD):

        @pl.when(n < count)
        def _():
            fetch(n)

    meanwhile()

    def step(n, carry):
        slot = n % AHEAD
        pltpu.make_async_copy(a_refs[0].at[0], a_buf.at[slot], a_sem.at[slot]).wait()
        pltpu.make_async_copy(b_refs[0].at[0], b_buf.at[slot], b_sem.at[slot]).wait()
        acc[c_of(list_ref[n])] += block_product(a_buf[slot], b_buf[slot])

        @pl.when(n + AHEAD < count)
        def _():
            fetch(n + AHEAD)

        return carry

    lax.fori_loop(0, count, step, 0)


def all_kernel(parts, list_ref, *rest):
    a_refs, b_refs = rest[:A_PARTS], rest[A_PARTS:parts]
    _, out_ref, acc, c_sem, touched, *buffers = rest[parts:]
    slots = acc.shape[0]

    def stored(c):
        return pltpu.make_async_copy(acc.at[c], out_ref.at[c], c_sem.at[c])

    def meanwhile():
        for c in range(slots):
            touched[c] = 0

        def mark(n, carry):
            touched[c_of(list_ref[n])] = 1
            return carry

        lax.fori_loop(0, list_ref[LIST], mark, 0)
        acc[...] = jnp.zeros_like(acc)

    multiply_listed(list_ref, a_refs, b_refs, acc, *buffers, meanwhile)
    for c in range(slots):
        pl.when(touched[c] == 1)(lambda c=c: stored(c).start())
    for c in range(slots):
        pl.when(touched[c] == 1)(lambda c=c: stored(c).wait())


def add_listed(list_ref, a_refs, b_refs, total_ref, out_ref, acc, c_sem, stage, *buffers):
    count = list_ref[LIST]

    def touched(was, act):
        def step(n, carry):
            c = c_of(list_ref[n])

            @pl.when(stage[c] == was)
            def _():
                stage[c] = was + 1
                act(c)

            return carry

        lax.fori_loop(0, count, step, 0)

    def fetched(c):
        return pltpu.make_async_copy(total_ref.at[c], acc.at[c], c_sem.at[c])

    def stored(c):
        return pltpu.make_async_copy(acc.at[c], out_ref.at[c], c_sem.at[c])

    for c in range(acc.shape[0]):
        stage[c] = 0

    def meanwhile():
        touched(0, lambda c: fetched(c).start())
        touched(1, lambda c: fetched(c).wait())

    multiply_listed(list_ref, a_refs, b_refs, acc, *buffers, meanwhile)
    touched(2, lambda c: stored(c).start())
    touched(3, lambda c: stored(c).wait())


def rest_kernel(parts, me_ref, turn_ref, info_ref, *rest):
    a_refs, b_refs = rest[:A_PARTS], rest[A_PARTS:parts]
    total_ref, out_ref, rest_list, *buffers = rest[parts:]
    extract(entries_of(info_ref, me_ref, turn_ref[0])[1], rest_list)
    add_listed(rest_list, a_refs, b_refs, total_ref, out_ref, *buffers)


def products(kernel, leading, a_parts, b_parts, total, slots, own_list=False):
    size = a_parts[0].shape[-1]
    parts = len(a_parts) + len(b_parts)
    smem = pl.BlockSpec(memory_space=pltpu.SMEM)
    vmem = pl.BlockSpec(memory_space=pltpu.VMEM)
    hbm = pl.BlockSpec(memory_space=pltpu.HBM)
    operands = [*leading, *a_parts, *b_parts] + ([] if total is None else [total])
    return pl.pallas_call(
        functools.partial(kernel, parts),
        in_specs=[smem if x.ndim == 1 else vmem for x in leading]
        + [pl.BlockSpec(memory_space=pl.ANY)] * parts
        + ([] if total is None else [hbm]),
        out_specs=hbm,
        out_shape=jax.ShapeDtypeStruct((slots, size, size), jnp.float32),
        scratch_shapes=([pltpu.SMEM((LIST + 1,), jnp.int32)] if own_list else [])
        + [
            pltpu.VMEM((slots, size, size), jnp.float32),
            pltpu.SemaphoreType.DMA((slots,)),
            pltpu.SMEM((slots,), jnp.int32),
            pltpu.VMEM((AHEAD, size, size), jnp.float32),
            pltpu.VMEM((AHEAD, size, size), jnp.float32),
            pltpu.SemaphoreType.DMA((AHEAD,)),
            pltpu.SemaphoreType.DMA((AHEAD,)),
        ],
        input_output_aliases={} if total is None else {len(operands) - 1: 0},
        compiler_params=pltpu.CompilerParams(vmem_limit_bytes=VMEM_LIMIT),
        cost_estimate=pl.CostEstimate(
            flops=8 * 3 * 2 * size**3, bytes_accessed=24 * size * size * 4, transcendentals=0
        ),
        name="products",
    )(*operands)


def to_row(block, rows, there):
    return lax.ppermute(block, "row", [(i, there(i)) for i in range(rows)])


def on_z(i):
    return (i & 9) | ((i + 2) & 6)


def back_z(i):
    return (i & 9) | ((i - 2) & 6)


def moved(block, there, columns):
    return lax.ppermute(block, COL, [(i, there(i)) for i in range(columns)])


def pair_kernel(tile_ref, beside_ref, _, pair_ref, __, sems):
    n = tile_ref.shape[0]
    copies = [
        pltpu.make_async_copy(tile_ref, pair_ref.at[pl.ds(0, n)], sems.at[0]),
        pltpu.make_async_copy(beside_ref, pair_ref.at[pl.ds(n, n)], sems.at[1]),
    ]
    for copy in copies:
        copy.start()
    for copy in copies:
        copy.wait()


def paired(tile, beside, passing):
    n, size = tile.shape[0], tile.shape[-1]
    anywhere = pl.BlockSpec(memory_space=pl.ANY)
    return pl.pallas_call(
        pair_kernel,
        in_specs=[anywhere] * 3,
        out_specs=[pl.BlockSpec(memory_space=pltpu.VMEM), anywhere],
        out_shape=[
            jax.ShapeDtypeStruct((2 * n, size, size), tile.dtype),
            jax.ShapeDtypeStruct(passing.shape, passing.dtype),
        ],
        scratch_shapes=[pltpu.SemaphoreType.DMA((2,))],
        input_output_aliases={2: 1},
        compiler_params=pltpu.CompilerParams(vmem_limit_bytes=4 << 20),
        name="pair",
    )(tile, beside, passing)


def hold_kernel(*refs):
    pass


def held_for(arrays, later):
    anywhere = pl.BlockSpec(memory_space=pl.ANY)
    return pl.pallas_call(
        hold_kernel,
        in_specs=[anywhere] * (len(arrays) + len(later)),
        out_specs=[anywhere] * len(arrays),
        out_shape=[jax.ShapeDtypeStruct(x.shape, x.dtype) for x in arrays],
        input_output_aliases={i: i for i in range(len(arrays))},
        compiler_params=pltpu.CompilerParams(vmem_limit_bytes=1 << 20),
        name="hold",
    )(*arrays, *later)


def among(held, bits, rows, columns):
    me = lax.axis_index("row") * columns + lax.axis_index(COL)
    group = jnp.zeros((2 ** len(bits),) + held.shape, held.dtype)
    for move in range(2 ** len(bits)):
        flip = sum(((move >> n) & 1) << bit for n, bit in enumerate(bits))
        got = held
        if move:
            pairs = [(i ^ flip, i) for i in range(rows * columns)]
            got = lax.ppermute(held, ("row", *COL), pairs)
        spot = sum((((me ^ flip) >> bit) & 1) << n for n, bit in enumerate(bits))
        group = lax.dynamic_update_index_in_dim(group, got, spot, 0)
    return group


def per_device(a_blocks, a_index, b_blocks, b_index, c_index):
    rows = lax.axis_size("row")
    columns = lax.axis_size(COL)
    row = lax.axis_index("row")
    me = jnp.stack([row, lax.axis_index(COL)])
    hold = columns // rows
    sa, sb, sc = a_blocks.shape[2], b_blocks.shape[3], c_index.shape[2]
    held = hold * sb
    size = a_blocks.shape[-1]

    own = b_blocks[0, 0].reshape(held, size, size)
    behind = to_row(own, rows, lambda i: (i + 2) % rows)
    ahead = to_row(own, rows, lambda i: (i - 2) % rows)
    near = [own, behind, ahead]

    blank = jnp.full((8 - sa,), -1, jnp.int32)
    mine = jnp.concatenate([a_index[0, 0], blank, b_index[0, 0].reshape(-1), c_index[0, 0]])
    spots = among(jnp.pad(mine, (0, 128 - mine.shape[0])), (5, 6), rows, columns)
    spots = among(spots, (1, 2), rows, columns)
    tile = a_blocks[0, 0]
    pair, spots = paired(tile, moved(tile, lambda i: i ^ 8, columns), spots)
    spots = among(spots, (3,), rows, columns)
    spots = among(spots, (4,), rows, columns)
    spots = among(spots, (0,), rows, columns).reshape(rows * columns, 128)
    a_behind = moved(pair, on_z, columns)
    a_ahead = moved(pair, back_z, columns)

    sends = [
        (FAR, 3, lambda i: ((i + 2) & 7) ^ 1),
        (FAR, 2, lambda i: (i - 2) & 7),
        (NEAR, 1, lambda i: i ^ 1),
    ]
    pack_list, info, maps = plan(me, spots, sends)
    packed = pack(pack_list, near, [n for n, *_ in sends])

    far_other, far_own, cross = [
        to_row(block, rows, there) for block, (*_, there) in zip(packed, sends)
    ]

    over, product_list, zeros = overflow(me, info, spots, maps, sc, size)
    (a_behind,) = held_for([a_behind], [info])
    a_far = moved(a_behind, on_z, columns)
    (a_far,) = held_for([a_far], [far_other, far_own, cross, over])
    a_mine = [pair, a_behind, a_ahead, a_far]
    a_parts = a_mine + [moved(block, lambda i: i ^ 1, columns) for block in a_mine]

    b_parts = near + [cross, far_own, far_other]
    total = products(all_kernel, [product_list], a_parts, b_parts, zeros, sc)

    turns = over[0]

    def again(state):
        turn, total = state
        listing = relist(me, turn[None], info, sends)
        packed = pack(listing, near, [n for n, *_ in sends])
        far_other, far_own, cross = [
            to_row(block, rows, there) for block, (*_, there) in zip(packed, sends)
        ]
        blocks = [cross, far_own, far_other]
        leading = [me, turn[None], info]
        total = products(rest_kernel, leading, a_parts, blocks, total, sc, own_list=True)
        return turn + 1, total

    _, total = lax.while_loop(lambda state: state[0] <= turns, again, (jnp.int32(1), total))
    return total[None, None]


def solution(mesh):
    rows, columns = mesh.devices.shape
    mesh = Mesh(mesh.devices.reshape(rows, 2, columns // 4, 2), ("row", *COL))
    in_specs = (
        P("row", COL, None, None, None),
        P("row", COL, None),
        P("row", COL, None, None, None, None),
        P("row", COL, None, None),
        P("row", COL, None),
    )
    out_specs = P("row", COL, None, None, None)
    return jax.shard_map(
        per_device, mesh=mesh, in_specs=in_specs, out_specs=out_specs, check_vma=False
    )
```

```python
import functools

import jax
import jax.numpy as jnp
from jax import lax
from jax.experimental import pallas as pl
from jax.experimental.pallas import tpu as pltpu
from jax.sharding import Mesh
from jax.sharding import PartitionSpec as P

SA = 4
PK = 8
NBD = 8
NEAR = 6
FAR = 3
COL = ("x_lo", "z", "core")
VMEM_LIMIT = 8 << 20
A_PARTS = 8
LIST = 512
AHEAD = 8


def matmul(a, b):
    return jnp.dot(a.astype(jnp.bfloat16), b, preferred_element_type=jnp.float32)


def lands_at(a_line, b):
    meet = (a_line >= 0) & (b >= 0) & ((a_line & (PK - 1)) == (b >> 3))
    return jnp.where(meet, (a_line >> 3) * NBD + (b & (NBD - 1)), -2)


def needed(a, b, c):
    need = jnp.zeros(b.shape, jnp.bool_)
    for s in range(SA):
        lands = lands_at(a[s : s + 1], b)
        for n in range(c.shape[0]):
            need = need | (lands == c[n : n + 1])
    return need


def lane_facts(shape, axis=1):
    lane = lax.broadcasted_iota(jnp.int32, shape, axis)
    r, p = lane >> 4, lane & 15
    owner = p >> 1
    far = (((owner >> 1) - (r >> 1)) & 3) == 2
    way = ((owner ^ r) & 1) + jnp.where(far, 2, 0)
    return r, p, owner, way


def code(a_slot, part, at, c_slot):
    return ((a_slot * 16 + part) * 128 + at) * 16 + c_slot


def a_of(word):
    return word >> 15


def part_of(word):
    return (word >> 11) & 15


def at_of(word):
    return (word >> 4) & 127


def c_of(word):
    return word & 15


def fetch_a(word, a_refs, dst, sem):
    a = a_of(word)
    fetch_block(a >> 3, a & 7, a_refs, dst, sem)


def fetch_block(part, at, refs, dst, sem):
    for i, ref in enumerate(refs):

        def start(ref=ref):
            pltpu.make_async_copy(ref.at[at], dst, sem).start()

        if len(refs) == 1:
            start()
        else:
            pl.when(part == i)(start)


def make_maps(maps_ref):
    shape = maps_ref.shape[1:]
    lane = lax.broadcasted_iota(jnp.int32, shape, 1)
    down = lax.broadcasted_iota(jnp.int32, shape, 0)
    r, p, owner, way = lane_facts(shape)
    r_down, p_down, _, way_down = lane_facts(shape, 0)
    holder = (p_down == 0) & (r_down == owner)
    alike = (r == r_down) & (way == way_down)
    y, xh, xl, z, core = lane >> 5, (lane >> 4) & 1, (lane >> 3) & 1, (lane >> 1) & 3, lane & 1
    listed_at = (((core * 2 + xh) * 2 + xl) * 4 + z) * 4 + y
    for n, flags in enumerate(
        [
            holder & ((p & 1) == 0),
            holder & ((p & 1) == 1),
            (p_down == 0) & (r == r_down),
            alike,
            alike & (down < lane),
            down == listed_at,
        ]
    ):
        maps_ref[n] = jnp.where(flags, 1.0, 0.0).astype(jnp.bfloat16)


def positions(spots_ref, maps_ref):
    spots = spots_ref[...].astype(jnp.float32).astype(jnp.bfloat16)
    return lax.dot_general(
        spots, maps_ref[5], (((0,), (0,)), ((), ())), preferred_element_type=jnp.float32
    )


def list_sends(sends, row, order, turn, pack_list):
    r, p, owner, _ = lane_facts(order.shape)
    t = lax.broadcasted_iota(jnp.int32, order.shape, 0)
    steps = ((owner >> 1) - (row >> 1)) & 3
    part = jnp.where(steps == 0, 0, jnp.where(steps == 3, 1, 2))
    word = (part * 16 + (p & 1) * 8 + t).astype(jnp.float32)
    n = 0
    for slots, which, there in sends:
        for e in range(slots):
            hit = (order == which * 128 + turn * slots + e) & (r == there(row))
            pack_list[n] = jnp.max(jnp.where(hit, word, -1.0)).astype(jnp.int32)
            n += 1


def relist_kernel(sends, me_ref, turn_ref, info_ref, pack_list):
    list_sends(sends, me_ref[0], info_ref[32:40], turn_ref[0], pack_list)


def relist(me, turn, info, sends):
    smem = pl.BlockSpec(memory_space=pltpu.SMEM)
    return pl.pallas_call(
        functools.partial(relist_kernel, sends),
        in_specs=[smem, smem, pl.BlockSpec(memory_space=pltpu.VMEM)],
        out_specs=smem,
        out_shape=jax.ShapeDtypeStruct((sum(n for n, *_ in sends),), jnp.int32),
        compiler_params=pltpu.CompilerParams(vmem_limit_bytes=4 << 20),
        name="relist",
    )(me, turn, info)


def plan_kernel(sends, me_ref, spots_ref, pack_list, info_ref, maps_ref):
    row, column = me_ref[0], me_ref[1]
    make_maps(maps_ref)
    held = positions(spots_ref, maps_ref)
    a = held[:8].astype(jnp.int32)
    turned = pltpu.roll(held[8:40], (128 - column) & 127, 1)
    b = matmul(turned[:8], maps_ref[0]) + matmul(turned[8:16], maps_ref[1])
    b = b.astype(jnp.int32)
    c = matmul(turned[16:32], maps_ref[2]).astype(jnp.int32)
    need = needed(a, b, c)

    r, p, owner, way = lane_facts(b.shape)
    t = lax.broadcasted_iota(jnp.int32, b.shape, 0)
    flags = jnp.where(need, 1.0, 0.0)
    alike = matmul(flags, maps_ref[3])
    upto = alike
    for step in (1, 2, 4):
        upto = upto + jnp.where(t >= step, pltpu.roll(upto, step, 0), 0.0)
    rank = (upto - alike + matmul(flags, maps_ref[4])).astype(jnp.int32)
    order = jnp.where(need, way * 128 + rank, -1)

    list_sends(sends, row, order, 0, pack_list)
    info_ref[0:8] = a
    info_ref[8:16] = b
    info_ref[16:32] = c
    info_ref[32:40] = order


def plan(me, spots, sends):
    smem = pl.BlockSpec(memory_space=pltpu.SMEM)
    vmem = pl.BlockSpec(memory_space=pltpu.VMEM)
    return pl.pallas_call(
        functools.partial(plan_kernel, sends),
        in_specs=[smem, vmem],
        out_specs=[smem, vmem, vmem],
        out_shape=[
            jax.ShapeDtypeStruct((sum(n for n, *_ in sends),), jnp.int32),
            jax.ShapeDtypeStruct((40, 128), jnp.int32),
            jax.ShapeDtypeStruct((6, 128, 128), jnp.bfloat16),
        ],
        compiler_params=pltpu.CompilerParams(vmem_limit_bytes=4 << 20),
        name="plan",
    )(me, spots)


def pack_kernel(sizes, list_ref, *rest):
    near, packed, sems = rest[:3], rest[3:-1], rest[-1]
    places = [(i, e) for i, size in enumerate(sizes) for e in range(size)]
    for n, (i, e) in enumerate(places):
        word = list_ref[n]

        @pl.when(word >= 0)
        def _():
            fetch_block(word >> 4, word & 15, near, packed[i].at[e], sems.at[n])

    for n, (i, e) in enumerate(places):

        @pl.when(list_ref[n] >= 0)
        def _():
            pltpu.make_async_copy(near[0].at[0], packed[i].at[e], sems.at[n]).wait()


def pack(listing, near, sizes):
    size = near[0].shape[-1]
    return pl.pallas_call(
        functools.partial(pack_kernel, sizes),
        in_specs=[pl.BlockSpec(memory_space=pltpu.SMEM)]
        + [pl.BlockSpec(memory_space=pl.ANY)] * 3,
        out_specs=[pl.BlockSpec(memory_space=pltpu.VMEM)] * len(sizes),
        scratch_shapes=[pltpu.SemaphoreType.DMA((sum(sizes),))],
        out_shape=[jax.ShapeDtypeStruct((n, size, size), jnp.float32) for n in sizes],
        compiler_params=pltpu.CompilerParams(vmem_limit_bytes=4 << 20),
        name="pack",
    )(listing, *near)


def overflow_kernel(
    me_ref, info_ref, spots_ref, maps_ref, over_ref, product_list, zeros_ref, zero, sem
):
    zero[...] = jnp.zeros_like(zero)
    stores = [pltpu.make_async_copy(zero, zeros_ref.at[c], sem.at[c]) for c in range(sem.shape[0])]
    for store in stores:
        store.start()
    extract(entries_of(info_ref, me_ref)[0], product_list)
    held = positions(spots_ref, maps_ref)
    a = held[:8].astype(jnp.int32)
    turned = [held[8:40]] + [pltpu.roll(held[8:40], 128 - q, 1) for q in range(1, 16)]
    b = matmul(jnp.concatenate([x[:8] for x in turned]), maps_ref[0])
    b = b + matmul(jnp.concatenate([x[8:16] for x in turned]), maps_ref[1])
    b = b.astype(jnp.int32)
    c = matmul(jnp.concatenate([x[16:32] for x in turned]), maps_ref[2]).astype(jnp.int32)
    flags = [
        jnp.where(needed(a, b[q * 8 : q * 8 + 8], c[q * 16 : q * 16 + 16]), 1.0, 0.0)
        for q in range(16)
    ]
    alike = matmul(jnp.concatenate(flags), maps_ref[3])
    most = jnp.sum(alike[:8], axis=0, keepdims=True)
    for q in range(1, 16):
        most = jnp.maximum(most, jnp.sum(alike[q * 8 : q * 8 + 8], axis=0, keepdims=True))
    *_, way = lane_facts(most.shape)
    slots = jnp.where(way == 0, 128, jnp.where(way == 1, NEAR, FAR))
    slots = slots.astype(jnp.float32)
    turns = sum(jnp.where(most > k * slots, 1.0, 0.0) for k in range(1, 17))
    over_ref[0] = jnp.max(turns).astype(jnp.int32)
    for store in stores:
        store.wait()


def overflow(me, info, spots, maps, slots, size):
    smem = pl.BlockSpec(memory_space=pltpu.SMEM)
    vmem = pl.BlockSpec(memory_space=pltpu.VMEM)
    return pl.pallas_call(
        overflow_kernel,
        in_specs=[smem, vmem, vmem, vmem],
        out_specs=[smem, smem, pl.BlockSpec(memory_space=pltpu.HBM)],
        out_shape=[
            jax.ShapeDtypeStruct((1,), jnp.int32),
            jax.ShapeDtypeStruct((LIST + 1,), jnp.int32),
            jax.ShapeDtypeStruct((slots, size, size), jnp.float32),
        ],
        scratch_shapes=[pltpu.VMEM((size, size), jnp.float32), pltpu.SemaphoreType.DMA((slots,))],
        compiler_params=pltpu.CompilerParams(vmem_limit_bytes=4 << 20),
        cost_estimate=pl.CostEstimate(flops=10**9, bytes_accessed=10**5, transcendentals=0),
        name="overflow",
    )(me, info, spots, maps)


def halves(x):
    high = x.astype(jnp.bfloat16)
    return high, (x - high.astype(jnp.float32)).astype(jnp.bfloat16)


def block_product(a, b):
    a_high, a_low = halves(a)
    b_high, b_low = halves(b)
    dot = functools.partial(jnp.dot, preferred_element_type=jnp.float32)
    return dot(a_high, b_high) + (dot(a_high, b_low) + dot(a_low, b_high))


def extract(entries, list_ref):
    def more(state):
        n, word, left = state
        list_ref[n] = word.astype(jnp.int32)
        left = jnp.where(left == word, -1.0, left)
        return n + 1, jnp.max(left), left

    n, *_ = lax.while_loop(
        lambda state: state[1] >= 0, more, (jnp.int32(0), jnp.max(entries), entries)
    )
    list_ref[LIST] = n


def entries_of(info_ref, me_ref, turn=1):
    row, column = me_ref[0], me_ref[1]
    b, c, order = info_ref[8:16], info_ref[16:32], info_ref[32:40]
    r, p, owner, way = lane_facts(b.shape)
    t = lax.broadcasted_iota(jnp.int32, b.shape, 0)
    rank = order & 127
    steps = ((owner >> 1) - (row >> 1)) & 3
    part = jnp.where(steps == 0, 0, jnp.where(steps == 3, 1, 2))
    slots = jnp.where(way == 1, NEAR, FAR)
    sent = (way > 0) & (rank < slots)
    at = rank - turn * slots
    later = (way > 0) & (at >= 0) & (at < slots)
    along = ((p >> 1) - (column >> 1)) & 3
    beside = ((p ^ column) >> 3) & 1
    a_part = jnp.where(along == 0, 0, jnp.where(along == 3, 1, jnp.where(along == 1, 2, 3)))
    a_at = (a_part + 4 * ((p ^ column) & 1)) * 8 + beside * SA
    found = [[], []]
    for s in range(SA):
        lands = lands_at(info_ref[s : s + 1], b)
        c_slot = jnp.full(b.shape, -1, jnp.int32)
        for n in range(c.shape[0]):
            c_slot = jnp.where(lands == c[n : n + 1], n, c_slot)
        live = (c_slot >= 0) & (r == row)
        a_slot = a_at + s
        at_hand = jnp.where(
            way == 0,
            code(a_slot, part, (p & 1) * 8 + t, c_slot),
            code(a_slot, 2 + way, rank, c_slot),
        )
        in_turn = code(a_slot, (way - 1) & 3, at, c_slot)
        found[0].append(jnp.where(live & ((way == 0) | sent), at_hand, -1).astype(jnp.float32))
        found[1].append(jnp.where(live & later, in_turn, -1).astype(jnp.float32))
    return [jnp.concatenate(x) for x in found]


def multiply_listed(list_ref, a_refs, b_refs, acc, a_buf, b_buf, a_sem, b_sem, meanwhile):
    count = list_ref[LIST]

    def fetch(n):
        slot = n % AHEAD
        word = list_ref[n]
        fetch_a(word, a_refs, a_buf.at[slot], a_sem.at[slot])
        fetch_block(part_of(word), at_of(word), b_refs, b_buf.at[slot], b_sem.at[slot])

    for n in range(AHEAD):

        @pl.when(n < count)
        def _():
            fetch(n)

    meanwhile()

    def step(n, carry):
        slot = n % AHEAD
        pltpu.make_async_copy(a_refs[0].at[0], a_buf.at[slot], a_sem.at[slot]).wait()
        pltpu.make_async_copy(b_refs[0].at[0], b_buf.at[slot], b_sem.at[slot]).wait()
        acc[c_of(list_ref[n])] += block_product(a_buf[slot], b_buf[slot])

        @pl.when(n + AHEAD < count)
        def _():
            fetch(n + AHEAD)

        return carry

    lax.fori_loop(0, count, step, 0)


def all_kernel(parts, list_ref, *rest):
    a_refs, b_refs = rest[:A_PARTS], rest[A_PARTS:parts]
    _, out_ref, acc, c_sem, touched, *buffers = rest[parts:]
    slots = acc.shape[0]

    def stored(c):
        return pltpu.make_async_copy(acc.at[c], out_ref.at[c], c_sem.at[c])

    def meanwhile():
        for c in range(slots):
            touched[c] = 0

        def mark(n, carry):
            touched[c_of(list_ref[n])] = 1
            return carry

        lax.fori_loop(0, list_ref[LIST], mark, 0)
        acc[...] = jnp.zeros_like(acc)

    multiply_listed(list_ref, a_refs, b_refs, acc, *buffers, meanwhile)
    for c in range(slots):
        pl.when(touched[c] == 1)(lambda c=c: stored(c).start())
    for c in range(slots):
        pl.when(touched[c] == 1)(lambda c=c: stored(c).wait())


def add_listed(list_ref, a_refs, b_refs, total_ref, out_ref, acc, c_sem, stage, *buffers):
    count = list_ref[LIST]

    def touched(was, act):
        def step(n, carry):
            c = c_of(list_ref[n])

            @pl.when(stage[c] == was)
            def _():
                stage[c] = was + 1
                act(c)

            return carry

        lax.fori_loop(0, count, step, 0)

    def fetched(c):
        return pltpu.make_async_copy(total_ref.at[c], acc.at[c], c_sem.at[c])

    def stored(c):
        return pltpu.make_async_copy(acc.at[c], out_ref.at[c], c_sem.at[c])

    for c in range(acc.shape[0]):
        stage[c] = 0

    def meanwhile():
        touched(0, lambda c: fetched(c).start())
        touched(1, lambda c: fetched(c).wait())

    multiply_listed(list_ref, a_refs, b_refs, acc, *buffers, meanwhile)
    touched(2, lambda c: stored(c).start())
    touched(3, lambda c: stored(c).wait())


def rest_kernel(parts, me_ref, turn_ref, info_ref, *rest):
    a_refs, b_refs = rest[:A_PARTS], rest[A_PARTS:parts]
    total_ref, out_ref, rest_list, *buffers = rest[parts:]
    extract(entries_of(info_ref, me_ref, turn_ref[0])[1], rest_list)
    add_listed(rest_list, a_refs, b_refs, total_ref, out_ref, *buffers)


def products(kernel, leading, a_parts, b_parts, total, slots, own_list=False):
    size = a_parts[0].shape[-1]
    parts = len(a_parts) + len(b_parts)
    smem = pl.BlockSpec(memory_space=pltpu.SMEM)
    vmem = pl.BlockSpec(memory_space=pltpu.VMEM)
    hbm = pl.BlockSpec(memory_space=pltpu.HBM)
    operands = [*leading, *a_parts, *b_parts] + ([] if total is None else [total])
    return pl.pallas_call(
        functools.partial(kernel, parts),
        in_specs=[smem if x.ndim == 1 else vmem for x in leading]
        + [pl.BlockSpec(memory_space=pl.ANY)] * parts
        + ([] if total is None else [hbm]),
        out_specs=hbm,
        out_shape=jax.ShapeDtypeStruct((slots, size, size), jnp.float32),
        scratch_shapes=([pltpu.SMEM((LIST + 1,), jnp.int32)] if own_list else [])
        + [
            pltpu.VMEM((slots, size, size), jnp.float32),
            pltpu.SemaphoreType.DMA((slots,)),
            pltpu.SMEM((slots,), jnp.int32),
            pltpu.VMEM((AHEAD, size, size), jnp.float32),
            pltpu.VMEM((AHEAD, size, size), jnp.float32),
            pltpu.SemaphoreType.DMA((AHEAD,)),
            pltpu.SemaphoreType.DMA((AHEAD,)),
        ],
        input_output_aliases={} if total is None else {len(operands) - 1: 0},
        compiler_params=pltpu.CompilerParams(vmem_limit_bytes=VMEM_LIMIT),
        cost_estimate=pl.CostEstimate(
            flops=8 * 3 * 2 * size**3, bytes_accessed=24 * size * size * 4, transcendentals=0
        ),
        name="products",
    )(*operands)


def to_row(block, rows, there):
    return lax.ppermute(block, "row", [(i, there(i)) for i in range(rows)])


def on_z(i):
    return (i & 9) | ((i + 2) & 6)


def back_z(i):
    return (i & 9) | ((i - 2) & 6)


def moved(block, there, columns):
    return lax.ppermute(block, COL, [(i, there(i)) for i in range(columns)])


def pair_kernel(tile_ref, beside_ref, _, pair_ref, __, sems):
    n = tile_ref.shape[0]
    copies = [
        pltpu.make_async_copy(tile_ref, pair_ref.at[pl.ds(0, n)], sems.at[0]),
        pltpu.make_async_copy(beside_ref, pair_ref.at[pl.ds(n, n)], sems.at[1]),
    ]
    for copy in copies:
        copy.start()
    for copy in copies:
        copy.wait()


def paired(tile, beside, passing):
    n, size = tile.shape[0], tile.shape[-1]
    anywhere = pl.BlockSpec(memory_space=pl.ANY)
    return pl.pallas_call(
        pair_kernel,
        in_specs=[anywhere] * 3,
        out_specs=[pl.BlockSpec(memory_space=pltpu.VMEM), anywhere],
        out_shape=[
            jax.ShapeDtypeStruct((2 * n, size, size), tile.dtype),
            jax.ShapeDtypeStruct(passing.shape, passing.dtype),
        ],
        scratch_shapes=[pltpu.SemaphoreType.DMA((2,))],
        input_output_aliases={2: 1},
        compiler_params=pltpu.CompilerParams(vmem_limit_bytes=4 << 20),
        name="pair",
    )(tile, beside, passing)


def hold_kernel(*refs):
    pass


def held_for(arrays, later):
    anywhere = pl.BlockSpec(memory_space=pl.ANY)
    return pl.pallas_call(
        hold_kernel,
        in_specs=[anywhere] * (len(arrays) + len(later)),
        out_specs=[anywhere] * len(arrays),
        out_shape=[jax.ShapeDtypeStruct(x.shape, x.dtype) for x in arrays],
        input_output_aliases={i: i for i in range(len(arrays))},
        compiler_params=pltpu.CompilerParams(vmem_limit_bytes=1 << 20),
        name="hold",
    )(*arrays, *later)


def among(held, bits, rows, columns):
    me = lax.axis_index("row") * columns + lax.axis_index(COL)
    group = jnp.zeros((2 ** len(bits),) + held.shape, held.dtype)
    for move in range(2 ** len(bits)):
        flip = sum(((move >> n) & 1) << bit for n, bit in enumerate(bits))
        got = held
        if move:
            pairs = [(i ^ flip, i) for i in range(rows * columns)]
            got = lax.ppermute(held, ("row", *COL), pairs)
        spot = sum((((me ^ flip) >> bit) & 1) << n for n, bit in enumerate(bits))
        group = lax.dynamic_update_index_in_dim(group, got, spot, 0)
    return group


def per_device(a_blocks, a_index, b_blocks, b_index, c_index):
    rows = lax.axis_size("row")
    columns = lax.axis_size(COL)
    row = lax.axis_index("row")
    me = jnp.stack([row, lax.axis_index(COL)])
    hold = columns // rows
    sa, sb, sc = a_blocks.shape[2], b_blocks.shape[3], c_index.shape[2]
    held = hold * sb
    size = a_blocks.shape[-1]

    own = b_blocks[0, 0].reshape(held, size, size)
    behind = to_row(own, rows, lambda i: (i + 2) % rows)
    ahead = to_row(own, rows, lambda i: (i - 2) % rows)
    near = [own, behind, ahead]

    blank = jnp.full((8 - sa,), -1, jnp.int32)
    mine = jnp.concatenate([a_index[0, 0], blank, b_index[0, 0].reshape(-1), c_index[0, 0]])
    spots = among(jnp.pad(mine, (0, 128 - mine.shape[0])), (5, 6), rows, columns)
    tile = a_blocks[0, 0]
    pair, spots = paired(tile, moved(tile, lambda i: i ^ 8, columns), spots)
    spots = among(spots, (1, 2), rows, columns)
    spots = among(spots, (3, 4), rows, columns)
    spots = among(spots, (0,), rows, columns).reshape(rows * columns, 128)
    a_behind = moved(pair, on_z, columns)
    a_ahead = moved(pair, back_z, columns)

    sends = [
        (FAR, 3, lambda i: ((i + 2) & 7) ^ 1),
        (FAR, 2, lambda i: (i - 2) & 7),
        (NEAR, 1, lambda i: i ^ 1),
    ]
    pack_list, info, maps = plan(me, spots, sends)
    packed = pack(pack_list, near, [n for n, *_ in sends])

    far_other, far_own, cross = [
        to_row(block, rows, there) for block, (*_, there) in zip(packed, sends)
    ]

    over, product_list, zeros = overflow(me, info, spots, maps, sc, size)
    (a_behind,) = held_for([a_behind], [info])
    a_far = moved(a_behind, on_z, columns)
    (a_far,) = held_for([a_far], [far_other, far_own, cross, over])
    a_mine = [pair, a_behind, a_ahead, a_far]
    a_parts = a_mine + [moved(block, lambda i: i ^ 1, columns) for block in a_mine]

    b_parts = near + [cross, far_own, far_other]
    total = products(all_kernel, [product_list], a_parts, b_parts, zeros, sc)

    turns = over[0]

    def again(state):
        turn, total = state
        listing = relist(me, turn[None], info, sends)
        packed = pack(listing, near, [n for n, *_ in sends])
        far_other, far_own, cross = [
            to_row(block, rows, there) for block, (*_, there) in zip(packed, sends)
        ]
        blocks = [cross, far_own, far_other]
        leading = [me, turn[None], info]
        total = products(rest_kernel, leading, a_parts, blocks, total, sc, own_list=True)
        return turn + 1, total

    _, total = lax.while_loop(lambda state: state[0] <= turns, again, (jnp.int32(1), total))
    return total[None, None]


def solution(mesh):
    rows, columns = mesh.devices.shape
    mesh = Mesh(mesh.devices.reshape(rows, 2, columns // 4, 2), ("row", *COL))
    in_specs = (
        P("row", COL, None, None, None),
        P("row", COL, None),
        P("row", COL, None, None, None, None),
        P("row", COL, None, None),
        P("row", COL, None),
    )
    out_specs = P("row", COL, None, None, None)
    return jax.shard_map(
        per_device, mesh=mesh, in_specs=in_specs, out_specs=out_specs, check_vma=False
    )
```

```python
import functools

import jax
import jax.numpy as jnp
from jax import lax
from jax.experimental import pallas as pl
from jax.experimental.pallas import tpu as pltpu
from jax.sharding import Mesh
from jax.sharding import PartitionSpec as P

SA = 4
PK = 8
NBD = 8
NEAR = 6
FAR = 3
COL = ("x_lo", "z", "core")
VMEM_LIMIT = 8 << 20
A_PARTS = 8
LIST = 512
AHEAD = 8


def matmul(a, b):
    return jnp.dot(a.astype(jnp.bfloat16), b, preferred_element_type=jnp.float32)


def lands_at(a_line, b):
    meet = (a_line >= 0) & (b >= 0) & ((a_line & (PK - 1)) == (b >> 3))
    return jnp.where(meet, (a_line >> 3) * NBD + (b & (NBD - 1)), -2)


def needed(a, b, c):
    need = jnp.zeros(b.shape, jnp.bool_)
    for s in range(SA):
        lands = lands_at(a[s : s + 1], b)
        for n in range(c.shape[0]):
            need = need | (lands == c[n : n + 1])
    return need


def lane_facts(shape, axis=1):
    lane = lax.broadcasted_iota(jnp.int32, shape, axis)
    r, p = lane >> 4, lane & 15
    owner = p >> 1
    far = (((owner >> 1) - (r >> 1)) & 3) == 2
    way = ((owner ^ r) & 1) + jnp.where(far, 2, 0)
    return r, p, owner, way


def code(a_slot, part, at, c_slot):
    return ((a_slot * 16 + part) * 128 + at) * 16 + c_slot


def a_of(word):
    return word >> 15


def part_of(word):
    return (word >> 11) & 15


def at_of(word):
    return (word >> 4) & 127


def c_of(word):
    return word & 15


def fetch_a(word, a_refs, dst, sem):
    a = a_of(word)
    fetch_block(a >> 3, a & 7, a_refs, dst, sem)


def fetch_block(part, at, refs, dst, sem):
    for i, ref in enumerate(refs):

        def start(ref=ref):
            pltpu.make_async_copy(ref.at[at], dst, sem).start()

        if len(refs) == 1:
            start()
        else:
            pl.when(part == i)(start)


def make_maps(maps_ref):
    shape = maps_ref.shape[1:]
    lane = lax.broadcasted_iota(jnp.int32, shape, 1)
    down = lax.broadcasted_iota(jnp.int32, shape, 0)
    r, p, owner, way = lane_facts(shape)
    r_down, p_down, _, way_down = lane_facts(shape, 0)
    holder = (p_down == 0) & (r_down == owner)
    alike = (r == r_down) & (way == way_down)
    y, xh, xl, z, core = lane >> 5, (lane >> 4) & 1, (lane >> 3) & 1, (lane >> 1) & 3, lane & 1
    listed_at = (((core * 2 + xh) * 2 + xl) * 4 + z) * 4 + y
    for n, flags in enumerate(
        [
            holder & ((p & 1) == 0),
            holder & ((p & 1) == 1),
            (p_down == 0) & (r == r_down),
            alike,
            alike & (down < lane),
            down == listed_at,
        ]
    ):
        maps_ref[n] = jnp.where(flags, 1.0, 0.0).astype(jnp.bfloat16)


def positions(spots_ref, maps_ref):
    spots = spots_ref[...].astype(jnp.float32).astype(jnp.bfloat16)
    return lax.dot_general(
        spots, maps_ref[5], (((0,), (0,)), ((), ())), preferred_element_type=jnp.float32
    )


def list_sends(sends, row, order, turn, pack_list):
    r, p, owner, _ = lane_facts(order.shape)
    t = lax.broadcasted_iota(jnp.int32, order.shape, 0)
    steps = ((owner >> 1) - (row >> 1)) & 3
    part = jnp.where(steps == 0, 0, jnp.where(steps == 3, 1, 2))
    word = (part * 16 + (p & 1) * 8 + t).astype(jnp.float32)
    n = 0
    for slots, which, there in sends:
        for e in range(slots):
            hit = (order == which * 128 + turn * slots + e) & (r == there(row))
            pack_list[n] = jnp.max(jnp.where(hit, word, -1.0)).astype(jnp.int32)
            n += 1


def relist_kernel(sends, me_ref, turn_ref, info_ref, pack_list):
    list_sends(sends, me_ref[0], info_ref[32:40], turn_ref[0], pack_list)


def relist(me, turn, info, sends):
    smem = pl.BlockSpec(memory_space=pltpu.SMEM)
    return pl.pallas_call(
        functools.partial(relist_kernel, sends),
        in_specs=[smem, smem, pl.BlockSpec(memory_space=pltpu.VMEM)],
        out_specs=smem,
        out_shape=jax.ShapeDtypeStruct((sum(n for n, *_ in sends),), jnp.int32),
        compiler_params=pltpu.CompilerParams(vmem_limit_bytes=4 << 20),
        name="relist",
    )(me, turn, info)


def plan_kernel(sends, me_ref, spots_ref, pack_list, info_ref, maps_ref):
    row, column = me_ref[0], me_ref[1]
    make_maps(maps_ref)
    held = positions(spots_ref, maps_ref)
    a = held[:8].astype(jnp.int32)
    turned = pltpu.roll(held[8:40], (128 - column) & 127, 1)
    b = matmul(turned[:8], maps_ref[0]) + matmul(turned[8:16], maps_ref[1])
    b = b.astype(jnp.int32)
    c = matmul(turned[16:32], maps_ref[2]).astype(jnp.int32)
    need = needed(a, b, c)

    r, p, owner, way = lane_facts(b.shape)
    t = lax.broadcasted_iota(jnp.int32, b.shape, 0)
    flags = jnp.where(need, 1.0, 0.0)
    alike = matmul(flags, maps_ref[3])
    upto = alike
    for step in (1, 2, 4):
        upto = upto + jnp.where(t >= step, pltpu.roll(upto, step, 0), 0.0)
    rank = (upto - alike + matmul(flags, maps_ref[4])).astype(jnp.int32)
    order = jnp.where(need, way * 128 + rank, -1)

    list_sends(sends, row, order, 0, pack_list)
    info_ref[0:8] = a
    info_ref[8:16] = b
    info_ref[16:32] = c
    info_ref[32:40] = order


def plan(me, spots, sends):
    smem = pl.BlockSpec(memory_space=pltpu.SMEM)
    vmem = pl.BlockSpec(memory_space=pltpu.VMEM)
    return pl.pallas_call(
        functools.partial(plan_kernel, sends),
        in_specs=[smem, vmem],
        out_specs=[smem, vmem, vmem],
        out_shape=[
            jax.ShapeDtypeStruct((sum(n for n, *_ in sends),), jnp.int32),
            jax.ShapeDtypeStruct((40, 128), jnp.int32),
            jax.ShapeDtypeStruct((6, 128, 128), jnp.bfloat16),
        ],
        compiler_params=pltpu.CompilerParams(vmem_limit_bytes=4 << 20),
        name="plan",
    )(me, spots)


def pack_kernel(sizes, list_ref, *rest):
    near, packed, sems = rest[:3], rest[3:-1], rest[-1]
    places = [(i, e) for i, size in enumerate(sizes) for e in range(size)]
    for n, (i, e) in enumerate(places):
        word = list_ref[n]

        @pl.when(word >= 0)
        def _():
            fetch_block(word >> 4, word & 15, near, packed[i].at[e], sems.at[n])

    for n, (i, e) in enumerate(places):

        @pl.when(list_ref[n] >= 0)
        def _():
            pltpu.make_async_copy(near[0].at[0], packed[i].at[e], sems.at[n]).wait()


def pack(listing, near, sizes):
    size = near[0].shape[-1]
    return pl.pallas_call(
        functools.partial(pack_kernel, sizes),
        in_specs=[pl.BlockSpec(memory_space=pltpu.SMEM)]
        + [pl.BlockSpec(memory_space=pl.ANY)] * 3,
        out_specs=[pl.BlockSpec(memory_space=pltpu.VMEM)] * len(sizes),
        scratch_shapes=[pltpu.SemaphoreType.DMA((sum(sizes),))],
        out_shape=[jax.ShapeDtypeStruct((n, size, size), jnp.float32) for n in sizes],
        compiler_params=pltpu.CompilerParams(vmem_limit_bytes=4 << 20),
        name="pack",
    )(listing, *near)


def overflow_kernel(
    me_ref, info_ref, spots_ref, maps_ref, over_ref, product_list, zeros_ref, zero, sem
):
    zero[...] = jnp.zeros_like(zero)
    stores = [pltpu.make_async_copy(zero, zeros_ref.at[c], sem.at[c]) for c in range(sem.shape[0])]
    for store in stores:
        store.start()
    extract(entries_of(info_ref, me_ref)[0], product_list)
    held = positions(spots_ref, maps_ref)
    a = held[:8].astype(jnp.int32)
    turned = [held[8:40]] + [pltpu.roll(held[8:40], 128 - q, 1) for q in range(1, 16)]
    b = matmul(jnp.concatenate([x[:8] for x in turned]), maps_ref[0])
    b = b + matmul(jnp.concatenate([x[8:16] for x in turned]), maps_ref[1])
    b = b.astype(jnp.int32)
    c = matmul(jnp.concatenate([x[16:32] for x in turned]), maps_ref[2]).astype(jnp.int32)
    flags = [
        jnp.where(needed(a, b[q * 8 : q * 8 + 8], c[q * 16 : q * 16 + 16]), 1.0, 0.0)
        for q in range(16)
    ]
    alike = matmul(jnp.concatenate(flags), maps_ref[3])
    most = jnp.sum(alike[:8], axis=0, keepdims=True)
    for q in range(1, 16):
        most = jnp.maximum(most, jnp.sum(alike[q * 8 : q * 8 + 8], axis=0, keepdims=True))
    *_, way = lane_facts(most.shape)
    slots = jnp.where(way == 0, 128, jnp.where(way == 1, NEAR, FAR))
    slots = slots.astype(jnp.float32)
    turns = sum(jnp.where(most > k * slots, 1.0, 0.0) for k in range(1, 17))
    over_ref[0] = jnp.max(turns).astype(jnp.int32)
    for store in stores:
        store.wait()


def overflow(me, info, spots, maps, slots, size):
    smem = pl.BlockSpec(memory_space=pltpu.SMEM)
    vmem = pl.BlockSpec(memory_space=pltpu.VMEM)
    return pl.pallas_call(
        overflow_kernel,
        in_specs=[smem, vmem, vmem, vmem],
        out_specs=[smem, smem, pl.BlockSpec(memory_space=pltpu.HBM)],
        out_shape=[
            jax.ShapeDtypeStruct((1,), jnp.int32),
            jax.ShapeDtypeStruct((LIST + 1,), jnp.int32),
            jax.ShapeDtypeStruct((slots, size, size), jnp.float32),
        ],
        scratch_shapes=[pltpu.VMEM((size, size), jnp.float32), pltpu.SemaphoreType.DMA((slots,))],
        compiler_params=pltpu.CompilerParams(vmem_limit_bytes=4 << 20),
        cost_estimate=pl.CostEstimate(flops=10**9, bytes_accessed=10**5, transcendentals=0),
        name="overflow",
    )(me, info, spots, maps)


def halves(x):
    high = x.astype(jnp.bfloat16)
    return high, (x - high.astype(jnp.float32)).astype(jnp.bfloat16)


def block_product(a, b):
    a_high, a_low = halves(a)
    b_high, b_low = halves(b)
    dot = functools.partial(jnp.dot, preferred_element_type=jnp.float32)
    return dot(a_high, b_high) + (dot(a_high, b_low) + dot(a_low, b_high))


def extract(entries, list_ref):
    def more(state):
        n, word, left = state
        list_ref[n] = word.astype(jnp.int32)
        left = jnp.where(left == word, -1.0, left)
        return n + 1, jnp.max(left), left

    n, *_ = lax.while_loop(
        lambda state: state[1] >= 0, more, (jnp.int32(0), jnp.max(entries), entries)
    )
    list_ref[LIST] = n


def entries_of(info_ref, me_ref, turn=1):
    row, column = me_ref[0], me_ref[1]
    b, c, order = info_ref[8:16], info_ref[16:32], info_ref[32:40]
    r, p, owner, way = lane_facts(b.shape)
    t = lax.broadcasted_iota(jnp.int32, b.shape, 0)
    rank = order & 127
    steps = ((owner >> 1) - (row >> 1)) & 3
    part = jnp.where(steps == 0, 0, jnp.where(steps == 3, 1, 2))
    slots = jnp.where(way == 1, NEAR, FAR)
    sent = (way > 0) & (rank < slots)
    at = rank - turn * slots
    later = (way > 0) & (at >= 0) & (at < slots)
    along = ((p >> 1) - (column >> 1)) & 3
    beside = ((p ^ column) >> 3) & 1
    a_part = jnp.where(along == 0, 0, jnp.where(along == 3, 1, jnp.where(along == 1, 2, 3)))
    a_at = (a_part + 4 * ((p ^ column) & 1)) * 8 + beside * SA
    found = [[], []]
    for s in range(SA):
        lands = lands_at(info_ref[s : s + 1], b)
        c_slot = jnp.full(b.shape, -1, jnp.int32)
        for n in range(c.shape[0]):
            c_slot = jnp.where(lands == c[n : n + 1], n, c_slot)
        live = (c_slot >= 0) & (r == row)
        a_slot = a_at + s
        at_hand = jnp.where(
            way == 0,
            code(a_slot, part, (p & 1) * 8 + t, c_slot),
            code(a_slot, 2 + way, rank, c_slot),
        )
        in_turn = code(a_slot, (way - 1) & 3, at, c_slot)
        found[0].append(jnp.where(live & ((way == 0) | sent), at_hand, -1).astype(jnp.float32))
        found[1].append(jnp.where(live & later, in_turn, -1).astype(jnp.float32))
    return [jnp.concatenate(x) for x in found]


def multiply_listed(list_ref, a_refs, b_refs, acc, a_buf, b_buf, a_sem, b_sem, meanwhile):
    count = list_ref[LIST]

    def fetch(n):
        slot = n % AHEAD
        word = list_ref[n]
        fetch_a(word, a_refs, a_buf.at[slot], a_sem.at[slot])
        fetch_block(part_of(word), at_of(word), b_refs, b_buf.at[slot], b_sem.at[slot])

    for n in range(AHEAD):

        @pl.when(n < count)
        def _():
            fetch(n)

    meanwhile()

    def step(n, carry):
        slot = n % AHEAD
        pltpu.make_async_copy(a_refs[0].at[0], a_buf.at[slot], a_sem.at[slot]).wait()
        pltpu.make_async_copy(b_refs[0].at[0], b_buf.at[slot], b_sem.at[slot]).wait()
        acc[c_of(list_ref[n])] += block_product(a_buf[slot], b_buf[slot])

        @pl.when(n + AHEAD < count)
        def _():
            fetch(n + AHEAD)

        return carry

    lax.fori_loop(0, count, step, 0)


def all_kernel(parts, list_ref, *rest):
    a_refs, b_refs = rest[:A_PARTS], rest[A_PARTS:parts]
    _, out_ref, acc, c_sem, touched, *buffers = rest[parts:]
    slots = acc.shape[0]

    def stored(c):
        return pltpu.make_async_copy(acc.at[c], out_ref.at[c], c_sem.at[c])

    def meanwhile():
        for c in range(slots):
            touched[c] = 0

        def mark(n, carry):
            touched[c_of(list_ref[n])] = 1
            return carry

        lax.fori_loop(0, list_ref[LIST], mark, 0)
        acc[...] = jnp.zeros_like(acc)

    multiply_listed(list_ref, a_refs, b_refs, acc, *buffers, meanwhile)
    for c in range(slots):
        pl.when(touched[c] == 1)(lambda c=c: stored(c).start())
    for c in range(slots):
        pl.when(touched[c] == 1)(lambda c=c: stored(c).wait())


def add_listed(list_ref, a_refs, b_refs, total_ref, out_ref, acc, c_sem, stage, *buffers):
    count = list_ref[LIST]

    def touched(was, act):
        def step(n, carry):
            c = c_of(list_ref[n])

            @pl.when(stage[c] == was)
            def _():
                stage[c] = was + 1
                act(c)

            return carry

        lax.fori_loop(0, count, step, 0)

    def fetched(c):
        return pltpu.make_async_copy(total_ref.at[c], acc.at[c], c_sem.at[c])

    def stored(c):
        return pltpu.make_async_copy(acc.at[c], out_ref.at[c], c_sem.at[c])

    for c in range(acc.shape[0]):
        stage[c] = 0

    def meanwhile():
        touched(0, lambda c: fetched(c).start())
        touched(1, lambda c: fetched(c).wait())

    multiply_listed(list_ref, a_refs, b_refs, acc, *buffers, meanwhile)
    touched(2, lambda c: stored(c).start())
    touched(3, lambda c: stored(c).wait())


def rest_kernel(parts, me_ref, turn_ref, info_ref, *rest):
    a_refs, b_refs = rest[:A_PARTS], rest[A_PARTS:parts]
    total_ref, out_ref, rest_list, *buffers = rest[parts:]
    extract(entries_of(info_ref, me_ref, turn_ref[0])[1], rest_list)
    add_listed(rest_list, a_refs, b_refs, total_ref, out_ref, *buffers)


def products(kernel, leading, a_parts, b_parts, total, slots, own_list=False):
    size = a_parts[0].shape[-1]
    parts = len(a_parts) + len(b_parts)
    smem = pl.BlockSpec(memory_space=pltpu.SMEM)
    vmem = pl.BlockSpec(memory_space=pltpu.VMEM)
    hbm = pl.BlockSpec(memory_space=pltpu.HBM)
    operands = [*leading, *a_parts, *b_parts] + ([] if total is None else [total])
    return pl.pallas_call(
        functools.partial(kernel, parts),
        in_specs=[smem if x.ndim == 1 else vmem for x in leading]
        + [pl.BlockSpec(memory_space=pl.ANY)] * parts
        + ([] if total is None else [hbm]),
        out_specs=hbm,
        out_shape=jax.ShapeDtypeStruct((slots, size, size), jnp.float32),
        scratch_shapes=([pltpu.SMEM((LIST + 1,), jnp.int32)] if own_list else [])
        + [
            pltpu.VMEM((slots, size, size), jnp.float32),
            pltpu.SemaphoreType.DMA((slots,)),
            pltpu.SMEM((slots,), jnp.int32),
            pltpu.VMEM((AHEAD, size, size), jnp.float32),
            pltpu.VMEM((AHEAD, size, size), jnp.float32),
            pltpu.SemaphoreType.DMA((AHEAD,)),
            pltpu.SemaphoreType.DMA((AHEAD,)),
        ],
        input_output_aliases={} if total is None else {len(operands) - 1: 0},
        compiler_params=pltpu.CompilerParams(vmem_limit_bytes=VMEM_LIMIT),
        cost_estimate=pl.CostEstimate(
            flops=8 * 3 * 2 * size**3, bytes_accessed=24 * size * size * 4, transcendentals=0
        ),
        name="products",
    )(*operands)


def to_row(block, rows, there):
    return lax.ppermute(block, "row", [(i, there(i)) for i in range(rows)])


def on_z(i):
    return (i & 9) | ((i + 2) & 6)


def back_z(i):
    return (i & 9) | ((i - 2) & 6)


def moved(block, there, columns):
    return lax.ppermute(block, COL, [(i, there(i)) for i in range(columns)])


def line_kernel(a_ref, b_ref, c_ref, blocks_ref, line_ref, tile_ref, sem):
    copy = pltpu.make_async_copy(blocks_ref, tile_ref, sem.at[0])
    copy.start()
    lane = lax.broadcasted_iota(jnp.int32, line_ref.shape, 1)
    line = jnp.full(line_ref.shape, -1, jnp.int32)
    for n in range(a_ref.shape[0]):
        line = jnp.where(lane == n, a_ref[n], line)
    for h in range(b_ref.shape[0]):
        for t in range(b_ref.shape[1]):
            line = jnp.where(lane == 8 + h * b_ref.shape[1] + t, b_ref[h, t], line)
    for n in range(c_ref.shape[0]):
        line = jnp.where(lane == 24 + n, c_ref[n], line)
    line_ref[...] = line
    copy.wait()


def line_of(a_where, b_where, c_where, blocks):
    smem = pl.BlockSpec(memory_space=pltpu.SMEM)
    vmem = pl.BlockSpec(memory_space=pltpu.VMEM)
    return pl.pallas_call(
        line_kernel,
        in_specs=[smem] * 3 + [pl.BlockSpec(memory_space=pl.ANY)],
        out_specs=[vmem, vmem],
        out_shape=[
            jax.ShapeDtypeStruct((1, 128), jnp.int32),
            jax.ShapeDtypeStruct(blocks.shape, blocks.dtype),
        ],
        scratch_shapes=[pltpu.SemaphoreType.DMA((1,))],
        compiler_params=pltpu.CompilerParams(vmem_limit_bytes=4 << 20),
        name="line",
    )(a_where, b_where, c_where, blocks)


def pair_kernel(tile_ref, beside_ref, _, pair_ref, __, sems):
    n = tile_ref.shape[0]
    copies = [
        pltpu.make_async_copy(tile_ref, pair_ref.at[pl.ds(0, n)], sems.at[0]),
        pltpu.make_async_copy(beside_ref, pair_ref.at[pl.ds(n, n)], sems.at[1]),
    ]
    for copy in copies:
        copy.start()
    for copy in copies:
        copy.wait()


def paired(tile, beside, passing):
    n, size = tile.shape[0], tile.shape[-1]
    anywhere = pl.BlockSpec(memory_space=pl.ANY)
    return pl.pallas_call(
        pair_kernel,
        in_specs=[anywhere] * 3,
        out_specs=[pl.BlockSpec(memory_space=pltpu.VMEM), anywhere],
        out_shape=[
            jax.ShapeDtypeStruct((2 * n, size, size), tile.dtype),
            jax.ShapeDtypeStruct(passing.shape, passing.dtype),
        ],
        scratch_shapes=[pltpu.SemaphoreType.DMA((2,))],
        input_output_aliases={2: 1},
        compiler_params=pltpu.CompilerParams(vmem_limit_bytes=4 << 20),
        name="pair",
    )(tile, beside, passing)


def hold_kernel(*refs):
    pass


def held_for(arrays, later):
    anywhere = pl.BlockSpec(memory_space=pl.ANY)
    return pl.pallas_call(
        hold_kernel,
        in_specs=[anywhere] * (len(arrays) + len(later)),
        out_specs=[anywhere] * len(arrays),
        out_shape=[jax.ShapeDtypeStruct(x.shape, x.dtype) for x in arrays],
        input_output_aliases={i: i for i in range(len(arrays))},
        compiler_params=pltpu.CompilerParams(vmem_limit_bytes=1 << 20),
        name="hold",
    )(*arrays, *later)


def among(held, bits, rows, columns):
    me = lax.axis_index("row") * columns + lax.axis_index(COL)
    group = jnp.zeros((2 ** len(bits),) + held.shape, held.dtype)
    for move in range(2 ** len(bits)):
        flip = sum(((move >> n) & 1) << bit for n, bit in enumerate(bits))
        got = held
        if move:
            pairs = [(i ^ flip, i) for i in range(rows * columns)]
            got = lax.ppermute(held, ("row", *COL), pairs)
        spot = sum((((me ^ flip) >> bit) & 1) << n for n, bit in enumerate(bits))
        group = lax.dynamic_update_index_in_dim(group, got, spot, 0)
    return group


def per_device(a_blocks, a_index, b_blocks, b_index, c_index):
    rows = lax.axis_size("row")
    columns = lax.axis_size(COL)
    row = lax.axis_index("row")
    me = jnp.stack([row, lax.axis_index(COL)])
    hold = columns // rows
    sa, sb, sc = a_blocks.shape[2], b_blocks.shape[3], c_index.shape[2]
    held = hold * sb
    size = a_blocks.shape[-1]

    own = b_blocks[0, 0].reshape(held, size, size)
    behind = to_row(own, rows, lambda i: (i + 2) % rows)
    ahead = to_row(own, rows, lambda i: (i - 2) % rows)
    near = [own, behind, ahead]

    mine, tile = line_of(a_index[0, 0], b_index[0, 0], c_index[0, 0], a_blocks[0, 0])
    spots = among(mine.reshape(128), (5, 6), rows, columns)
    pair, spots = paired(tile, moved(tile, lambda i: i ^ 8, columns), spots)
    spots = among(spots, (1, 2), rows, columns)
    spots = among(spots, (3, 4), rows, columns)
    spots = among(spots, (0,), rows, columns).reshape(rows * columns, 128)
    a_behind = moved(pair, on_z, columns)
    a_ahead = moved(pair, back_z, columns)

    sends = [
        (FAR, 3, lambda i: ((i + 2) & 7) ^ 1),
        (FAR, 2, lambda i: (i - 2) & 7),
        (NEAR, 1, lambda i: i ^ 1),
    ]
    pack_list, info, maps = plan(me, spots, sends)
    packed = pack(pack_list, near, [n for n, *_ in sends])

    far_other, far_own, cross = [
        to_row(block, rows, there) for block, (*_, there) in zip(packed, sends)
    ]

    over, product_list, zeros = overflow(me, info, spots, maps, sc, size)
    (a_behind,) = held_for([a_behind], [info])
    a_far = moved(a_behind, on_z, columns)
    (a_far,) = held_for([a_far], [far_other, far_own, cross, over])
    a_mine = [pair, a_behind, a_ahead, a_far]
    a_parts = a_mine + [moved(block, lambda i: i ^ 1, columns) for block in a_mine]

    b_parts = near + [cross, far_own, far_other]
    total = products(all_kernel, [product_list], a_parts, b_parts, zeros, sc)

    turns = over[0]

    def again(state):
        turn, total = state
        listing = relist(me, turn[None], info, sends)
        packed = pack(listing, near, [n for n, *_ in sends])
        far_other, far_own, cross = [
            to_row(block, rows, there) for block, (*_, there) in zip(packed, sends)
        ]
        blocks = [cross, far_own, far_other]
        leading = [me, turn[None], info]
        total = products(rest_kernel, leading, a_parts, blocks, total, sc, own_list=True)
        return turn + 1, total

    _, total = lax.while_loop(lambda state: state[0] <= turns, again, (jnp.int32(1), total))
    return total[None, None]


def solution(mesh):
    rows, columns = mesh.devices.shape
    mesh = Mesh(mesh.devices.reshape(rows, 2, columns // 4, 2), ("row", *COL))
    in_specs = (
        P("row", COL, None, None, None),
        P("row", COL, None),
        P("row", COL, None, None, None, None),
        P("row", COL, None, None),
        P("row", COL, None),
    )
    out_specs = P("row", COL, None, None, None)
    return jax.shard_map(
        per_device, mesh=mesh, in_specs=in_specs, out_specs=out_specs, check_vma=False
    )
```

```python
import functools

import jax
import jax.numpy as jnp
from jax import lax
from jax.experimental import pallas as pl
from jax.experimental.pallas import tpu as pltpu
from jax.sharding import Mesh
from jax.sharding import PartitionSpec as P

SA = 4
PK = 8
NBD = 8
NEAR = 6
FAR = 3
COL = ("x_lo", "z", "core")
VMEM_LIMIT = 8 << 20
A_PARTS = 8
LIST = 512
AHEAD = 8


def matmul(a, b):
    return jnp.dot(a.astype(jnp.bfloat16), b, preferred_element_type=jnp.float32)


def lands_at(a_line, b):
    meet = (a_line >= 0) & (b >= 0) & ((a_line & (PK - 1)) == (b >> 3))
    return jnp.where(meet, (a_line >> 3) * NBD + (b & (NBD - 1)), -2)


def needed(a, b, c):
    need = jnp.zeros(b.shape, jnp.bool_)
    for s in range(SA):
        lands = lands_at(a[s : s + 1], b)
        for n in range(c.shape[0]):
            need = need | (lands == c[n : n + 1])
    return need


def lane_facts(shape, axis=1):
    lane = lax.broadcasted_iota(jnp.int32, shape, axis)
    r, p = lane >> 4, lane & 15
    owner = p >> 1
    far = (((owner >> 1) - (r >> 1)) & 3) == 2
    way = ((owner ^ r) & 1) + jnp.where(far, 2, 0)
    return r, p, owner, way


def code(a_slot, part, at, c_slot):
    return ((a_slot * 16 + part) * 128 + at) * 16 + c_slot


def a_of(word):
    return word >> 15


def part_of(word):
    return (word >> 11) & 15


def at_of(word):
    return (word >> 4) & 127


def c_of(word):
    return word & 15


def fetch_a(word, a_refs, dst, sem):
    a = a_of(word)
    fetch_block(a >> 3, a & 7, a_refs, dst, sem)


def fetch_block(part, at, refs, dst, sem):
    for i, ref in enumerate(refs):

        def start(ref=ref):
            pltpu.make_async_copy(ref.at[at], dst, sem).start()

        if len(refs) == 1:
            start()
        else:
            pl.when(part == i)(start)


def make_maps(maps_ref):
    shape = maps_ref.shape[1:]
    lane = lax.broadcasted_iota(jnp.int32, shape, 1)
    down = lax.broadcasted_iota(jnp.int32, shape, 0)
    r, p, owner, way = lane_facts(shape)
    r_down, p_down, _, way_down = lane_facts(shape, 0)
    holder = (p_down == 0) & (r_down == owner)
    alike = (r == r_down) & (way == way_down)
    y, xh, xl, z, core = lane >> 5, (lane >> 4) & 1, (lane >> 3) & 1, (lane >> 1) & 3, lane & 1
    listed_at = (((core * 2 + xh) * 2 + xl) * 4 + z) * 4 + y
    for n, flags in enumerate(
        [
            holder & ((p & 1) == 0),
            holder & ((p & 1) == 1),
            (p_down == 0) & (r == r_down),
            alike,
            alike & (down < lane),
            down == listed_at,
        ]
    ):
        maps_ref[n] = jnp.where(flags, 1.0, 0.0).astype(jnp.bfloat16)


def positions(spots_ref, maps_ref):
    spots = spots_ref[...].astype(jnp.float32).astype(jnp.bfloat16)
    return lax.dot_general(
        spots, maps_ref[5], (((0,), (0,)), ((), ())), preferred_element_type=jnp.float32
    )


def list_sends(sends, row, order, turn, pack_list):
    r, p, owner, _ = lane_facts(order.shape)
    t = lax.broadcasted_iota(jnp.int32, order.shape, 0)
    steps = ((owner >> 1) - (row >> 1)) & 3
    part = jnp.where(steps == 0, 0, jnp.where(steps == 3, 1, 2))
    word = (part * 16 + (p & 1) * 8 + t).astype(jnp.float32)
    n = 0
    for slots, which, there in sends:
        for e in range(slots):
            hit = (order == which * 128 + turn * slots + e) & (r == there(row))
            pack_list[n] = jnp.max(jnp.where(hit, word, -1.0)).astype(jnp.int32)
            n += 1


def relist_kernel(sends, me_ref, turn_ref, info_ref, pack_list):
    list_sends(sends, me_ref[0], info_ref[32:40], turn_ref[0], pack_list)


def relist(me, turn, info, sends):
    smem = pl.BlockSpec(memory_space=pltpu.SMEM)
    return pl.pallas_call(
        functools.partial(relist_kernel, sends),
        in_specs=[smem, smem, pl.BlockSpec(memory_space=pltpu.VMEM)],
        out_specs=smem,
        out_shape=jax.ShapeDtypeStruct((sum(n for n, *_ in sends),), jnp.int32),
        compiler_params=pltpu.CompilerParams(vmem_limit_bytes=4 << 20),
        name="relist",
    )(me, turn, info)


def plan_kernel(sends, me_ref, spots_ref, pack_list, info_ref, maps_ref):
    row, column = me_ref[0], me_ref[1]
    make_maps(maps_ref)
    held = positions(spots_ref, maps_ref)
    a = held[:8].astype(jnp.int32)
    turned = pltpu.roll(held[8:40], (128 - column) & 127, 1)
    b = matmul(turned[:8], maps_ref[0]) + matmul(turned[8:16], maps_ref[1])
    b = b.astype(jnp.int32)
    c = matmul(turned[16:32], maps_ref[2]).astype(jnp.int32)
    need = needed(a, b, c)

    r, p, owner, way = lane_facts(b.shape)
    t = lax.broadcasted_iota(jnp.int32, b.shape, 0)
    flags = jnp.where(need, 1.0, 0.0)
    alike = matmul(flags, maps_ref[3])
    upto = alike
    for step in (1, 2, 4):
        upto = upto + jnp.where(t >= step, pltpu.roll(upto, step, 0), 0.0)
    rank = (upto - alike + matmul(flags, maps_ref[4])).astype(jnp.int32)
    order = jnp.where(need, way * 128 + rank, -1)

    list_sends(sends, row, order, 0, pack_list)
    info_ref[0:8] = a
    info_ref[8:16] = b
    info_ref[16:32] = c
    info_ref[32:40] = order


def plan(me, spots, sends):
    smem = pl.BlockSpec(memory_space=pltpu.SMEM)
    vmem = pl.BlockSpec(memory_space=pltpu.VMEM)
    return pl.pallas_call(
        functools.partial(plan_kernel, sends),
        in_specs=[smem, vmem],
        out_specs=[smem, vmem, vmem],
        out_shape=[
            jax.ShapeDtypeStruct((sum(n for n, *_ in sends),), jnp.int32),
            jax.ShapeDtypeStruct((40, 128), jnp.int32),
            jax.ShapeDtypeStruct((6, 128, 128), jnp.bfloat16),
        ],
        compiler_params=pltpu.CompilerParams(vmem_limit_bytes=4 << 20),
        name="plan",
    )(me, spots)


def pack_kernel(sizes, list_ref, *rest):
    near, packed, sems = rest[:3], rest[3:-1], rest[-1]
    places = [(i, e) for i, size in enumerate(sizes) for e in range(size)]
    for n, (i, e) in enumerate(places):
        word = list_ref[n]

        @pl.when(word >= 0)
        def _():
            fetch_block(word >> 4, word & 15, near, packed[i].at[e], sems.at[n])

    for n, (i, e) in enumerate(places):

        @pl.when(list_ref[n] >= 0)
        def _():
            pltpu.make_async_copy(near[0].at[0], packed[i].at[e], sems.at[n]).wait()


def pack(listing, near, sizes):
    size = near[0].shape[-1]
    return pl.pallas_call(
        functools.partial(pack_kernel, sizes),
        in_specs=[pl.BlockSpec(memory_space=pltpu.SMEM)]
        + [pl.BlockSpec(memory_space=pl.ANY)] * 3,
        out_specs=[pl.BlockSpec(memory_space=pltpu.VMEM)] * len(sizes),
        scratch_shapes=[pltpu.SemaphoreType.DMA((sum(sizes),))],
        out_shape=[jax.ShapeDtypeStruct((n, size, size), jnp.float32) for n in sizes],
        compiler_params=pltpu.CompilerParams(vmem_limit_bytes=4 << 20),
        name="pack",
    )(listing, *near)


def overflow_kernel(
    me_ref, info_ref, spots_ref, maps_ref, over_ref, product_list, zeros_ref, zero, sem
):
    zero[...] = jnp.zeros_like(zero)
    stores = [pltpu.make_async_copy(zero, zeros_ref.at[c], sem.at[c]) for c in range(sem.shape[0])]
    for store in stores:
        store.start()
    extract(entries_of(info_ref, me_ref)[0], product_list)
    held = positions(spots_ref, maps_ref)
    a = held[:8].astype(jnp.int32)
    turned = [held[8:40]] + [pltpu.roll(held[8:40], 128 - q, 1) for q in range(1, 16)]
    b = matmul(jnp.concatenate([x[:8] for x in turned]), maps_ref[0])
    b = b + matmul(jnp.concatenate([x[8:16] for x in turned]), maps_ref[1])
    b = b.astype(jnp.int32)
    c = matmul(jnp.concatenate([x[16:32] for x in turned]), maps_ref[2]).astype(jnp.int32)
    flags = [
        jnp.where(needed(a, b[q * 8 : q * 8 + 8], c[q * 16 : q * 16 + 16]), 1.0, 0.0)
        for q in range(16)
    ]
    alike = matmul(jnp.concatenate(flags), maps_ref[3])
    most = jnp.sum(alike[:8], axis=0, keepdims=True)
    for q in range(1, 16):
        most = jnp.maximum(most, jnp.sum(alike[q * 8 : q * 8 + 8], axis=0, keepdims=True))
    *_, way = lane_facts(most.shape)
    slots = jnp.where(way == 0, 128, jnp.where(way == 1, NEAR, FAR))
    slots = slots.astype(jnp.float32)
    turns = sum(jnp.where(most > k * slots, 1.0, 0.0) for k in range(1, 17))
    over_ref[0] = jnp.max(turns).astype(jnp.int32)
    for store in stores:
        store.wait()


def overflow(me, info, spots, maps, slots, size):
    smem = pl.BlockSpec(memory_space=pltpu.SMEM)
    vmem = pl.BlockSpec(memory_space=pltpu.VMEM)
    return pl.pallas_call(
        overflow_kernel,
        in_specs=[smem, vmem, vmem, vmem],
        out_specs=[smem, smem, pl.BlockSpec(memory_space=pltpu.HBM)],
        out_shape=[
            jax.ShapeDtypeStruct((1,), jnp.int32),
            jax.ShapeDtypeStruct((LIST + 1,), jnp.int32),
            jax.ShapeDtypeStruct((slots, size, size), jnp.float32),
        ],
        scratch_shapes=[pltpu.VMEM((size, size), jnp.float32), pltpu.SemaphoreType.DMA((slots,))],
        compiler_params=pltpu.CompilerParams(vmem_limit_bytes=4 << 20),
        cost_estimate=pl.CostEstimate(flops=10**9, bytes_accessed=10**5, transcendentals=0),
        name="overflow",
    )(me, info, spots, maps)


def halves(x):
    high = x.astype(jnp.bfloat16)
    return high, (x - high.astype(jnp.float32)).astype(jnp.bfloat16)


def block_product(a, b):
    a_high, a_low = halves(a)
    b_high, b_low = halves(b)
    dot = functools.partial(jnp.dot, preferred_element_type=jnp.float32)
    return dot(a_high, b_high) + (dot(a_high, b_low) + dot(a_low, b_high))


def extract(entries, list_ref):
    def more(state):
        n, word, left = state
        list_ref[n] = word.astype(jnp.int32)
        left = jnp.where(left == word, -1.0, left)
        return n + 1, jnp.max(left), left

    n, *_ = lax.while_loop(
        lambda state: state[1] >= 0, more, (jnp.int32(0), jnp.max(entries), entries)
    )
    list_ref[LIST] = n


def entries_of(info_ref, me_ref, turn=1):
    row, column = me_ref[0], me_ref[1]
    b, c, order = info_ref[8:16], info_ref[16:32], info_ref[32:40]
    r, p, owner, way = lane_facts(b.shape)
    t = lax.broadcasted_iota(jnp.int32, b.shape, 0)
    rank = order & 127
    steps = ((owner >> 1) - (row >> 1)) & 3
    part = jnp.where(steps == 0, 0, jnp.where(steps == 3, 1, 2))
    slots = jnp.where(way == 1, NEAR, FAR)
    sent = (way > 0) & (rank < slots)
    at = rank - turn * slots
    later = (way > 0) & (at >= 0) & (at < slots)
    along = ((p >> 1) - (column >> 1)) & 3
    beside = ((p ^ column) >> 3) & 1
    a_part = jnp.where(along == 0, 0, jnp.where(along == 3, 1, jnp.where(along == 1, 2, 3)))
    a_at = (a_part + 4 * ((p ^ column) & 1)) * 8 + beside * SA
    found = [[], []]
    for s in range(SA):
        lands = lands_at(info_ref[s : s + 1], b)
        c_slot = jnp.full(b.shape, -1, jnp.int32)
        for n in range(c.shape[0]):
            c_slot = jnp.where(lands == c[n : n + 1], n, c_slot)
        live = (c_slot >= 0) & (r == row)
        a_slot = a_at + s
        at_hand = jnp.where(
            way == 0,
            code(a_slot, part, (p & 1) * 8 + t, c_slot),
            code(a_slot, 2 + way, rank, c_slot),
        )
        in_turn = code(a_slot, (way - 1) & 3, at, c_slot)
        found[0].append(jnp.where(live & ((way == 0) | sent), at_hand, -1).astype(jnp.float32))
        found[1].append(jnp.where(live & later, in_turn, -1).astype(jnp.float32))
    return [jnp.concatenate(x) for x in found]


def multiply_listed(list_ref, a_refs, b_refs, acc, a_buf, b_buf, a_sem, b_sem, meanwhile):
    count = list_ref[LIST]

    def fetch(n):
        slot = n % AHEAD
        word = list_ref[n]
        fetch_a(word, a_refs, a_buf.at[slot], a_sem.at[slot])
        fetch_block(part_of(word), at_of(word), b_refs, b_buf.at[slot], b_sem.at[slot])

    for n in range(AHEAD):

        @pl.when(n < count)
        def _():
            fetch(n)

    meanwhile()

    def step(n, carry):
        slot = n % AHEAD
        pltpu.make_async_copy(a_refs[0].at[0], a_buf.at[slot], a_sem.at[slot]).wait()
        pltpu.make_async_copy(b_refs[0].at[0], b_buf.at[slot], b_sem.at[slot]).wait()
        acc[c_of(list_ref[n])] += block_product(a_buf[slot], b_buf[slot])

        @pl.when(n + AHEAD < count)
        def _():
            fetch(n + AHEAD)

        return carry

    lax.fori_loop(0, count, step, 0)


def all_kernel(parts, list_ref, *rest):
    a_refs, b_refs = rest[:A_PARTS], rest[A_PARTS:parts]
    _, out_ref, acc, c_sem, touched, *buffers = rest[parts:]
    slots = acc.shape[0]

    def stored(c):
        return pltpu.make_async_copy(acc.at[c], out_ref.at[c], c_sem.at[c])

    def meanwhile():
        for c in range(slots):
            touched[c] = 0

        def mark(n, carry):
            touched[c_of(list_ref[n])] = 1
            return carry

        lax.fori_loop(0, list_ref[LIST], mark, 0)
        acc[...] = jnp.zeros_like(acc)

    multiply_listed(list_ref, a_refs, b_refs, acc, *buffers, meanwhile)
    for c in range(slots):
        pl.when(touched[c] == 1)(lambda c=c: stored(c).start())
    for c in range(slots):
        pl.when(touched[c] == 1)(lambda c=c: stored(c).wait())


def add_listed(list_ref, a_refs, b_refs, total_ref, out_ref, acc, c_sem, stage, *buffers):
    count = list_ref[LIST]

    def touched(was, act):
        def step(n, carry):
            c = c_of(list_ref[n])

            @pl.when(stage[c] == was)
            def _():
                stage[c] = was + 1
                act(c)

            return carry

        lax.fori_loop(0, count, step, 0)

    def fetched(c):
        return pltpu.make_async_copy(total_ref.at[c], acc.at[c], c_sem.at[c])

    def stored(c):
        return pltpu.make_async_copy(acc.at[c], out_ref.at[c], c_sem.at[c])

    for c in range(acc.shape[0]):
        stage[c] = 0

    def meanwhile():
        touched(0, lambda c: fetched(c).start())
        touched(1, lambda c: fetched(c).wait())

    multiply_listed(list_ref, a_refs, b_refs, acc, *buffers, meanwhile)
    touched(2, lambda c: stored(c).start())
    touched(3, lambda c: stored(c).wait())


def rest_kernel(parts, me_ref, turn_ref, info_ref, *rest):
    a_refs, b_refs = rest[:A_PARTS], rest[A_PARTS:parts]
    total_ref, out_ref, rest_list, *buffers = rest[parts:]
    extract(entries_of(info_ref, me_ref, turn_ref[0])[1], rest_list)
    add_listed(rest_list, a_refs, b_refs, total_ref, out_ref, *buffers)


def products(kernel, leading, a_parts, b_parts, total, slots, own_list=False):
    size = a_parts[0].shape[-1]
    parts = len(a_parts) + len(b_parts)
    smem = pl.BlockSpec(memory_space=pltpu.SMEM)
    vmem = pl.BlockSpec(memory_space=pltpu.VMEM)
    hbm = pl.BlockSpec(memory_space=pltpu.HBM)
    operands = [*leading, *a_parts, *b_parts] + ([] if total is None else [total])
    return pl.pallas_call(
        functools.partial(kernel, parts),
        in_specs=[smem if x.ndim == 1 else vmem for x in leading]
        + [pl.BlockSpec(memory_space=pl.ANY)] * parts
        + ([] if total is None else [hbm]),
        out_specs=hbm,
        out_shape=jax.ShapeDtypeStruct((slots, size, size), jnp.float32),
        scratch_shapes=([pltpu.SMEM((LIST + 1,), jnp.int32)] if own_list else [])
        + [
            pltpu.VMEM((slots, size, size), jnp.float32),
            pltpu.SemaphoreType.DMA((slots,)),
            pltpu.SMEM((slots,), jnp.int32),
            pltpu.VMEM((AHEAD, size, size), jnp.float32),
            pltpu.VMEM((AHEAD, size, size), jnp.float32),
            pltpu.SemaphoreType.DMA((AHEAD,)),
            pltpu.SemaphoreType.DMA((AHEAD,)),
        ],
        input_output_aliases={} if total is None else {len(operands) - 1: 0},
        compiler_params=pltpu.CompilerParams(vmem_limit_bytes=VMEM_LIMIT),
        cost_estimate=pl.CostEstimate(
            flops=8 * 3 * 2 * size**3, bytes_accessed=24 * size * size * 4, transcendentals=0
        ),
        name="products",
    )(*operands)


def to_row(block, rows, there):
    return lax.ppermute(block, "row", [(i, there(i)) for i in range(rows)])


def on_z(i):
    return (i & 9) | ((i + 2) & 6)


def back_z(i):
    return (i & 9) | ((i - 2) & 6)


def moved(block, there, columns):
    return lax.ppermute(block, COL, [(i, there(i)) for i in range(columns)])


def line_kernel(a_in, b_in, c_in, blocks_ref, line_ref, tile_ref, a_ref, b_ref, c_ref, sem):
    copies = [
        pltpu.make_async_copy(source, target, sem.at[n])
        for n, (source, target) in enumerate(
            [(a_in, a_ref), (b_in, b_ref), (c_in, c_ref), (blocks_ref, tile_ref)]
        )
    ]
    for copy in copies:
        copy.start()
    for copy in copies[:3]:
        copy.wait()
    lane = lax.broadcasted_iota(jnp.int32, line_ref.shape, 1)
    line = jnp.full(line_ref.shape, -1, jnp.int32)
    for n in range(a_ref.shape[0]):
        line = jnp.where(lane == n, a_ref[n], line)
    for h in range(b_ref.shape[0]):
        for t in range(b_ref.shape[1]):
            line = jnp.where(lane == 8 + h * b_ref.shape[1] + t, b_ref[h, t], line)
    for n in range(c_ref.shape[0]):
        line = jnp.where(lane == 24 + n, c_ref[n], line)
    line_ref[...] = line
    copies[3].wait()


def line_of(a_where, b_where, c_where, blocks):
    anywhere = pl.BlockSpec(memory_space=pl.ANY)
    vmem = pl.BlockSpec(memory_space=pltpu.VMEM)
    return pl.pallas_call(
        line_kernel,
        in_specs=[anywhere] * 4,
        out_specs=[vmem, vmem],
        out_shape=[
            jax.ShapeDtypeStruct((1, 128), jnp.int32),
            jax.ShapeDtypeStruct(blocks.shape, blocks.dtype),
        ],
        scratch_shapes=[pltpu.SMEM(x.shape, x.dtype) for x in (a_where, b_where, c_where)]
        + [pltpu.SemaphoreType.DMA((4,))],
        compiler_params=pltpu.CompilerParams(vmem_limit_bytes=4 << 20),
        name="line",
    )(a_where, b_where, c_where, blocks)


def pair_kernel(tile_ref, beside_ref, _, pair_ref, __, sems):
    n = tile_ref.shape[0]
    copies = [
        pltpu.make_async_copy(tile_ref, pair_ref.at[pl.ds(0, n)], sems.at[0]),
        pltpu.make_async_copy(beside_ref, pair_ref.at[pl.ds(n, n)], sems.at[1]),
    ]
    for copy in copies:
        copy.start()
    for copy in copies:
        copy.wait()


def paired(tile, beside, passing):
    n, size = tile.shape[0], tile.shape[-1]
    anywhere = pl.BlockSpec(memory_space=pl.ANY)
    return pl.pallas_call(
        pair_kernel,
        in_specs=[anywhere] * 3,
        out_specs=[pl.BlockSpec(memory_space=pltpu.VMEM), anywhere],
        out_shape=[
            jax.ShapeDtypeStruct((2 * n, size, size), tile.dtype),
            jax.ShapeDtypeStruct(passing.shape, passing.dtype),
        ],
        scratch_shapes=[pltpu.SemaphoreType.DMA((2,))],
        input_output_aliases={2: 1},
        compiler_params=pltpu.CompilerParams(vmem_limit_bytes=4 << 20),
        name="pair",
    )(tile, beside, passing)


def hold_kernel(*refs):
    pass


def held_for(arrays, later):
    anywhere = pl.BlockSpec(memory_space=pl.ANY)
    return pl.pallas_call(
        hold_kernel,
        in_specs=[anywhere] * (len(arrays) + len(later)),
        out_specs=[anywhere] * len(arrays),
        out_shape=[jax.ShapeDtypeStruct(x.shape, x.dtype) for x in arrays],
        input_output_aliases={i: i for i in range(len(arrays))},
        compiler_params=pltpu.CompilerParams(vmem_limit_bytes=1 << 20),
        name="hold",
    )(*arrays, *later)


def among(held, bits, rows, columns):
    me = lax.axis_index("row") * columns + lax.axis_index(COL)
    group = jnp.zeros((2 ** len(bits),) + held.shape, held.dtype)
    for move in range(2 ** len(bits)):
        flip = sum(((move >> n) & 1) << bit for n, bit in enumerate(bits))
        got = held
        if move:
            pairs = [(i ^ flip, i) for i in range(rows * columns)]
            got = lax.ppermute(held, ("row", *COL), pairs)
        spot = sum((((me ^ flip) >> bit) & 1) << n for n, bit in enumerate(bits))
        group = lax.dynamic_update_index_in_dim(group, got, spot, 0)
    return group


def per_device(a_blocks, a_index, b_blocks, b_index, c_index):
    rows = lax.axis_size("row")
    columns = lax.axis_size(COL)
    row = lax.axis_index("row")
    me = jnp.stack([row, lax.axis_index(COL)])
    hold = columns // rows
    sa, sb, sc = a_blocks.shape[2], b_blocks.shape[3], c_index.shape[2]
    held = hold * sb
    size = a_blocks.shape[-1]

    own = b_blocks[0, 0].reshape(held, size, size)
    behind = to_row(own, rows, lambda i: (i + 2) % rows)
    ahead = to_row(own, rows, lambda i: (i - 2) % rows)
    near = [own, behind, ahead]

    mine, tile = line_of(a_index[0, 0], b_index[0, 0], c_index[0, 0], a_blocks[0, 0])
    spots = among(mine.reshape(128), (5, 6), rows, columns)
    pair, spots = paired(tile, moved(tile, lambda i: i ^ 8, columns), spots)
    spots = among(spots, (1, 2), rows, columns)
    spots = among(spots, (3, 4), rows, columns)
    spots = among(spots, (0,), rows, columns).reshape(rows * columns, 128)
    a_behind = moved(pair, on_z, columns)
    a_ahead = moved(pair, back_z, columns)

    sends = [
        (FAR, 3, lambda i: ((i + 2) & 7) ^ 1),
        (FAR, 2, lambda i: (i - 2) & 7),
        (NEAR, 1, lambda i: i ^ 1),
    ]
    pack_list, info, maps = plan(me, spots, sends)
    packed = pack(pack_list, near, [n for n, *_ in sends])

    far_other, far_own, cross = [
        to_row(block, rows, there) for block, (*_, there) in zip(packed, sends)
    ]

    over, product_list, zeros = overflow(me, info, spots, maps, sc, size)
    (a_behind,) = held_for([a_behind], [info])
    a_far = moved(a_behind, on_z, columns)
    (a_far,) = held_for([a_far], [far_other, far_own, cross, over])
    a_mine = [pair, a_behind, a_ahead, a_far]
    a_parts = a_mine + [moved(block, lambda i: i ^ 1, columns) for block in a_mine]

    b_parts = near + [cross, far_own, far_other]
    total = products(all_kernel, [product_list], a_parts, b_parts, zeros, sc)

    turns = over[0]

    def again(state):
        turn, total = state
        listing = relist(me, turn[None], info, sends)
        packed = pack(listing, near, [n for n, *_ in sends])
        far_other, far_own, cross = [
            to_row(block, rows, there) for block, (*_, there) in zip(packed, sends)
        ]
        blocks = [cross, far_own, far_other]
        leading = [me, turn[None], info]
        total = products(rest_kernel, leading, a_parts, blocks, total, sc, own_list=True)
        return turn + 1, total

    _, total = lax.while_loop(lambda state: state[0] <= turns, again, (jnp.int32(1), total))
    return total[None, None]


def solution(mesh):
    rows, columns = mesh.devices.shape
    mesh = Mesh(mesh.devices.reshape(rows, 2, columns // 4, 2), ("row", *COL))
    in_specs = (
        P("row", COL, None, None, None),
        P("row", COL, None),
        P("row", COL, None, None, None, None),
        P("row", COL, None, None),
        P("row", COL, None),
    )
    out_specs = P("row", COL, None, None, None)
    return jax.shard_map(
        per_device, mesh=mesh, in_specs=in_specs, out_specs=out_specs, check_vma=False
    )
```

```python
import functools

import jax
import jax.numpy as jnp
from jax import lax
from jax.experimental import pallas as pl
from jax.experimental.pallas import tpu as pltpu
from jax.sharding import Mesh
from jax.sharding import PartitionSpec as P

SA = 4
PK = 8
NBD = 8
NEAR = 6
FAR = 3
COL = ("x_lo", "z", "core")
VMEM_LIMIT = 8 << 20
A_PARTS = 8
LIST = 512
AHEAD = 16


def matmul(a, b):
    return jnp.dot(a.astype(jnp.bfloat16), b, preferred_element_type=jnp.float32)


def lands_at(a_line, b):
    meet = (a_line >= 0) & (b >= 0) & ((a_line & (PK - 1)) == (b >> 3))
    return jnp.where(meet, (a_line >> 3) * NBD + (b & (NBD - 1)), -2)


def needed(a, b, c):
    need = jnp.zeros(b.shape, jnp.bool_)
    for s in range(SA):
        lands = lands_at(a[s : s + 1], b)
        for n in range(c.shape[0]):
            need = need | (lands == c[n : n + 1])
    return need


def lane_facts(shape, axis=1):
    lane = lax.broadcasted_iota(jnp.int32, shape, axis)
    r, p = lane >> 4, lane & 15
    owner = p >> 1
    far = (((owner >> 1) - (r >> 1)) & 3) == 2
    way = ((owner ^ r) & 1) + jnp.where(far, 2, 0)
    return r, p, owner, way


def code(a_slot, part, at, c_slot):
    return ((a_slot * 16 + part) * 128 + at) * 16 + c_slot


def a_of(word):
    return word >> 15


def part_of(word):
    return (word >> 11) & 15


def at_of(word):
    return (word >> 4) & 127


def c_of(word):
    return word & 15


def fetch_a(word, a_refs, dst, sem):
    a = a_of(word)
    fetch_block(a >> 3, a & 7, a_refs, dst, sem)


def fetch_block(part, at, refs, dst, sem):
    for i, ref in enumerate(refs):

        def start(ref=ref):
            pltpu.make_async_copy(ref.at[at], dst, sem).start()

        if len(refs) == 1:
            start()
        else:
            pl.when(part == i)(start)


def make_maps(maps_ref):
    shape = maps_ref.shape[1:]
    lane = lax.broadcasted_iota(jnp.int32, shape, 1)
    down = lax.broadcasted_iota(jnp.int32, shape, 0)
    r, p, owner, way = lane_facts(shape)
    r_down, p_down, _, way_down = lane_facts(shape, 0)
    holder = (p_down == 0) & (r_down == owner)
    alike = (r == r_down) & (way == way_down)
    y, xh, xl, z, core = lane >> 5, (lane >> 4) & 1, (lane >> 3) & 1, (lane >> 1) & 3, lane & 1
    listed_at = (((core * 2 + xh) * 2 + xl) * 4 + z) * 4 + y
    for n, flags in enumerate(
        [
            holder & ((p & 1) == 0),
            holder & ((p & 1) == 1),
            (p_down == 0) & (r == r_down),
            alike,
            alike & (down < lane),
            down == listed_at,
        ]
    ):
        maps_ref[n] = jnp.where(flags, 1.0, 0.0).astype(jnp.bfloat16)


def positions(spots_ref, maps_ref):
    spots = spots_ref[...].astype(jnp.float32).astype(jnp.bfloat16)
    return lax.dot_general(
        spots, maps_ref[5], (((0,), (0,)), ((), ())), preferred_element_type=jnp.float32
    )


def list_sends(sends, row, order, turn, pack_list):
    r, p, owner, _ = lane_facts(order.shape)
    t = lax.broadcasted_iota(jnp.int32, order.shape, 0)
    steps = ((owner >> 1) - (row >> 1)) & 3
    part = jnp.where(steps == 0, 0, jnp.where(steps == 3, 1, 2))
    word = (part * 16 + (p & 1) * 8 + t).astype(jnp.float32)
    n = 0
    for slots, which, there in sends:
        for e in range(slots):
            hit = (order == which * 128 + turn * slots + e) & (r == there(row))
            pack_list[n] = jnp.max(jnp.where(hit, word, -1.0)).astype(jnp.int32)
            n += 1


def relist_kernel(sends, me_ref, turn_ref, info_ref, pack_list):
    list_sends(sends, me_ref[0], info_ref[32:40], turn_ref[0], pack_list)


def relist(me, turn, info, sends):
    smem = pl.BlockSpec(memory_space=pltpu.SMEM)
    return pl.pallas_call(
        functools.partial(relist_kernel, sends),
        in_specs=[smem, smem, pl.BlockSpec(memory_space=pltpu.VMEM)],
        out_specs=smem,
        out_shape=jax.ShapeDtypeStruct((sum(n for n, *_ in sends),), jnp.int32),
        compiler_params=pltpu.CompilerParams(vmem_limit_bytes=4 << 20),
        name="relist",
    )(me, turn, info)


def plan_kernel(sends, me_ref, spots_ref, pack_list, info_ref, maps_ref):
    row, column = me_ref[0], me_ref[1]
    make_maps(maps_ref)
    held = positions(spots_ref, maps_ref)
    a = held[:8].astype(jnp.int32)
    turned = pltpu.roll(held[8:40], (128 - column) & 127, 1)
    b = matmul(turned[:8], maps_ref[0]) + matmul(turned[8:16], maps_ref[1])
    b = b.astype(jnp.int32)
    c = matmul(turned[16:32], maps_ref[2]).astype(jnp.int32)
    need = needed(a, b, c)

    r, p, owner, way = lane_facts(b.shape)
    t = lax.broadcasted_iota(jnp.int32, b.shape, 0)
    flags = jnp.where(need, 1.0, 0.0)
    alike = matmul(flags, maps_ref[3])
    upto = alike
    for step in (1, 2, 4):
        upto = upto + jnp.where(t >= step, pltpu.roll(upto, step, 0), 0.0)
    rank = (upto - alike + matmul(flags, maps_ref[4])).astype(jnp.int32)
    order = jnp.where(need, way * 128 + rank, -1)

    list_sends(sends, row, order, 0, pack_list)
    info_ref[0:8] = a
    info_ref[8:16] = b
    info_ref[16:32] = c
    info_ref[32:40] = order


def plan(me, spots, sends):
    smem = pl.BlockSpec(memory_space=pltpu.SMEM)
    vmem = pl.BlockSpec(memory_space=pltpu.VMEM)
    return pl.pallas_call(
        functools.partial(plan_kernel, sends),
        in_specs=[smem, vmem],
        out_specs=[smem, vmem, vmem],
        out_shape=[
            jax.ShapeDtypeStruct((sum(n for n, *_ in sends),), jnp.int32),
            jax.ShapeDtypeStruct((40, 128), jnp.int32),
            jax.ShapeDtypeStruct((6, 128, 128), jnp.bfloat16),
        ],
        compiler_params=pltpu.CompilerParams(vmem_limit_bytes=4 << 20),
        name="plan",
    )(me, spots)


def pack_kernel(sizes, list_ref, *rest):
    near, packed, sems = rest[:3], rest[3:-1], rest[-1]
    places = [(i, e) for i, size in enumerate(sizes) for e in range(size)]
    for n, (i, e) in enumerate(places):
        word = list_ref[n]

        @pl.when(word >= 0)
        def _():
            fetch_block(word >> 4, word & 15, near, packed[i].at[e], sems.at[n])

    for n, (i, e) in enumerate(places):

        @pl.when(list_ref[n] >= 0)
        def _():
            pltpu.make_async_copy(near[0].at[0], packed[i].at[e], sems.at[n]).wait()


def pack(listing, near, sizes):
    size = near[0].shape[-1]
    return pl.pallas_call(
        functools.partial(pack_kernel, sizes),
        in_specs=[pl.BlockSpec(memory_space=pltpu.SMEM)]
        + [pl.BlockSpec(memory_space=pl.ANY)] * 3,
        out_specs=[pl.BlockSpec(memory_space=pltpu.VMEM)] * len(sizes),
        scratch_shapes=[pltpu.SemaphoreType.DMA((sum(sizes),))],
        out_shape=[jax.ShapeDtypeStruct((n, size, size), jnp.float32) for n in sizes],
        compiler_params=pltpu.CompilerParams(vmem_limit_bytes=4 << 20),
        name="pack",
    )(listing, *near)


def overflow_kernel(
    me_ref, info_ref, spots_ref, maps_ref, over_ref, product_list, zeros_ref, zero, sem
):
    zero[...] = jnp.zeros_like(zero)
    stores = [pltpu.make_async_copy(zero, zeros_ref.at[c], sem.at[c]) for c in range(sem.shape[0])]
    for store in stores:
        store.start()
    extract(entries_of(info_ref, me_ref)[0], product_list)
    held = positions(spots_ref, maps_ref)
    a = held[:8].astype(jnp.int32)
    turned = [held[8:40]] + [pltpu.roll(held[8:40], 128 - q, 1) for q in range(1, 16)]
    b = matmul(jnp.concatenate([x[:8] for x in turned]), maps_ref[0])
    b = b + matmul(jnp.concatenate([x[8:16] for x in turned]), maps_ref[1])
    b = b.astype(jnp.int32)
    c = matmul(jnp.concatenate([x[16:32] for x in turned]), maps_ref[2]).astype(jnp.int32)
    flags = [
        jnp.where(needed(a, b[q * 8 : q * 8 + 8], c[q * 16 : q * 16 + 16]), 1.0, 0.0)
        for q in range(16)
    ]
    alike = matmul(jnp.concatenate(flags), maps_ref[3])
    most = jnp.sum(alike[:8], axis=0, keepdims=True)
    for q in range(1, 16):
        most = jnp.maximum(most, jnp.sum(alike[q * 8 : q * 8 + 8], axis=0, keepdims=True))
    *_, way = lane_facts(most.shape)
    slots = jnp.where(way == 0, 128, jnp.where(way == 1, NEAR, FAR))
    slots = slots.astype(jnp.float32)
    turns = sum(jnp.where(most > k * slots, 1.0, 0.0) for k in range(1, 17))
    over_ref[0] = jnp.max(turns).astype(jnp.int32)
    for store in stores:
        store.wait()


def overflow(me, info, spots, maps, slots, size):
    smem = pl.BlockSpec(memory_space=pltpu.SMEM)
    vmem = pl.BlockSpec(memory_space=pltpu.VMEM)
    return pl.pallas_call(
        overflow_kernel,
        in_specs=[smem, vmem, vmem, vmem],
        out_specs=[smem, smem, pl.BlockSpec(memory_space=pltpu.HBM)],
        out_shape=[
            jax.ShapeDtypeStruct((1,), jnp.int32),
            jax.ShapeDtypeStruct((LIST + 1,), jnp.int32),
            jax.ShapeDtypeStruct((slots, size, size), jnp.float32),
        ],
        scratch_shapes=[pltpu.VMEM((size, size), jnp.float32), pltpu.SemaphoreType.DMA((slots,))],
        compiler_params=pltpu.CompilerParams(vmem_limit_bytes=4 << 20),
        cost_estimate=pl.CostEstimate(flops=10**9, bytes_accessed=10**5, transcendentals=0),
        name="overflow",
    )(me, info, spots, maps)


def halves(x):
    high = x.astype(jnp.bfloat16)
    return high, (x - high.astype(jnp.float32)).astype(jnp.bfloat16)


def block_product(a, b):
    a_high, a_low = halves(a)
    b_high, b_low = halves(b)
    dot = functools.partial(jnp.dot, preferred_element_type=jnp.float32)
    return dot(a_high, b_high) + (dot(a_high, b_low) + dot(a_low, b_high))


def extract(entries, list_ref):
    def more(state):
        n, word, left = state
        list_ref[n] = word.astype(jnp.int32)
        left = jnp.where(left == word, -1.0, left)
        return n + 1, jnp.max(left), left

    n, *_ = lax.while_loop(
        lambda state: state[1] >= 0, more, (jnp.int32(0), jnp.max(entries), entries)
    )
    list_ref[LIST] = n


def entries_of(info_ref, me_ref, turn=1):
    row, column = me_ref[0], me_ref[1]
    b, c, order = info_ref[8:16], info_ref[16:32], info_ref[32:40]
    r, p, owner, way = lane_facts(b.shape)
    t = lax.broadcasted_iota(jnp.int32, b.shape, 0)
    rank = order & 127
    steps = ((owner >> 1) - (row >> 1)) & 3
    part = jnp.where(steps == 0, 0, jnp.where(steps == 3, 1, 2))
    slots = jnp.where(way == 1, NEAR, FAR)
    sent = (way > 0) & (rank < slots)
    at = rank - turn * slots
    later = (way > 0) & (at >= 0) & (at < slots)
    along = ((p >> 1) - (column >> 1)) & 3
    beside = ((p ^ column) >> 3) & 1
    a_part = jnp.where(along == 0, 0, jnp.where(along == 3, 1, jnp.where(along == 1, 2, 3)))
    a_at = (a_part + 4 * ((p ^ column) & 1)) * 8 + beside * SA
    found = [[], []]
    for s in range(SA):
        lands = lands_at(info_ref[s : s + 1], b)
        c_slot = jnp.full(b.shape, -1, jnp.int32)
        for n in range(c.shape[0]):
            c_slot = jnp.where(lands == c[n : n + 1], n, c_slot)
        live = (c_slot >= 0) & (r == row)
        a_slot = a_at + s
        at_hand = jnp.where(
            way == 0,
            code(a_slot, part, (p & 1) * 8 + t, c_slot),
            code(a_slot, 2 + way, rank, c_slot),
        )
        in_turn = code(a_slot, (way - 1) & 3, at, c_slot)
        found[0].append(jnp.where(live & ((way == 0) | sent), at_hand, -1).astype(jnp.float32))
        found[1].append(jnp.where(live & later, in_turn, -1).astype(jnp.float32))
    return [jnp.concatenate(x) for x in found]


def multiply_listed(list_ref, a_refs, b_refs, acc, a_buf, b_buf, a_sem, b_sem, meanwhile):
    count = list_ref[LIST]

    def fetch(n):
        slot = n % AHEAD
        word = list_ref[n]
        fetch_a(word, a_refs, a_buf.at[slot], a_sem.at[slot])
        fetch_block(part_of(word), at_of(word), b_refs, b_buf.at[slot], b_sem.at[slot])

    for n in range(AHEAD):

        @pl.when(n < count)
        def _():
            fetch(n)

    meanwhile()

    def step(n, carry):
        slot = n % AHEAD
        pltpu.make_async_copy(a_refs[0].at[0], a_buf.at[slot], a_sem.at[slot]).wait()
        pltpu.make_async_copy(b_refs[0].at[0], b_buf.at[slot], b_sem.at[slot]).wait()
        acc[c_of(list_ref[n])] += block_product(a_buf[slot], b_buf[slot])

        @pl.when(n + AHEAD < count)
        def _():
            fetch(n + AHEAD)

        return carry

    lax.fori_loop(0, count, step, 0)


def all_kernel(parts, list_ref, *rest):
    a_refs, b_refs = rest[:A_PARTS], rest[A_PARTS:parts]
    _, out_ref, acc, c_sem, touched, *buffers = rest[parts:]
    slots = acc.shape[0]

    def stored(c):
        return pltpu.make_async_copy(acc.at[c], out_ref.at[c], c_sem.at[c])

    def meanwhile():
        for c in range(slots):
            touched[c] = 0

        def mark(n, carry):
            touched[c_of(list_ref[n])] = 1
            return carry

        lax.fori_loop(0, list_ref[LIST], mark, 0)
        acc[...] = jnp.zeros_like(acc)

    multiply_listed(list_ref, a_refs, b_refs, acc, *buffers, meanwhile)
    for c in range(slots):
        pl.when(touched[c] == 1)(lambda c=c: stored(c).start())
    for c in range(slots):
        pl.when(touched[c] == 1)(lambda c=c: stored(c).wait())


def add_listed(list_ref, a_refs, b_refs, total_ref, out_ref, acc, c_sem, stage, *buffers):
    count = list_ref[LIST]

    def touched(was, act):
        def step(n, carry):
            c = c_of(list_ref[n])

            @pl.when(stage[c] == was)
            def _():
                stage[c] = was + 1
                act(c)

            return carry

        lax.fori_loop(0, count, step, 0)

    def fetched(c):
        return pltpu.make_async_copy(total_ref.at[c], acc.at[c], c_sem.at[c])

    def stored(c):
        return pltpu.make_async_copy(acc.at[c], out_ref.at[c], c_sem.at[c])

    for c in range(acc.shape[0]):
        stage[c] = 0

    def meanwhile():
        touched(0, lambda c: fetched(c).start())
        touched(1, lambda c: fetched(c).wait())

    multiply_listed(list_ref, a_refs, b_refs, acc, *buffers, meanwhile)
    touched(2, lambda c: stored(c).start())
    touched(3, lambda c: stored(c).wait())


def rest_kernel(parts, me_ref, turn_ref, info_ref, *rest):
    a_refs, b_refs = rest[:A_PARTS], rest[A_PARTS:parts]
    total_ref, out_ref, rest_list, *buffers = rest[parts:]
    extract(entries_of(info_ref, me_ref, turn_ref[0])[1], rest_list)
    add_listed(rest_list, a_refs, b_refs, total_ref, out_ref, *buffers)


def products(kernel, leading, a_parts, b_parts, total, slots, own_list=False):
    size = a_parts[0].shape[-1]
    parts = len(a_parts) + len(b_parts)
    smem = pl.BlockSpec(memory_space=pltpu.SMEM)
    vmem = pl.BlockSpec(memory_space=pltpu.VMEM)
    hbm = pl.BlockSpec(memory_space=pltpu.HBM)
    operands = [*leading, *a_parts, *b_parts] + ([] if total is None else [total])
    return pl.pallas_call(
        functools.partial(kernel, parts),
        in_specs=[smem if x.ndim == 1 else vmem for x in leading]
        + [pl.BlockSpec(memory_space=pl.ANY)] * parts
        + ([] if total is None else [hbm]),
        out_specs=hbm,
        out_shape=jax.ShapeDtypeStruct((slots, size, size), jnp.float32),
        scratch_shapes=([pltpu.SMEM((LIST + 1,), jnp.int32)] if own_list else [])
        + [
            pltpu.VMEM((slots, size, size), jnp.float32),
            pltpu.SemaphoreType.DMA((slots,)),
            pltpu.SMEM((slots,), jnp.int32),
            pltpu.VMEM((AHEAD, size, size), jnp.float32),
            pltpu.VMEM((AHEAD, size, size), jnp.float32),
            pltpu.SemaphoreType.DMA((AHEAD,)),
            pltpu.SemaphoreType.DMA((AHEAD,)),
        ],
        input_output_aliases={} if total is None else {len(operands) - 1: 0},
        compiler_params=pltpu.CompilerParams(vmem_limit_bytes=VMEM_LIMIT),
        cost_estimate=pl.CostEstimate(
            flops=8 * 3 * 2 * size**3, bytes_accessed=24 * size * size * 4, transcendentals=0
        ),
        name="products",
    )(*operands)


def to_row(block, rows, there):
    return lax.ppermute(block, "row", [(i, there(i)) for i in range(rows)])


def on_z(i):
    return (i & 9) | ((i + 2) & 6)


def back_z(i):
    return (i & 9) | ((i - 2) & 6)


def moved(block, there, columns):
    return lax.ppermute(block, COL, [(i, there(i)) for i in range(columns)])


def line_kernel(a_ref, b_ref, c_ref, blocks_ref, line_ref, tile_ref, sem):
    copy = pltpu.make_async_copy(blocks_ref, tile_ref, sem.at[0])
    copy.start()
    lane = lax.broadcasted_iota(jnp.int32, line_ref.shape, 1)
    line = jnp.full(line_ref.shape, -1, jnp.int32)
    for n in range(a_ref.shape[0]):
        line = jnp.where(lane == n, a_ref[n], line)
    for h in range(b_ref.shape[0]):
        for t in range(b_ref.shape[1]):
            line = jnp.where(lane == 8 + h * b_ref.shape[1] + t, b_ref[h, t], line)
    for n in range(c_ref.shape[0]):
        line = jnp.where(lane == 24 + n, c_ref[n], line)
    line_ref[...] = line
    copy.wait()


def line_of(a_where, b_where, c_where, blocks):
    smem = pl.BlockSpec(memory_space=pltpu.SMEM)
    vmem = pl.BlockSpec(memory_space=pltpu.VMEM)
    return pl.pallas_call(
        line_kernel,
        in_specs=[smem] * 3 + [pl.BlockSpec(memory_space=pl.ANY)],
        out_specs=[vmem, vmem],
        out_shape=[
            jax.ShapeDtypeStruct((1, 128), jnp.int32),
            jax.ShapeDtypeStruct(blocks.shape, blocks.dtype),
        ],
        scratch_shapes=[pltpu.SemaphoreType.DMA((1,))],
        compiler_params=pltpu.CompilerParams(vmem_limit_bytes=4 << 20),
        name="line",
    )(a_where, b_where, c_where, blocks)


def pair_kernel(tile_ref, beside_ref, _, pair_ref, __, sems):
    n = tile_ref.shape[0]
    copies = [
        pltpu.make_async_copy(tile_ref, pair_ref.at[pl.ds(0, n)], sems.at[0]),
        pltpu.make_async_copy(beside_ref, pair_ref.at[pl.ds(n, n)], sems.at[1]),
    ]
    for copy in copies:
        copy.start()
    for copy in copies:
        copy.wait()


def paired(tile, beside, passing):
    n, size = tile.shape[0], tile.shape[-1]
    anywhere = pl.BlockSpec(memory_space=pl.ANY)
    return pl.pallas_call(
        pair_kernel,
        in_specs=[anywhere] * 3,
        out_specs=[pl.BlockSpec(memory_space=pltpu.VMEM), anywhere],
        out_shape=[
            jax.ShapeDtypeStruct((2 * n, size, size), tile.dtype),
            jax.ShapeDtypeStruct(passing.shape, passing.dtype),
        ],
        scratch_shapes=[pltpu.SemaphoreType.DMA((2,))],
        input_output_aliases={2: 1},
        compiler_params=pltpu.CompilerParams(vmem_limit_bytes=4 << 20),
        name="pair",
    )(tile, beside, passing)


def hold_kernel(*refs):
    pass


def held_for(arrays, later):
    anywhere = pl.BlockSpec(memory_space=pl.ANY)
    return pl.pallas_call(
        hold_kernel,
        in_specs=[anywhere] * (len(arrays) + len(later)),
        out_specs=[anywhere] * len(arrays),
        out_shape=[jax.ShapeDtypeStruct(x.shape, x.dtype) for x in arrays],
        input_output_aliases={i: i for i in range(len(arrays))},
        compiler_params=pltpu.CompilerParams(vmem_limit_bytes=1 << 20),
        name="hold",
    )(*arrays, *later)


def among(held, bits, rows, columns):
    me = lax.axis_index("row") * columns + lax.axis_index(COL)
    group = jnp.zeros((2 ** len(bits),) + held.shape, held.dtype)
    for move in range(2 ** len(bits)):
        flip = sum(((move >> n) & 1) << bit for n, bit in enumerate(bits))
        got = held
        if move:
            pairs = [(i ^ flip, i) for i in range(rows * columns)]
            got = lax.ppermute(held, ("row", *COL), pairs)
        spot = sum((((me ^ flip) >> bit) & 1) << n for n, bit in enumerate(bits))
        group = lax.dynamic_update_index_in_dim(group, got, spot, 0)
    return group


def per_device(a_blocks, a_index, b_blocks, b_index, c_index):
    rows = lax.axis_size("row")
    columns = lax.axis_size(COL)
    row = lax.axis_index("row")
    me = jnp.stack([row, lax.axis_index(COL)])
    hold = columns // rows
    sa, sb, sc = a_blocks.shape[2], b_blocks.shape[3], c_index.shape[2]
    held = hold * sb
    size = a_blocks.shape[-1]

    own = b_blocks[0, 0].reshape(held, size, size)
    behind = to_row(own, rows, lambda i: (i + 2) % rows)
    ahead = to_row(own, rows, lambda i: (i - 2) % rows)
    near = [own, behind, ahead]

    mine, tile = line_of(a_index[0, 0], b_index[0, 0], c_index[0, 0], a_blocks[0, 0])
    spots = among(mine.reshape(128), (5, 6), rows, columns)
    pair, spots = paired(tile, moved(tile, lambda i: i ^ 8, columns), spots)
    spots = among(spots, (1, 2), rows, columns)
    spots = among(spots, (3, 4), rows, columns)
    spots = among(spots, (0,), rows, columns).reshape(rows * columns, 128)
    a_behind = moved(pair, on_z, columns)
    a_ahead = moved(pair, back_z, columns)

    sends = [
        (FAR, 3, lambda i: ((i + 2) & 7) ^ 1),
        (FAR, 2, lambda i: (i - 2) & 7),
        (NEAR, 1, lambda i: i ^ 1),
    ]
    pack_list, info, maps = plan(me, spots, sends)
    packed = pack(pack_list, near, [n for n, *_ in sends])

    far_other, far_own, cross = [
        to_row(block, rows, there) for block, (*_, there) in zip(packed, sends)
    ]

    over, product_list, zeros = overflow(me, info, spots, maps, sc, size)
    (a_behind,) = held_for([a_behind], [info])
    a_far = moved(a_behind, on_z, columns)
    (a_far,) = held_for([a_far], [far_other, far_own, cross, over])
    a_mine = [pair, a_behind, a_ahead, a_far]
    a_parts = a_mine + [moved(block, lambda i: i ^ 1, columns) for block in a_mine]

    b_parts = near + [cross, far_own, far_other]
    total = products(all_kernel, [product_list], a_parts, b_parts, zeros, sc)

    turns = over[0]

    def again(state):
        turn, total = state
        listing = relist(me, turn[None], info, sends)
        packed = pack(listing, near, [n for n, *_ in sends])
        far_other, far_own, cross = [
            to_row(block, rows, there) for block, (*_, there) in zip(packed, sends)
        ]
        blocks = [cross, far_own, far_other]
        leading = [me, turn[None], info]
        total = products(rest_kernel, leading, a_parts, blocks, total, sc, own_list=True)
        return turn + 1, total

    _, total = lax.while_loop(lambda state: state[0] <= turns, again, (jnp.int32(1), total))
    return total[None, None]


def solution(mesh):
    rows, columns = mesh.devices.shape
    mesh = Mesh(mesh.devices.reshape(rows, 2, columns // 4, 2), ("row", *COL))
    in_specs = (
        P("row", COL, None, None, None),
        P("row", COL, None),
        P("row", COL, None, None, None, None),
        P("row", COL, None, None),
        P("row", COL, None),
    )
    out_specs = P("row", COL, None, None, None)
    return jax.shard_map(
        per_device, mesh=mesh, in_specs=in_specs, out_specs=out_specs, check_vma=False
    )
```
